32 devices in a mesh: clip: 8 (over y, x, core), seq: 4 (over z).
Axes of the slice: x: 2, y: 2, z: 4, core: 2. Of those that a mesh axis runs over, the one named last changes fastest.
Arguments:
- tokens: bfloat16 [32, 380, 768], P('clip', 'seq'), may hold values from -6 to 6
- freq_index: int32 [32, 7], P('clip'), may hold values from 0 to 11, as said below
- time_index: int32 [32, 54], P('clip'), may hold values from 0 to 98, as said below
- freq_table: bfloat16 [12, 768], replicated, may hold values from -3 to 3
- time_table: bfloat16 [99, 768], replicated, may hold values from -3 to 3
- norm1_gain: bfloat16 [768], replicated, may hold values from 0.25 to 1.75
- norm1_shift: bfloat16 [768], replicated, may hold values from -2 to 2
- qkv_weight: bfloat16 [768, 2304], replicated, may hold values from -0.21875 to 0.21875
- qv_bias: bfloat16 [2, 768], replicated, may hold values from -2 to 2
- proj_weight: bfloat16 [768, 768], replicated, may hold values from -2.5 to 2.5
- proj_bias: bfloat16 [768], replicated, may hold values from -2 to 2
- norm2_gain: bfloat16 [768], replicated, may hold values from 0.25 to 1.75
- norm2_shift: bfloat16 [768], replicated, may hold values from -2 to 2
- fc1_weight: bfloat16 [768, 3072], replicated, may hold values from -0.21875 to 0.21875
- fc1_bias: bfloat16 [3072], replicated, may hold values from -3 to 3
- fc2_weight: bfloat16 [3072, 768], replicated, may hold values from -0.15625 to 0.15625
- fc2_bias: bfloat16 [768], replicated, may hold values from -2 to 2
- cotangent: bfloat16 [32, 380, 768], P('clip', 'seq'), may hold values from -6 to 6
Outputs:
- block_out: bfloat16 [32, 380, 768], P('clip', 'seq')
- input_grad: bfloat16 [32, 380, 768], P('clip', 'seq')
- freq_table_grad: float32 [12, 768], replicated
- time_table_grad: float32 [99, 768], replicated
- norm1_gain_grad: float32 [768], replicated
- norm1_shift_grad: float32 [768], replicated
- qkv_weight_grad: float32 [768, 2304], P('clip')
- qv_bias_grad: float32 [2, 768], replicated
- proj_weight_grad: float32 [768, 768], P('clip')
- proj_bias_grad: float32 [768], replicated
- norm2_gain_grad: float32 [768], replicated
- norm2_shift_grad: float32 [768], replicated
- fc1_weight_grad: float32 [768, 3072], P('clip')
- fc1_bias_grad: float32 [3072], replicated
- fc2_weight_grad: float32 [3072, 768], P('clip')
- fc2_bias_grad: float32 [768], replicated
The draws below stay inside these ranges and needn't reach their ends.
Inputs may be any that keep to these rules, and one draw needn't show every extreme that they name: `freq_index`: each clip's 7 frequency rows are distinct and increasing. `time_index`: each clip's 54 time columns are distinct and increasing.
All inputs are finite; a program needn't handle non-finite values.
Results may differ from the reference program's by a relative error of at most 0.012.
Values may be sent and summed in bfloat16 or wider, within the bound.
A program may use at most 192 MiB of HBM per device.

```python
import jax
import jax.numpy as jnp
from jax import lax

D = 768
HEADS = 12
HDIM = 64
FF = 3072
FREQ = 12
TIME = 99
FKEEP = 7
TKEEP = 54
ROWS = 380
CLIPS_DEV = 4
CLIPS = 32
N_CLIP = 8


def pick_sorted(key, total_count, kept_count):
    keys_all = jax.random.split(key, CLIPS)

    def one_clip(clip_key):
        return jax.random.permutation(clip_key, total_count)[:kept_count]
    chosen = jax.vmap(one_clip)(keys_all)
    return jnp.sort(chosen, -1).astype(jnp.int32)


def draw_freq_index(key, part):
    key = jax.random.fold_in(key, 11)
    return pick_sorted(key, FREQ, FKEEP)


def draw_time_index(key, part):
    key = jax.random.fold_in(key, 23)
    return pick_sorted(key, TIME, TKEEP)


def spiked(entries, key, source, target, parts, factor):
    owner, partner = [(jnp.arange(entries.shape[dim]) // (entries.shape[dim] // parts)).reshape([-1 if axis == dim else 1 for axis in range(entries.ndim)]) for dim in (source, target)]
    chosen = jax.random.permutation(key, parts)[partner]
    strong = (owner == chosen) | (owner == (partner + parts // 2) % parts)
    return jnp.where(strong, factor * entries, entries)


def steps_of(rng, shape, cuts, low, top_value):
    def one(dim, parts):
        steps = jax.random.uniform(jax.random.fold_in(jax.random.fold_in(rng, 6), dim), (parts,), jnp.float32, low / len(cuts), top_value / len(cuts))
        return jnp.repeat(jnp.exp(steps), shape[dim] // parts).reshape((-1,) + (1,) * (len(shape) - dim - 1))

    loudness = one(*cuts[0])
    for cut in cuts[1:]:
        loudness = loudness * one(*cut)
    return loudness


def gaussian(key, shape, spread, most, shards=(), kind=jnp.bfloat16):
    result = spread * jax.random.normal(key, shape, jnp.float32)
    if shards:
        result = result * steps_of(key, shape, shards, -0.22, 0.18)
    return jnp.clip(result, -most, most).astype(kind)


def gaussian_with(stream_key, shape, width, reach, cuts, heavy, kind=jnp.bfloat16):
    values = width * jax.random.normal(stream_key, shape, jnp.float32)
    if cuts:
        values = values * steps_of(stream_key, shape, cuts, -0.22, 0.18)
    return jnp.clip(spiked(values, jax.random.fold_in(stream_key, 3), *heavy), -reach, reach).astype(kind)


def setup_inputs(seed: int = 0) -> dict:
    key_of = jax.random.split(jax.random.key(seed), 19)
    return {
        "tokens": gaussian_with(key_of[0], (CLIPS, ROWS, D), 1.0, 6.0, ((0, 8), (1, 4)), (0, 2, 8, 2.0)),
        "freq_index": draw_freq_index(jax.random.fold_in(key_of[18], 71), 0),
        "time_index": draw_time_index(jax.random.fold_in(key_of[18], 71), 0),
        "freq_table": gaussian(key_of[3], (FREQ, D), 0.5, 3.0),
        "time_table": gaussian(key_of[4], (TIME, D), 0.5, 3.0),
        "norm1_gain": jnp.clip(1.0 + 0.15 * jax.random.normal(key_of[5], (D,), jnp.float32), 0.25, 1.75).astype(jnp.bfloat16),
        "norm1_shift": gaussian(key_of[6], (D,), 0.3, 2.0),
        "qkv_weight": gaussian(key_of[7], (D, 3 * D), D ** -0.5, 0.21875),
        "qv_bias": gaussian(key_of[8], (2, D), 0.3, 2.0),
        "proj_weight": gaussian(key_of[9], (D, D), (max(1, 3 * D // ROWS)) ** -0.5, 2.5),
        "proj_bias": gaussian(key_of[10], (D,), 0.3, 2.0),
        "norm2_gain": jnp.clip(1.0 + 0.15 * jax.random.normal(key_of[11], (D,), jnp.float32), 0.25, 1.75).astype(jnp.bfloat16),
        "norm2_shift": gaussian(key_of[12], (D,), 0.3, 2.0),
        "fc1_weight": gaussian(key_of[13], (D, FF), D ** -0.5, 0.21875),
        "fc1_bias": gaussian(key_of[14], (FF,), 0.5, 3.0),
        "fc2_weight": gaussian(key_of[15], (FF, D), (FF // 2) ** -0.5, 0.15625),
        "fc2_bias": gaussian(key_of[16], (D,), 0.3, 2.0),
        "cotangent": gaussian_with(key_of[17], (CLIPS, ROWS, D), 1.0, 6.0, ((0, 8), (1, 4)), (0, 2, 8, 2.0)),
    }


@jax.custom_vjp
def low(v):
    return lax.optimization_barrier(v.astype(jnp.bfloat16)).astype(jnp.float32)

@jax.custom_vjp
def low_back(v):
    return v

def low_keep(v):
    return (low(v), None)

def low_pass(kept, grad):
    return (grad,)

def back_keep(v):
    return (v, None)

def back_low(kept, grad):
    return (low(grad),)
low.defvjp(low_keep, low_pass)
low_back.defvjp(back_keep, back_low)

def layer_norm(values, gain_vec, offset_vec):
    row_mean = lax.optimization_barrier(jnp.mean(values, -1, keepdims=True))
    centered = values - row_mean
    variance = lax.optimization_barrier(jnp.mean(centered * centered, -1, keepdims=True))
    return centered * lax.rsqrt(variance + 1e-06) * gain_vec + offset_vec

def project(values, matrix):
    return jnp.einsum('nrd,de->nre', values, matrix, precision=lax.Precision.HIGHEST)

def encoder_block(tokens, freq_pick, time_pick, tables, params):
    freq_table, time_table = tables
    norm1_gain, norm1_shift, qkv_weight, qv_bias, proj_weight, proj_bias, norm2_gain, norm2_shift, fc1_weight, fc1_bias, fc2_weight, fc2_bias = params
    clip_count = tokens.shape[0]
    model_width = tokens.shape[2]
    patch_rows = freq_table[freq_pick][:, :, None, :] + time_table[time_pick][:, None, :, :]
    patch_rows = patch_rows.reshape(clip_count, FKEEP * TKEEP, model_width)
    stream_in = tokens + jnp.concatenate([jnp.zeros_like(tokens[:, :2]), patch_rows], 1)
    normed_first = low(layer_norm(stream_in, norm1_gain, norm1_shift))
    bias_full = jnp.concatenate([qv_bias[0], jnp.zeros_like(qv_bias[0]), qv_bias[1]])
    projected = low(low_back(project(normed_first, qkv_weight) + bias_full))
    projected = projected.reshape(clip_count, ROWS, 3, HEADS, HDIM)
    query_part = projected[:, :, 0]
    key_part = projected[:, :, 1]
    value_part = projected[:, :, 2]
    scores = low_back(jnp.einsum('nqhe,nkhe->nhqk', query_part, key_part, precision=lax.Precision.HIGHEST) * HDIM ** (-0.5))
    probs_low = low(jax.nn.softmax(scores, -1))
    attended = jnp.einsum('nhqk,nkhe->nqhe', probs_low, value_part, precision=lax.Precision.HIGHEST)
    attended = low(low_back(attended.reshape(clip_count, ROWS, model_width)))
    branch = low_back(project(attended, proj_weight) + proj_bias)
    stream_mid = stream_in + branch
    normed_second = low(layer_norm(stream_mid, norm2_gain, norm2_shift))
    hidden = low_back(project(normed_second, fc1_weight) + fc1_bias)
    activated = low(jax.nn.gelu(hidden, approximate=False))
    mlp_out = low_back(project(activated, fc2_weight) + fc2_bias)
    return stream_mid + mlp_out

def reference(tokens, freq_index, time_index, freq_table, time_table, norm1_gain, norm1_shift, qkv_weight, qv_bias, proj_weight, proj_bias, norm2_gain, norm2_shift, fc1_weight, fc1_bias, fc2_weight, fc2_bias, cotangent):
    params = tuple((p.astype(jnp.float32) for p in (norm1_gain, norm1_shift, qkv_weight, qv_bias, proj_weight, proj_bias, norm2_gain, norm2_shift, fc1_weight, fc1_bias, fc2_weight, fc2_bias)))
    tables = (freq_table.astype(jnp.float32), time_table.astype(jnp.float32))
    token_groups = tokens.astype(jnp.float32).reshape(N_CLIP, CLIPS_DEV, ROWS, D)
    cot_groups = cotangent.astype(jnp.float32).reshape(N_CLIP, CLIPS_DEV, ROWS, D)
    freq_groups = freq_index.reshape(N_CLIP, CLIPS_DEV, FKEEP)
    time_groups = time_index.reshape(N_CLIP, CLIPS_DEV, TKEEP)

    def group_step(totals, group_item):
        group_tokens, freq_pick, time_pick, cot_group = group_item

        def forward(tok_in, tab_in, par_in):
            return encoder_block(tok_in, freq_pick, time_pick, tab_in, par_in)
        output, pullback = jax.vjp(forward, group_tokens, tables, params)
        grad_tokens, grad_tables, grad_params = pullback(cot_group)
        totals = jax.tree.map(jnp.add, totals, (grad_tables, grad_params))
        return (totals, (output.astype(jnp.bfloat16), grad_tokens.astype(jnp.bfloat16)))
    start = jax.tree.map(jnp.zeros_like, (tables, params))
    totals, results = lax.scan(group_step, start, (token_groups, freq_groups, time_groups, cot_groups))
    block_out = results[0].reshape(CLIPS, ROWS, D)
    input_grad = results[1].reshape(CLIPS, ROWS, D)
    grad_tables, grad_params = totals
    return (block_out, input_grad, grad_tables[0], grad_tables[1], grad_params[0], grad_params[1], grad_params[2], grad_params[3], grad_params[4], grad_params[5], grad_params[6], grad_params[7], grad_params[8], grad_params[9], grad_params[10], grad_params[11])
```

```python
import functools

import jax
import jax.numpy as jnp
from jax import lax
from jax.experimental import pallas as pl
from jax.experimental.pallas import tpu as pltpu
from jax.sharding import PartitionSpec as P

F32, BF16 = jnp.float32, jnp.bfloat16
MESH = pl.DeviceIdType.MESH
HDIM = 64
FKEEP = 7
TKEEP = 54
SPLIT = 4
GROUP = 8
PAD = 16
TIMES = 112
SLOTS = 64
UNITS = 12
NT = (((1,), (1,)), ((), ()))
TN = (((0,), (0,)), ((), ()))
ERF_P = 0.3275911
ERF_C = (0.254829592, -0.284496736, 1.421413741, -1.453152027, 1.061405429)


def dot(a, b, dims=(((1,), (0,)), ((), ()))):
    return lax.dot_general(a, b, dims, preferred_element_type=F32)


def normal_cdf_pdf(h):
    bell = jnp.exp(-0.5 * h * h)
    t = 1.0 / (1.0 + (ERF_P * 2.0**-0.5) * jnp.abs(h))
    tail = ERF_C[4]
    for coefficient in ERF_C[3::-1]:
        tail = tail * t + coefficient
    tail = 0.5 * tail * t * bell
    return jnp.where(h >= 0, 1.0 - tail, tail), bell * 0.3989422804014327


def normalize(v):
    centered = v - jnp.mean(v, -1, keepdims=True)
    rstd = lax.rsqrt(jnp.mean(centered * centered, -1, keepdims=True) + 1e-06)
    return centered * rstd, rstd


def row(ref):
    return ref[...].astype(F32).reshape(1, -1)


def block_kernel(
    tokens, freq_index, time_index, freq_table, time_table,
    gain1, shift1, qkv_hbm, qv_bias, proj_hbm, proj_bias, gain2, shift2,
    fc1_hbm, fc1_bias, fc2_hbm, fc2_bias, cotangent,
    out_hbm, grad_hbm, shares_hbm, small_hbm,
    w_qkv, w_proj, w_fc1, w_fc2, tok_in, cot_in, stream_in, normed, qkv, probs, attended, mid,
    work, left, left_out, right, unit, got1, got2, end_in, mid_in, final, staged, staged_grad,
    tables, picks, pay, pay_in, pay_mid, pay_out,
    w_sem, tok_s, tok_r, cot_s, cot_r, out_s, out_r, grad_s, grad_r, left_s, left_r, right_s, right_r,
    one_s, one_r, two_s, two_r, end_s, end_r, mid_s, mid_r, fin_s, fin_r, share_s,
    pay_s, pay_r, payz_s, payz_r, payo_s, payo_r,
):
    width = stream_in.shape[1]
    rows = tok_in.shape[1]
    padded = stream_in.shape[0] // SPLIT
    many = stream_in.shape[0]
    shard = width // GROUP
    half = width // 2
    pairs = width // (2 * HDIM)
    heavy = 3 * width
    step = 256 if width % 256 == 0 else 128

    c, z = lax.axis_index("clip"), lax.axis_index("seq")
    low = c % GROUP
    core, x, y = low % 2, (low // 2) % 2, low // 4
    base = c - low

    def peer(bits):
        px = 1 - x if bits & 2 else x
        py = 1 - y if bits & 4 else y
        pc = 1 - core if bits & 1 else core
        return pc + 2 * px + 4 * py

    def at(bits):
        return (base + peer(bits), z)

    def along(d):
        return (c, (z + d) % SPLIT)

    is_end = (z == 0) | (z == SPLIT - 1)
    is_mid = (z == 1) | (z == 2)
    to_mid = (c, jnp.where(z == 0, 1, 2))
    to_end = (c, jnp.where(z == 1, 0, 3))
    to_other = (c, jnp.where(z == 1, 2, 1))

    def remote(src, dst, send, recv, device):
        return pltpu.make_async_remote_copy(
            src_ref=src, dst_ref=dst, send_sem=send, recv_sem=recv, device_id=device, device_id_type=MESH
        )

    weights = [
        pltpu.make_async_copy(src, dst, w_sem.at[i])
        for i, (src, dst) in enumerate(
            ((qkv_hbm, w_qkv), (proj_hbm, w_proj), (fc1_hbm, w_fc1), (fc2_hbm, w_fc2))
        )
    ]
    barrier = pltpu.get_barrier_semaphore()
    for d in range(1, SPLIT):
        pl.semaphore_signal(barrier, inc=1, device_id=along(d), device_id_type=MESH)
    for bits in range(1, GROUP):
        pl.semaphore_signal(barrier, inc=1, device_id=at(bits), device_id_type=MESH)
    own_tok = pltpu.make_async_copy(tokens.at[z], tok_in.at[z], tok_r.at[z])
    own_cot = pltpu.make_async_copy(cotangent.at[z], cot_in.at[z], cot_r.at[z])
    own_tok.start()
    own_cot.start()
    pl.semaphore_wait(barrier, SPLIT - 1 + GROUP - 1)

    def spread(src, dst, send, recv):
        return [
            remote(src.at[(z + d) % SPLIT], dst.at[z], send.at[d - 1], recv.at[z], along(d))
            for d in range(1, SPLIT)
        ]

    tok_out = spread(tokens, tok_in, tok_s, tok_r)
    cot_out = spread(cotangent, cot_in, cot_s, cot_r)
    for copy in tok_out:
        copy.start()
    for copy in weights:
        copy.start()

    def wait_block(src, dst, send, recv, k):
        @pl.when(z == k)
        def _():
            pltpu.make_async_copy(src.at[k], dst.at[k], recv.at[k]).wait()

        @pl.when(z != k)
        def _():
            remote(src.at[k], dst.at[k], send.at[0], recv.at[k], along(1)).wait_recv()

    lane = lax.broadcasted_iota(jnp.int32, (8, 128), 1)
    index = jnp.full((8, 128), -1, jnp.int32)
    for s in range(TKEEP):
        index = jnp.where(lane == s, time_index[z, s], index)
    for s in range(FKEEP):
        index = jnp.where(lane == SLOTS + s, freq_index[z, s] + TIMES, index)
    column = lax.broadcasted_iota(jnp.int32, (128, 128), 0)
    pick = jnp.where(column == index[:1], 1.0, 0.0)
    picks[...] = pick.astype(BF16)
    tables[...] = jnp.zeros_like(tables)
    tables[pl.ds(0, time_table.shape[0]), :] = time_table[...].astype(F32)
    tables[pl.ds(TIMES, freq_table.shape[0]), :] = freq_table[...].astype(F32)
    by_slot = dot(pick.T.astype(BF16), tables[...].astype(BF16)).astype(BF16)

    def slots_of(row_number, slot):
        block = sum((row_number >= padded * k).astype(jnp.int32) for k in range(1, SPLIT))
        inside = row_number - padded * block
        patch = row_number - (padded - rows) * block - 2
        frequency = sum((patch >= TKEEP * k).astype(jnp.int32) for k in range(1, FKEEP))
        time = patch - TKEEP * frequency
        hit = (slot == time) | (slot == SLOTS + frequency)
        return jnp.where(hit & (inside < rows) & (patch >= 0), 1.0, 0.0).astype(BF16)

    g1, s1 = row(gain1), row(shift1)
    for k in range(SPLIT):
        place = padded * k
        number = lax.broadcasted_iota(jnp.int32, (padded, 128), 0) + place
        slot = lax.broadcasted_iota(jnp.int32, (padded, 128), 1)
        position = dot(slots_of(number, slot), by_slot)
        wait_block(tokens, tok_in, tok_s, tok_r, k)
        stream_in[pl.ds(place, rows), :] = tok_in[k].astype(F32) + position[:rows]
        stream_in[pl.ds(place + rows, padded - rows), :] = jnp.zeros((padded - rows, width), F32)

        @pl.loop(0, padded // 32)
        def _(b):
            at_row = pl.ds(pl.multiple_of(place + b * 32, 32), 32)
            hat, _ = normalize(stream_in[at_row, :])
            normed[at_row, :] = (hat * g1 + s1).astype(BF16)

    for copy in cot_out:
        copy.start()

    def hand_left(i, q, turned):
        for side in range(2):

            @pl.when(core == side)
            def _():
                left[i, q, :, pl.ds(0, many)] = turned[side]
                left_out[i, q] = turned[1 - side]

    def left_copy(i):
        return remote(
            left_out.at[i], left.at[i, :, :, pl.ds(many, many)], left_s.at[i], left_r.at[i], at(1)
        )

    def hand_all(i, source):
        turned = source[...].T.reshape(4, 2, shard, many)
        for q in range(4):
            hand_left(i, q, turned[q])
        left_copy(i).start()

    def right_copy(g):
        return remote(
            right.at[g, pl.ds(0, many)], right.at[g, pl.ds(many, many)], right_s.at[g], right_r.at[g], at(1)
        )

    weights[0].wait()
    hand_all(6, normed)
    bias_q, bias_v = qv_bias[0:1, :].astype(F32), qv_bias[1:2, :].astype(F32)
    for t, (bias, scale) in enumerate(((bias_q, HDIM**-0.5), (None, 1.0), (bias_v, 1.0))):
        for n in range(0, width, step):
            part = dot(normed[...], w_qkv[:, pl.ds(t * width + n, step)])
            if bias is not None:
                part = part + bias[:, n : n + step]
            part = part.astype(BF16)
            if scale != 1.0:
                part = part * jnp.asarray(scale, BF16)
            qkv[:, pl.ds(t * width + n, step)] = part

    key_number = lax.broadcasted_iota(jnp.int32, (8, many), 1)
    key_block = sum((key_number >= padded * k).astype(jnp.int32) for k in range(1, SPLIT))
    key_mask = jnp.where(key_number - padded * key_block < rows, 0.0, -1e30)[:1]
    head_lane = lax.broadcasted_iota(jnp.int32, (8, 2 * HDIM), 1)
    one_head = [
        jnp.where(head_lane < HDIM, 1.0, 0.0)[:1].astype(BF16),
        jnp.where(head_lane < HDIM, 0.0, 1.0)[:1].astype(BF16),
    ]

    def lanes(t, p):
        return pl.ds(pl.multiple_of(t * width + p * (2 * HDIM), 2 * HDIM), 2 * HDIM)

    @pl.loop(0, pairs)
    def _(p):
        query, key, value = (qkv[:, lanes(t, p)] for t in range(3))
        total = None
        for h in range(2):
            scores = dot(query * one_head[h], key, NT) + key_mask
            weight = jnp.exp(scores - jnp.max(scores, -1, keepdims=True))
            weight = (weight * (1.0 / jnp.sum(weight, -1, keepdims=True))).astype(BF16)
            probs[2 * p + h] = weight
            part = dot(weight, value * one_head[h])
            total = part if total is None else total + part
        attended[:, lanes(0, p)] = total.astype(BF16)

    weights[1].wait()
    hand_all(5, attended)
    bias = row(proj_bias)
    for n in range(0, width, step):
        mid[:, pl.ds(n, step)] = (
            stream_in[:, pl.ds(n, step)]
            + dot(attended[...], w_proj[:, pl.ds(n, step)])
            + bias[:, n : n + step]
        )
    g2, s2 = row(gain2), row(shift2)

    @pl.loop(0, many // 32)
    def _(b):
        at_row = pl.ds(pl.multiple_of(b * 32, 32), 32)
        hat, _ = normalize(mid[at_row, :])
        normed[at_row, :] = (hat * g2 + s2).astype(BF16)

    weights[2].wait()
    hand_all(4, normed)
    for q in range(4):
        for n in range(0, width, step):
            place = q * width + n
            work[:, pl.ds(n, step)] = (
                dot(normed[...], w_fc1[:, pl.ds(place, step)])
                + fc1_bias[pl.ds(place, step)].astype(F32).reshape(1, step)
            )

        @pl.loop(0, many // 32)
        def _(b):
            at_row = pl.ds(pl.multiple_of(b * 32, 32), 32)
            hidden = work[at_row, :]
            cdf, pdf = normal_cdf_pdf(hidden)
            unit[8 + q, at_row, :] = (hidden * cdf).astype(BF16)
            right[1 + q, at_row, :] = (cdf + hidden * pdf).astype(BF16)

        turned = unit[8 + q].T.reshape(2, 4, shard, many)
        for u in range(4):
            hand_left(u, q, turned[:, u])

    for u in range(4):
        left_copy(u).start()

    for k in range(SPLIT):
        place = padded * k
        wait_block(cotangent, cot_in, cot_s, cot_r, k)
        work[pl.ds(place, rows), :] = cot_in[k].astype(F32)
        work[pl.ds(place + rows, padded - rows), :] = jnp.zeros((padded - rows, width), F32)
    right[0, pl.ds(0, many), :] = work[...].astype(BF16)
    right_copy(0).start()

    def column_sums(ref_value):
        return jnp.sum(ref_value.astype(F32), 0, keepdims=True)

    pay[pl.ds(99 + 7, 1), :] = column_sums(work[...])

    A, B = pl.ds(0, half), pl.ds(half, half)

    def grid_of(i):
        return unit.at[i].reshape(2, 2, shard, width)

    def one_copies(i):
        u = grid_of(i)
        return (
            remote(u.at[:, 1 - x, :, A], got1.at[i, 0], one_s.at[i, 0], one_r.at[i, 0], at(2)),
            remote(u.at[1 - y, :, :, B], got1.at[i, 1], one_s.at[i, 1], one_r.at[i, 1], at(4)),
        )

    def two_copies(i):
        u = grid_of(i)
        return (
            remote(u.at[1 - y, x, :, A], got2.at[i, 0], two_s.at[i, 0], two_r.at[i, 0], at(4)),
            remote(u.at[y, 1 - x, :, B], got2.at[i, 1], two_s.at[i, 1], two_r.at[i, 1], at(2)),
        )

    def end_copy(i):
        return remote(grid_of(i).at[y, x], end_in.at[i], end_s.at[i], end_r.at[i], to_mid)

    own_part = jnp.where(z == 2, 1, 0)
    oth_part = 1 - own_part
    own_cols = pl.ds(pl.multiple_of(own_part * half, 128), half)
    oth_cols = pl.ds(pl.multiple_of(oth_part * half, 128), half)

    def mid_copy(i):
        return remote(grid_of(i).at[y, x, :, oth_cols], mid_in.at[i], mid_s.at[i], mid_r.at[i], to_other)

    def fin_copy(i, part, cols, which, device):
        return remote(final.at[i, :, cols], final.at[i, :, cols], fin_s.at[i, which], fin_r.at[i, part], device)

    def share_copy(i):
        return pltpu.make_async_copy(final.at[i], shares_hbm.at[i], share_s.at[i])

    def product(i, l, g, first_left, first_right):
        if first_left:
            left_copy(l).wait_recv()
        if first_right:
            right_copy(g).wait_recv()
        for n in range(0, width, step):
            part = dot(left[l].reshape(4 * shard, 2 * many), right[g, :, pl.ds(n, step)])
            unit[i, :, pl.ds(n, step)] = part.astype(BF16)
        for copy in one_copies(i):
            copy.start()

    def tick1(i):
        u = grid_of(i)
        first, second = one_copies(i)
        first.wait_recv()
        second.wait_recv()
        u[1 - y, x, :, A] = (u[1 - y, x, :, A].astype(F32) + got1[i, 0, 1 - y].astype(F32)).astype(BF16)
        u[y, 1 - x, :, B] = (u[y, 1 - x, :, B].astype(F32) + got1[i, 1, 1 - x].astype(F32)).astype(BF16)
        for copy in two_copies(i):
            copy.start()

    def tick2(i):
        for copy in two_copies(i):
            copy.wait_recv()

        @pl.when(is_end)
        def _():
            u = grid_of(i)
            u[y, x, :, A] = (
                u[y, x, :, A].astype(F32) + got1[i, 0, y].astype(F32) + got2[i, 0].astype(F32)
            ).astype(BF16)
            u[y, x, :, B] = (
                u[y, x, :, B].astype(F32) + got1[i, 1, x].astype(F32) + got2[i, 1].astype(F32)
            ).astype(BF16)
            end_copy(i).start()

    def sum_of(i, part, cols):
        near = jnp.where(part == 0, y, x)
        return (
            grid_of(i)[y, x, :, cols].astype(F32)
            + got1[i, part, near].astype(F32)
            + got2[i, part].astype(F32)
            + end_in[i, :, cols].astype(F32)
        )

    def tick3(i):
        @pl.when(is_mid)
        def _():
            end_copy(i).wait_recv()
            grid_of(i)[y, x, :, oth_cols] = sum_of(i, oth_part, oth_cols).astype(BF16)
            mid_copy(i).start()

    def tick4(i):
        @pl.when(is_mid)
        def _():
            mid_copy(i).wait_recv()
            final[i, :, own_cols] = (sum_of(i, own_part, own_cols) + mid_in[i].astype(F32)).astype(BF16)
            fin_copy(i, own_part, own_cols, 0, to_other).start()
            fin_copy(i, own_part, own_cols, 1, to_end).start()

    def tick5(i):
        @pl.when(is_mid)
        def _():
            fin_copy(i, oth_part, oth_cols, 2, to_end).wait_recv()
            fin_copy(i, oth_part, oth_cols, 2, to_end).start()

        @pl.when(is_end)
        def _():
            fin_copy(i, 0, A, 0, to_mid).wait_recv()
            fin_copy(i, 1, B, 0, to_mid).wait_recv()

        share_copy(i).start()

    ticks = (tick1, tick2, tick3, tick4, tick5)

    def advance(n):
        for k in range(len(ticks) - 1, -1, -1):
            if 0 <= n - k < UNITS:
                ticks[k](n - k)

    for i in range(4):
        product(i, i, 0, True, i == 0)

    weights[3].wait()
    bias = row(fc2_bias)
    for n in range(0, width, step):
        part = mid[:, pl.ds(n, step)] + bias[:, n : n + step]
        for q in range(4):
            part = part + dot(unit[8 + q], w_fc2[pl.ds(q * width, width), pl.ds(n, step)])
        for k in range(SPLIT):
            staged[k, :, pl.ds(n, step)] = part[padded * k : padded * k + rows].astype(BF16)

    def give(src, dst, send, recv):
        own = pltpu.make_async_copy(src.at[z], dst.at[z], recv.at[z])
        return [own] + [
            remote(src.at[(z + d) % SPLIT], dst.at[z], send.at[d - 1], recv.at[z], along(d))
            for d in range(1, SPLIT)
        ]

    out_copies = give(staged, out_hbm, out_s, out_r)
    for copy in out_copies:
        copy.start()
    advance(0)

    def grad_hidden(q):
        for n in range(0, width, step):
            part = dot(right[0, pl.ds(0, many), :], w_fc2[pl.ds(q * width + n, step), :], NT)
            part = (part * right[1 + q, pl.ds(0, many), pl.ds(n, step)].astype(F32)).astype(BF16)
            right[1 + q, pl.ds(0, many), pl.ds(n, step)] = part
            pay[pl.ds(99 + 8 + q, 1), pl.ds(n, step)] = column_sums(part)
        right_copy(1 + q).start()

    grad_hidden(0)
    grad_hidden(1)
    product(4, 4, 1, True, True)
    product(5, 4, 2, False, True)
    advance(1)
    grad_hidden(2)
    grad_hidden(3)
    product(6, 4, 3, False, True)
    product(7, 4, 4, False, True)
    advance(2)

    for n in range(0, width, step):
        part = None
        for q in range(4):
            term = dot(right[1 + q, pl.ds(0, many), :], w_fc1[pl.ds(n, step), pl.ds(q * width, width)], NT)
            part = term if part is None else part + term
        work[:, pl.ds(n, step)] = part

    def norm_back(grad, value, gain):
        hat, rstd = normalize(value)
        g = grad * gain
        back = rstd * (g - jnp.mean(g, -1, keepdims=True) - hat * jnp.mean(g * hat, -1, keepdims=True))
        return back, hat

    zero = jnp.zeros((1, width), F32)

    def back_second(b, sums):
        at_row = pl.ds(pl.multiple_of(b * 32, 32), 32)
        grad = work[at_row, :]
        back, hat = norm_back(grad, mid[at_row, :], g2)
        back = back + right[0, at_row, :].astype(F32)
        mid[at_row, :] = back
        branch = back.astype(BF16)
        right[5, at_row, :] = branch
        return (
            sums[0] + column_sums(grad * hat),
            sums[1] + column_sums(grad),
            sums[2] + column_sums(branch),
        )

    sums = lax.fori_loop(0, many // 32, back_second, (zero, zero, zero))
    pay[pl.ds(99 + 5, 1), :] = sums[0]
    pay[pl.ds(99 + 6, 1), :] = sums[1]
    pay[pl.ds(99 + 4, 1), :] = sums[2]
    right_copy(5).start()
    for n in range(0, width, step):
        normed[:, pl.ds(n, step)] = dot(
            right[5, pl.ds(0, many), :], w_proj[pl.ds(n, step), :], NT
        ).astype(BF16)
    product(8, 5, 5, True, True)
    advance(3)

    def attend_back(p):
        query, key, value = (qkv[:, lanes(t, p)] for t in range(3))
        grad_out = normed[:, lanes(0, p)]
        grads = None
        for h in range(2):
            weight_low = probs[2 * p + h]
            weight = weight_low.astype(F32)
            grad_probs = dot(grad_out * one_head[h], value, NT) * weight
            inner = jnp.sum(grad_probs, -1, keepdims=True)
            grad_scores = (grad_probs - weight * inner).astype(BF16)
            terms = (
                dot(grad_scores, key * one_head[h]),
                dot(grad_scores, query * one_head[h], TN),
                dot(weight_low, grad_out * one_head[h], TN),
            )
            grads = terms if grads is None else tuple(a + b for a, b in zip(grads, terms, strict=True))
        for t, (grad, scale) in enumerate(zip(grads, (HDIM**-0.5, 1.0, 1.0), strict=True)):
            low_grad = (grad * scale).astype(BF16)
            right[6 + t, pl.ds(0, many), lanes(0, p)] = low_grad
            if t != 1:
                pay[pl.ds(99 + 2 + t // 2, 1), lanes(0, p)] = column_sums(low_grad)

    parts = 3
    for s in range(parts):
        @pl.loop(s * pairs // parts, (s + 1) * pairs // parts)
        def _(p):
            attend_back(p)

        if s < parts - 1:
            advance(4 + s)
    for t in range(3):
        right_copy(6 + t).start()
    for t in range(3):
        product(9 + t, 6, 6 + t, t == 0, True)
    advance(6)

    for n in range(0, width, step):
        part = None
        for t in range(3):
            term = dot(right[6 + t, pl.ds(0, many), :], w_qkv[pl.ds(n, step), pl.ds(t * width, width)], NT)
            part = term if part is None else part + term
        work[:, pl.ds(n, step)] = part

    def back_first(b, sums):
        at_row = pl.ds(pl.multiple_of(b * 32, 32), 32)
        grad = work[at_row, :]
        back, hat = norm_back(grad, stream_in[at_row, :], g1)
        mid[at_row, :] = mid[at_row, :] + back
        return sums[0] + column_sums(grad * hat), sums[1] + column_sums(grad)

    sums = lax.fori_loop(0, many // 32, back_first, (zero, zero))
    pay[pl.ds(99, 1), :] = sums[0]
    pay[pl.ds(100, 1), :] = sums[1]
    for k in range(SPLIT):
        staged_grad[k] = mid[pl.ds(padded * k, padded), :][:rows].astype(BF16)
    grad_copies = give(staged_grad, grad_hbm, grad_s, grad_r)
    for copy in grad_copies:
        copy.start()

    def halves(v):
        high = v.astype(BF16)
        return high, (v - high.astype(F32)).astype(BF16)

    number = lax.broadcasted_iota(jnp.int32, (128, many), 1)
    slot = lax.broadcasted_iota(jnp.int32, (128, many), 0)
    slots = slots_of(number, slot)
    for n in range(0, width, step):
        by = sum(dot(slots, v) for v in halves(mid[:, pl.ds(n, step)]))
        table_grad = sum(dot(picks[...], v) for v in halves(by))
        pay[pl.ds(0, 99), pl.ds(n, step)] = table_grad[:99]
        pay[pl.ds(TIMES, 16), pl.ds(n, step)] = table_grad[TIMES:]
    pay[pl.ds(111, 1), :] = zero

    def pay_copy(bits):
        return remote(pay.at[pl.ds(16 * peer(bits), 16)], pay_in.at[low], pay_s.at[bits - 1], pay_r.at[low], at(bits))

    def pay_wait(bits):
        remote(
            pay.at[pl.ds(0, 16)], pay_in.at[peer(bits)], pay_s.at[bits - 1], pay_r.at[peer(bits)], at(bits)
        ).wait_recv()

    def payz_copy(d):
        return remote(pay_mid.at[z], pay_mid.at[z], payz_s.at[d - 1], payz_r.at[z], along(d))

    def payo_copy(bits):
        return remote(pay_out.at[low], pay_out.at[low], payo_s.at[bits - 1], payo_r.at[low], at(bits))

    for bits in range(1, GROUP):
        pay_copy(bits).start()
    advance(7)
    for bits in range(1, GROUP):
        pay_wait(bits)
    pay_in[low] = pay[pl.ds(pl.multiple_of(16 * low, 16), 16), :]
    pay_mid[z] = sum(pay_in[s] for s in range(GROUP))
    for d in range(1, SPLIT):
        payz_copy(d).start()
    advance(8)
    for d in range(1, SPLIT):
        k = (z + d) % SPLIT
        remote(pay_mid.at[k], pay_mid.at[k], payz_s.at[d - 1], payz_r.at[k], along(d)).wait_recv()
    pay_out[low] = sum(pay_mid[s] for s in range(SPLIT))
    for bits in range(1, GROUP):
        payo_copy(bits).start()
    for n in range(9, UNITS + len(ticks) - 1):
        advance(n)
    for bits in range(1, GROUP):
        remote(
            pay_out.at[low], pay_out.at[peer(bits)], payo_s.at[bits - 1], payo_r.at[peer(bits)], at(bits)
        ).wait_recv()
    last = pltpu.make_async_copy(pay_out, small_hbm, w_sem.at[0])
    last.start()

    for copies in (tok_out, cot_out, out_copies[1:], grad_copies[1:]):
        for copy in copies:
            copy.wait_send()
    for k in range(SPLIT):
        wait_block(staged, out_hbm, out_s, out_r, k)
        wait_block(staged_grad, grad_hbm, grad_s, grad_r, k)
    for i in range(left.shape[0]):
        left_copy(i).wait_send()
    for g in range(right.shape[0]):
        right_copy(g).wait_send()

    @pl.loop(0, UNITS)
    def _(i):
        for copy in (*one_copies(i), *two_copies(i)):
            copy.wait_send()

        @pl.when(is_end)
        def _():
            end_copy(i).wait_send()

        @pl.when(is_mid)
        def _():
            mid_copy(i).wait_send()
            fin_copy(i, own_part, own_cols, 0, to_other).wait_send()
            fin_copy(i, own_part, own_cols, 1, to_end).wait_send()
            fin_copy(i, oth_part, oth_cols, 2, to_end).wait_send()

        share_copy(i).wait()

    for bits in range(1, GROUP):
        pay_copy(bits).wait_send()
        payo_copy(bits).wait_send()
    for d in range(1, SPLIT):
        payz_copy(d).wait_send()
    last.wait()


def on_device(
    tokens, freq_index, time_index, freq_table, time_table,
    norm1_gain, norm1_shift, qkv_weight, qv_bias, proj_weight, proj_bias, norm2_gain, norm2_shift,
    fc1_weight, fc1_bias, fc2_weight, fc2_bias, cotangent,
):
    clips, rows, width = tokens.shape
    groups = lax.axis_size("seq")
    clip_devices = lax.axis_size("clip")
    assert clips == SPLIT and groups == SPLIT and clip_devices % GROUP == 0
    hidden_width = fc1_weight.shape[1]
    assert hidden_width == 4 * width
    padded = -(-rows // 32) * 32
    many = SPLIT * padded
    shard = width // GROUP
    half = width // 2
    heads = width // HDIM

    vmem = pl.BlockSpec(memory_space=pltpu.VMEM)
    smem = pl.BlockSpec(memory_space=pltpu.SMEM)
    anywhere = pl.BlockSpec(memory_space=pl.ANY)
    dma = pltpu.SemaphoreType.DMA
    blocks = (SPLIT, rows, width)
    out, grad, shares, small = pl.pallas_call(
        block_kernel,
        out_shape=(
            jax.ShapeDtypeStruct(blocks, BF16),
            jax.ShapeDtypeStruct(blocks, BF16),
            jax.ShapeDtypeStruct((UNITS, shard, width), BF16),
            jax.ShapeDtypeStruct((GROUP, 16, width), F32),
        ),
        in_specs=[
            anywhere, smem, smem, vmem, vmem, vmem, vmem, anywhere, vmem, anywhere, vmem, vmem, vmem,
            anywhere, vmem, anywhere, vmem, anywhere,
        ],
        out_specs=(anywhere,) * 4,
        scratch_shapes=[
            pltpu.VMEM((width, 3 * width), BF16),
            pltpu.VMEM((width, width), BF16),
            pltpu.VMEM((width, hidden_width), BF16),
            pltpu.VMEM((hidden_width, width), BF16),
            pltpu.VMEM(blocks, BF16),
            pltpu.VMEM(blocks, BF16),
            pltpu.VMEM((many, width), F32),
            pltpu.VMEM((many, width), BF16),
            pltpu.VMEM((many, 3 * width), BF16),
            pltpu.VMEM((heads, many, many), BF16),
            pltpu.VMEM((many, width), BF16),
            pltpu.VMEM((many, width), F32),
            pltpu.VMEM((many, width), F32),
            pltpu.VMEM((7, 4, shard, 2 * many), BF16),
            pltpu.VMEM((7, 4, shard, many), BF16),
            pltpu.VMEM((9, 2 * many, width), BF16),
            pltpu.VMEM((UNITS, 4 * shard, width), BF16),
            pltpu.VMEM((UNITS, 2, 2, shard, half), BF16),
            pltpu.VMEM((UNITS, 2, shard, half), BF16),
            pltpu.VMEM((UNITS, shard, width), BF16),
            pltpu.VMEM((UNITS, shard, half), BF16),
            pltpu.VMEM((UNITS, shard, width), BF16),
            pltpu.VMEM(blocks, BF16),
            pltpu.VMEM(blocks, BF16),
            pltpu.VMEM((128, width), F32),
            pltpu.VMEM((128, 128), BF16),
            pltpu.VMEM((128, width), F32),
            pltpu.VMEM((GROUP, 16, width), F32),
            pltpu.VMEM((SPLIT, 16, width), F32),
            pltpu.VMEM((GROUP, 16, width), F32),
            dma((4,)),
            dma((3,)), dma((4,)), dma((3,)), dma((4,)), dma((3,)), dma((4,)), dma((3,)), dma((4,)),
            dma((7,)), dma((7,)), dma((9,)), dma((9,)),
            dma((UNITS, 2)), dma((UNITS, 2)), dma((UNITS, 2)), dma((UNITS, 2)),
            dma((UNITS,)), dma((UNITS,)), dma((UNITS,)), dma((UNITS,)),
            dma((UNITS, 3)), dma((UNITS, 2)), dma((UNITS,)),
            dma((7,)), dma((8,)), dma((3,)), dma((4,)), dma((7,)), dma((8,)),
        ],
        compiler_params=pltpu.CompilerParams(
            collective_id=1, has_side_effects=True, vmem_limit_bytes=63 * 2**20
        ),
    )(
        tokens, freq_index, time_index, freq_table, time_table,
        norm1_gain, norm1_shift, qkv_weight, qv_bias, proj_weight, proj_bias, norm2_gain, norm2_shift,
        fc1_weight, fc1_bias, fc2_weight, fc2_bias, cotangent,
    )
    shares = shares.astype(F32)
    small = small.reshape(GROUP * 16, width)
    if clip_devices > GROUP:
        count = clip_devices // GROUP
        same = [[h * GROUP + b for h in range(count)] for b in range(GROUP)]
        small = lax.psum(small, "clip", axis_index_groups=same)
        fc2 = shares[:4].reshape(4 * shard, width)
        rest = shares[4:].transpose(1, 0, 2).reshape(shard, 8 * width)
        summed = [
            lax.psum_scatter(v, "clip", scatter_dimension=0, axis_index_groups=same, tiled=True)
            for v in (fc2, rest)
        ]
        moves = [(h * GROUP + b, b * count + h) for h in range(count) for b in range(GROUP)]
        fc2, rest = (lax.ppermute(v, "clip", moves) for v in summed)
    else:
        fc2 = shares[:4].reshape(4 * shard, width)
        rest = shares[4:].transpose(1, 0, 2).reshape(shard, 8 * width)
    fc1, proj, qkv = rest[:, : 4 * width], rest[:, 4 * width : 5 * width], rest[:, 5 * width :]
    return (
        out,
        grad,
        small[TIMES : TIMES + freq_table.shape[0]],
        small[: time_table.shape[0]],
        small[99],
        small[100],
        qkv,
        small[101:103],
        proj,
        small[103],
        small[104],
        small[105],
        fc1,
        small[107:111].reshape(-1),
        fc2,
        small[106],
    )


def solution(mesh):
    rows_split, clip_split = P("clip", "seq", None), P("clip", None)
    in_specs = (rows_split, clip_split, clip_split) + (P(),) * 14 + (rows_split,)
    out_specs = (
        rows_split, rows_split, P(), P(), P(), P(), clip_split, P(), clip_split, P(), P(), P(), clip_split,
        P(), clip_split, P(),
    )
    return jax.shard_map(on_device, mesh=mesh, in_specs=in_specs, out_specs=out_specs, check_vma=False)
```

```python
import functools

import jax
import jax.numpy as jnp
from jax import lax
from jax.experimental import pallas as pl
from jax.experimental.pallas import tpu as pltpu
from jax.sharding import PartitionSpec as P

F32, BF16 = jnp.float32, jnp.bfloat16
MESH = pl.DeviceIdType.MESH
HDIM = 64
FKEEP = 7
TKEEP = 54
SPLIT = 4
GROUP = 8
PAD = 16
TIMES = 112
SLOTS = 64
BLOCK = 96
UNITS = 12
ORDER = (
    "t0_0", "t0_1", "gh0", "gh1", "t0_2", "gh2", "gh3", "out", "sec", "t1_0", "t0_3", "sen", "t1_1", "t0_4", "att",
    "ab0", "t2_0", "ab1", "t1_2", "t0_5", "ab2", "fir", "t2_1", "t1_3", "fin", "t0_6", "t3_0", "t2_2", "tab", "t1_4",
    "t0_7", "pay2", "t3_1", "t2_3", "t1_5", "t0_8", "t4_0", "pay3", "t3_2", "t2_4", "t1_6", "t0_9", "t4_1", "t5_0",
    "t3_3", "t2_5", "t1_7", "t0_10", "t4_2", "t5_1", "t3_4", "t2_6", "t1_8", "t0_11", "t4_3", "t5_2", "t3_5", "t2_7",
    "t1_9", "t4_4", "t5_3", "t3_6", "t2_8", "t1_10", "t4_5", "t5_4", "t3_7", "t2_9", "t1_11", "t4_6", "t5_5", "t3_8",
    "t2_10", "t4_7", "t5_6", "t3_9", "t2_11", "t4_8", "t5_7", "t3_10", "t4_9", "t5_8", "t3_11", "t4_10", "t5_9",
    "t4_11", "t5_10", "t5_11",
)
NT = (((1,), (1,)), ((), ()))
TN = (((0,), (0,)), ((), ()))
ERF_P = 0.3275911
ERF_C = (0.254829592, -0.284496736, 1.421413741, -1.453152027, 1.061405429)


def dot(a, b, dims=(((1,), (0,)), ((), ()))):
    return lax.dot_general(a, b, dims, preferred_element_type=F32)


def normal_cdf_pdf(h):
    bell = jnp.exp(-0.5 * h * h)
    t = 1.0 / (1.0 + (ERF_P * 2.0**-0.5) * jnp.abs(h))
    tail = ERF_C[4]
    for coefficient in ERF_C[3::-1]:
        tail = tail * t + coefficient
    tail = 0.5 * tail * t * bell
    return jnp.where(h >= 0, 1.0 - tail, tail), bell * 0.3989422804014327


def normalize(v):
    centered = v - jnp.mean(v, -1, keepdims=True)
    rstd = lax.rsqrt(jnp.mean(centered * centered, -1, keepdims=True) + 1e-06)
    return centered * rstd, rstd


def row(ref):
    return ref[...].astype(F32).reshape(1, -1)


def block_kernel(
    tokens, freq_index_hbm, time_index_hbm, freq_table_hbm, time_table_hbm,
    gain1_hbm, shift1_hbm, qkv_hbm, qv_bias_hbm, proj_hbm, proj_bias_hbm, gain2_hbm, shift2_hbm,
    fc1_hbm, fc1_bias_hbm, fc2_hbm, fc2_bias_hbm, cotangent,
    out_hbm, grad_hbm, shares_hbm, small_hbm,
    freq_index, time_index, freq_table, time_table, gain1, shift1, qv_bias, proj_bias, gain2, shift2, fc1_bias, fc2_bias,
    raw, wide, w_qkv, w_proj, w_fc1, w_fc2, tok_in, cot_in, wide_cot, stream_in, normed, qkv, probs, attended, mid,
    work, left, left_out, right, unit, got1, got2, end_in, mid_in, final, staged, staged_grad,
    picks, pay, pay_low, pay_in, pay_mid, pay_out,
    v_sem, raw_sem, w_sem, tok_s, tok_r, cot_s, cot_r, out_s, out_r, grad_s, grad_r, left_s, left_r, right_s, right_r,
    one_s, one_r, two_s, two_r, end_s, end_r, mid_s, mid_r, fin_s, fin_r, share_s,
    pay_s, pay_r, payz_s, payz_r, payo_s, payo_r,
):
    width = stream_in.shape[1]
    rows = tok_in.shape[1]
    padded = stream_in.shape[0] // SPLIT
    many = stream_in.shape[0]
    shard = width // GROUP
    half = width // 2
    pairs = width // (2 * HDIM)
    heavy = 3 * width
    step = 256 if width % 256 == 0 else 128

    c, z = lax.axis_index("clip"), lax.axis_index("seq")
    low = c % GROUP
    core, x, y = low % 2, (low // 2) % 2, low // 4
    base = c - low

    def peer(bits):
        px = 1 - x if bits & 2 else x
        py = 1 - y if bits & 4 else y
        pc = 1 - core if bits & 1 else core
        return pc + 2 * px + 4 * py

    def at(bits):
        return (base + peer(bits), z)

    def along(d):
        return (c, (z + d) % SPLIT)

    is_end = (z == 0) | (z == SPLIT - 1)
    is_mid = (z == 1) | (z == 2)
    to_mid = (c, jnp.where(z == 0, 1, 2))
    to_end = (c, jnp.where(z == 1, 0, 3))
    to_other = (c, jnp.where(z == 1, 2, 1))

    def remote(src, dst, send, recv, device):
        return pltpu.make_async_remote_copy(
            src_ref=src, dst_ref=dst, send_sem=send, recv_sem=recv, device_id=device, device_id_type=MESH
        )

    small = [
        pltpu.make_async_copy(src, dst, v_sem.at[i])
        for i, (src, dst) in enumerate(
            (
                (freq_index_hbm, freq_index), (time_index_hbm, time_index),
                (freq_table_hbm, freq_table), (time_table_hbm, time_table),
                (gain1_hbm, gain1), (shift1_hbm, shift1), (qv_bias_hbm, qv_bias), (proj_bias_hbm, proj_bias),
                (gain2_hbm, gain2), (shift2_hbm, shift2), (fc1_bias_hbm, fc1_bias), (fc2_bias_hbm, fc2_bias),
            )
        )
    ]
    weights = [
        pltpu.make_async_copy(src, dst, w_sem.at[i])
        for i, (src, dst) in enumerate(
            ((qkv_hbm, w_qkv), (proj_hbm, w_proj), (fc1_hbm, w_fc1), (fc2_hbm, w_fc2))
        )
    ]
    raw_tok = pltpu.make_async_copy(tokens, raw, raw_sem.at[0])
    raw_cot = pltpu.make_async_copy(cotangent, raw, raw_sem.at[1])
    raw_tok.start()
    barrier = pltpu.get_barrier_semaphore()
    for d in range(1, SPLIT):
        pl.semaphore_signal(barrier, inc=1, device_id=along(d), device_id_type=MESH)
    for bits in range(1, GROUP):
        pl.semaphore_signal(barrier, inc=1, device_id=at(bits), device_id_type=MESH)
    for copy in small:
        copy.start()

    def spread(src, dst, send, recv):
        return [
            remote(src.at[(z + d) % SPLIT], dst.at[z], send.at[d - 1], recv.at[z], along(d))
            for d in range(1, SPLIT)
        ]

    def by_clip(staging):
        for n in range(0, width, step):
            wide[...] = raw[:, :, pl.ds(n, step)].astype(F32)
            for k in range(SPLIT):
                staging[k, :, pl.ds(n, step)] = wide[:, k, :].astype(BF16)

    tok_out = spread(staged, tok_in, tok_s, tok_r)
    cot_out = spread(staged_grad, cot_in, cot_s, cot_r)
    raw_tok.wait()
    by_clip(staged)
    raw_cot.start()
    pl.semaphore_wait(barrier, SPLIT - 1 + GROUP - 1)
    for copy in tok_out:
        copy.start()
    for copy in weights:
        copy.start()
    own_tok = pltpu.make_async_copy(staged.at[z], tok_in.at[z], tok_r.at[z])
    own_tok.start()
    raw_cot.wait()
    by_clip(staged_grad)
    own_cot = pltpu.make_async_copy(staged_grad.at[z], cot_in.at[z], cot_r.at[z])
    own_cot.start()
    for copy in small:
        copy.wait()

    def wait_block(src, dst, send, recv, k):
        @pl.when(z == k)
        def _():
            pltpu.make_async_copy(src.at[k], dst.at[k], recv.at[k]).wait()

        @pl.when(z != k)
        def _():
            remote(src.at[k], dst.at[k], send.at[0], recv.at[k], along(1)).wait_recv()

    lane = lax.broadcasted_iota(jnp.int32, (8, 128), 1)
    index = jnp.full((8, 128), -1, jnp.int32)
    for s in range(TKEEP):
        index = jnp.where(lane == s, time_index[z, s], index)
    for s in range(FKEEP):
        index = jnp.where(lane == SLOTS + s, freq_index[z, s] + TIMES, index)
    column = lax.broadcasted_iota(jnp.int32, (128, 128), 0)
    pick = jnp.where(column == index[:1], 1.0, 0.0)
    picks[...] = pick.astype(BF16)
    pay[...] = jnp.zeros_like(pay)
    pay[pl.ds(0, time_table.shape[0]), :] = time_table[...].astype(F32)
    pay[pl.ds(TIMES, freq_table.shape[0]), :] = freq_table[...].astype(F32)
    by_slot = dot(pick.T.astype(BF16), pay[...].astype(BF16)).astype(BF16)

    def slots_of(row_number, slot):
        block = sum((row_number >= padded * k).astype(jnp.int32) for k in range(1, SPLIT))
        inside = row_number - padded * block
        patch = row_number - (padded - rows) * block - 2
        frequency = sum((patch >= TKEEP * k).astype(jnp.int32) for k in range(1, FKEEP))
        time = patch - TKEEP * frequency
        hit = (slot == time) | (slot == SLOTS + frequency)
        return jnp.where(hit & (inside < rows) & (patch >= 0), 1.0, 0.0).astype(BF16)

    g1, s1 = row(gain1), row(shift1)
    bias_q, bias_v = qv_bias[0:1, :].astype(F32), qv_bias[1:2, :].astype(F32)
    weights[0].wait()
    for d in range(SPLIT):
        k = (z, jnp.where(z % 2 == 0, z + 1, z - 1), jnp.where(z < 2, 2, 1), jnp.where(z < 2, 3, 0))[d]
        place = pl.multiple_of(padded * k, 32)
        block_rows = pl.ds(place, padded)
        number = lax.broadcasted_iota(jnp.int32, (padded, 128), 0) + place
        slot = lax.broadcasted_iota(jnp.int32, (padded, 128), 1)
        position = dot(slots_of(number, slot), by_slot)
        if d == 0:
            own_tok.wait()
        else:
            remote(staged.at[k], tok_in.at[k], tok_s.at[0], tok_r.at[k], along(1)).wait_recv()
        stream_in[pl.ds(place, rows), :] = tok_in[k].astype(F32) + position[:rows]
        stream_in[pl.ds(place + rows, padded - rows), :] = jnp.zeros((padded - rows, width), F32)
        hat, _ = normalize(stream_in[block_rows, :])
        normed[block_rows, :] = (hat * g1 + s1).astype(BF16)
        for t, (bias, scale) in enumerate(((bias_q, HDIM**-0.5), (None, 1.0), (bias_v, 1.0))):
            for n in range(0, width, step):
                part = dot(normed[block_rows, :], w_qkv[:, pl.ds(t * width + n, step)])
                if bias is not None:
                    part = part + bias[:, n : n + step]
                part = part.astype(BF16)
                if scale != 1.0:
                    part = part * jnp.asarray(scale, BF16)
                qkv[block_rows, pl.ds(t * width + n, step)] = part

    for copy in cot_out:
        copy.start()

    def hand_left(i, q, turned):
        for side in range(2):

            @pl.when(core == side)
            def _():
                left[i, q, :, pl.ds(0, many)] = turned[side]
                left_out[i, q] = turned[1 - side]

    def left_copy(i):
        if i >= 4:
            return remote(
                left_out.at[i], left.at[i, :, :, pl.ds(many, many)], left_s.at[i], left_r.at[i], at(1)
            )
        return left_quarter(i)

    def left_quarter(q):
        return remote(
            left_out.at[pl.ds(0, 4), q], left.at[pl.ds(0, 4), q, :, pl.ds(many, many)], left_s.at[q], left_r.at[q], at(1)
        )

    def hand_all(i, source):
        turned = source[...].T.reshape(4, 2, shard, many)
        for q in range(4):
            hand_left(i, q, turned[q])
        left_copy(i).start()

    def right_copy(g):
        return remote(
            right.at[g, pl.ds(0, many)], right.at[g, pl.ds(many, many)], right_s.at[g], right_r.at[g], at(1)
        )

    hand_all(6, normed)

    key_number = lax.broadcasted_iota(jnp.int32, (8, many), 1)
    key_block = sum((key_number >= padded * k).astype(jnp.int32) for k in range(1, SPLIT))
    key_mask = jnp.where(key_number - padded * key_block < rows, 0.0, -1e30)[:1]
    head_lane = lax.broadcasted_iota(jnp.int32, (8, 2 * HDIM), 1)
    one_head = [
        jnp.where(head_lane < HDIM, 1.0, 0.0)[:1].astype(BF16),
        jnp.where(head_lane < HDIM, 0.0, 1.0)[:1].astype(BF16),
    ]

    def lanes(t, p):
        return pl.ds(pl.multiple_of(t * width + p * (2 * HDIM), 2 * HDIM), 2 * HDIM)

    @pl.loop(0, pairs)
    def _(p):
        query, key, value = (qkv[:, lanes(t, p)] for t in range(3))
        total = None
        for h in range(2):
            scores = dot(query * one_head[h], key, NT) + key_mask
            weight = jnp.exp(scores - jnp.max(scores, -1, keepdims=True))
            weight = (weight * (1.0 / jnp.sum(weight, -1, keepdims=True))).astype(BF16)
            probs[2 * p + h] = weight
            part = dot(weight, value * one_head[h])
            total = part if total is None else total + part
        attended[:, lanes(0, p)] = total.astype(BF16)

    weights[1].wait()
    hand_all(5, attended)
    bias = row(proj_bias)
    for n in range(0, width, step):
        mid[:, pl.ds(n, step)] = (
            stream_in[:, pl.ds(n, step)]
            + dot(attended[...], w_proj[:, pl.ds(n, step)])
            + bias[:, n : n + step]
        )
    g2, s2 = row(gain2), row(shift2)

    @pl.loop(0, many // BLOCK)
    def _(b):
        at_row = pl.ds(pl.multiple_of(b * BLOCK, BLOCK), BLOCK)
        hat, _ = normalize(mid[at_row, :])
        normed[at_row, :] = (hat * g2 + s2).astype(BF16)

    def column_sums(value):
        return jnp.sum(value.astype(F32), 0, keepdims=True)

    def first_matrix(q, n):
        place = pl.ds(pl.multiple_of(q * width + n, 128), step)
        work[:, pl.ds(n, step)] = dot(normed[...], w_fc1[:, place]) + fc1_bias[place].astype(F32).reshape(1, step)

    def activate(q, n):
        for r in range(0, many, 64):
            here = pl.ds(r, 64)
            hidden = work[here, pl.ds(n, step)]
            cdf, pdf = normal_cdf_pdf(hidden)
            unit[8 + q, here, pl.ds(n, step)] = (hidden * cdf).astype(BF16)
            right[1 + q, here, pl.ds(n, step)] = (cdf + hidden * pdf).astype(BF16)

    def hand_quarter(q):
        turned = unit[8 + q].T.reshape(2, 4, shard, many)
        for u in range(4):
            hand_left(u, q, turned[:, u])
        left_quarter(q).start()

    weights[2].wait()
    hand_all(4, normed)
    first_matrix(0, 0)

    def quarter(q, more):
        for n in range(step, width, step):
            first_matrix(q, n)
            activate(q, n - step)
        if more:
            first_matrix(q + 1, 0)
        activate(q, width - step)
        hand_quarter(q)

    @pl.loop(0, 3)
    def _(q):
        quarter(q, True)

    wide_cot[pl.ds(rows, padded - rows), :] = jnp.zeros((padded - rows, step), F32)
    for k in range(SPLIT):
        wait_block(staged_grad, cot_in, cot_s, cot_r, k)
        for n in range(0, width, step):
            wide_cot[pl.ds(0, rows), :] = cot_in[k, :, pl.ds(n, step)].astype(F32)
            right[0, pl.ds(padded * k, padded), pl.ds(n, step)] = wide_cot[...].astype(BF16)
    for n in range(0, width, step):
        pay[pl.ds(99 + 7, 1), pl.ds(n, step)] = column_sums(right[0, pl.ds(0, many), pl.ds(n, step)])
    right_copy(0).start()

    quarter(3, False)

    A, B = pl.ds(0, half), pl.ds(half, half)

    def grid_of(i):
        return unit.at[i].reshape(2, 2, shard, width)

    def one_copies(i):
        u = grid_of(i)
        return (
            remote(u.at[:, 1 - x, :, A], got1.at[i, 0], one_s.at[i, 0], one_r.at[i, 0], at(2)),
            remote(u.at[1 - y, :, :, B], got1.at[i, 1], one_s.at[i, 1], one_r.at[i, 1], at(4)),
        )

    def two_copies(i):
        u = grid_of(i)
        return (
            remote(u.at[1 - y, x, :, A], got2.at[i, 0], two_s.at[i, 0], two_r.at[i, 0], at(4)),
            remote(u.at[y, 1 - x, :, B], got2.at[i, 1], two_s.at[i, 1], two_r.at[i, 1], at(2)),
        )

    def end_copy(i):
        return remote(grid_of(i).at[y, x], end_in.at[i], end_s.at[i], end_r.at[i], to_mid)

    own_part = jnp.where(z == 2, 1, 0)
    oth_part = 1 - own_part
    own_cols = pl.ds(pl.multiple_of(own_part * half, 128), half)
    oth_cols = pl.ds(pl.multiple_of(oth_part * half, 128), half)

    def mid_copy(i):
        return remote(grid_of(i).at[y, x, :, oth_cols], mid_in.at[i], mid_s.at[i], mid_r.at[i], to_other)

    def fin_copy(i, part, cols, which, device):
        return remote(final.at[i, :, cols], final.at[i, :, cols], fin_s.at[i, which], fin_r.at[i, part], device)

    def share_copy(i):
        return pltpu.make_async_copy(final.at[i], shares_hbm.at[i], share_s.at[i])

    def product(i):
        l = i if i < 4 else 4 if i < 8 else 5 if i == 8 else 6
        g = 0 if i < 4 else i - 3
        for other in range(4) if i == 0 else (l,) if i in (4, 8, 9) else ():
            left_copy(other).wait_recv()
        if i == 0 or i >= 4:
            right_copy(g).wait_recv()
        for n in range(0, width, step):
            part = dot(left[l].reshape(4 * shard, 2 * many), right[g, :, pl.ds(n, step)])
            unit[i, :, pl.ds(n, step)] = part.astype(BF16)
        for copy in one_copies(i):
            copy.start()

    def tick1(i):
        u = grid_of(i)
        first, second = one_copies(i)
        first.wait_recv()
        second.wait_recv()
        u[1 - y, x, :, A] = (u[1 - y, x, :, A].astype(F32) + got1[i, 0, 1 - y].astype(F32)).astype(BF16)
        u[y, 1 - x, :, B] = (u[y, 1 - x, :, B].astype(F32) + got1[i, 1, 1 - x].astype(F32)).astype(BF16)
        for copy in two_copies(i):
            copy.start()

    def tick2(i):
        for copy in two_copies(i):
            copy.wait_recv()

        @pl.when(is_end)
        def _():
            u = grid_of(i)
            u[y, x, :, A] = (
                u[y, x, :, A].astype(F32) + got1[i, 0, y].astype(F32) + got2[i, 0].astype(F32)
            ).astype(BF16)
            u[y, x, :, B] = (
                u[y, x, :, B].astype(F32) + got1[i, 1, x].astype(F32) + got2[i, 1].astype(F32)
            ).astype(BF16)
            end_copy(i).start()

    def sum_of(i, part, cols):
        near = jnp.where(part == 0, y, x)
        return (
            grid_of(i)[y, x, :, cols].astype(F32)
            + got1[i, part, near].astype(F32)
            + got2[i, part].astype(F32)
            + end_in[i, :, cols].astype(F32)
        )

    def tick3(i):
        @pl.when(is_mid)
        def _():
            end_copy(i).wait_recv()
            grid_of(i)[y, x, :, oth_cols] = sum_of(i, oth_part, oth_cols).astype(BF16)
            mid_copy(i).start()

    def tick4(i):
        @pl.when(is_mid)
        def _():
            mid_copy(i).wait_recv()
            final[i, :, own_cols] = (sum_of(i, own_part, own_cols) + mid_in[i].astype(F32)).astype(BF16)
            fin_copy(i, own_part, own_cols, 0, to_other).start()
            fin_copy(i, own_part, own_cols, 1, to_end).start()

    def tick5(i):
        @pl.when(is_mid)
        def _():
            fin_copy(i, oth_part, oth_cols, 2, to_end).wait_recv()
            fin_copy(i, oth_part, oth_cols, 2, to_end).start()

        @pl.when(is_end)
        def _():
            fin_copy(i, 0, A, 0, to_mid).wait_recv()
            fin_copy(i, 1, B, 0, to_mid).wait_recv()

        share_copy(i).start()

    bias_out = row(fc2_bias)

    def block_out(n):
        part = mid[:, pl.ds(n, step)] + bias_out[:, n : n + step]
        for q in range(4):
            part = part + dot(unit[8 + q], w_fc2[pl.ds(q * width, width), pl.ds(n, step)])
        for k in range(SPLIT):
            staged[k, :, pl.ds(n, step)] = part[padded * k : padded * k + rows].astype(BF16)

    def give(src, dst, send, recv):
        own = pltpu.make_async_copy(src.at[z], dst.at[z], recv.at[z])
        return [own] + [
            remote(src.at[(z + d) % SPLIT], dst.at[z], send.at[d - 1], recv.at[z], along(d))
            for d in range(1, SPLIT)
        ]

    out_copies = give(staged, out_hbm, out_s, out_r)
    grad_copies = give(staged_grad, grad_hbm, grad_s, grad_r)

    def out_all():
        for copy in tok_out:
            copy.wait_send()
        for n in range(0, width, step):
            block_out(n)
        for copy in out_copies:
            copy.start()

    def grad_hidden(q):
        for n in range(0, width, step):
            part = dot(right[0, pl.ds(0, many), :], w_fc2[pl.ds(q * width + n, step), :], NT)
            part = (part * right[1 + q, pl.ds(0, many), pl.ds(n, step)].astype(F32)).astype(BF16)
            right[1 + q, pl.ds(0, many), pl.ds(n, step)] = part
            pay[pl.ds(99 + 8 + q, 1), pl.ds(n, step)] = column_sums(part)
        right_copy(1 + q).start()

    def grad_second():
        for n in range(0, width, step):
            part = None
            for q in range(4):
                term = dot(right[1 + q, pl.ds(0, many), :], w_fc1[pl.ds(n, step), pl.ds(q * width, width)], NT)
                part = term if part is None else part + term
            work[:, pl.ds(n, step)] = part

    def norm_back(grad, value, gain):
        hat, rstd = normalize(value)
        g = grad * gain
        back = rstd * (g - jnp.mean(g, -1, keepdims=True) - hat * jnp.mean(g * hat, -1, keepdims=True))
        return back, hat

    zero = jnp.zeros((1, width), F32)

    def second_norm():
        def block(b, sums):
            at_row = pl.ds(pl.multiple_of(b * BLOCK, BLOCK), BLOCK)
            grad = work[at_row, :]
            back, hat = norm_back(grad, mid[at_row, :], g2)
            back = back + right[0, at_row, :].astype(F32)
            mid[at_row, :] = back
            branch = back.astype(BF16)
            right[5, at_row, :] = branch
            return (
                sums[0] + column_sums(grad * hat),
                sums[1] + column_sums(grad),
                sums[2] + column_sums(branch),
            )

        sums = lax.fori_loop(0, many // BLOCK, block, (zero, zero, zero))
        pay[pl.ds(99 + 5, 1), :] = sums[0]
        pay[pl.ds(99 + 6, 1), :] = sums[1]
        pay[pl.ds(99 + 4, 1), :] = sums[2]
        right_copy(5).start()

    def grad_attended():
        for n in range(0, width, step):
            normed[:, pl.ds(n, step)] = dot(
                right[5, pl.ds(0, many), :], w_proj[pl.ds(n, step), :], NT
            ).astype(BF16)

    def attend_back(p):
        query, key, value = (qkv[:, lanes(t, p)] for t in range(3))
        grad_out = normed[:, lanes(0, p)]
        grads = None
        for h in range(2):
            weight_low = probs[2 * p + h]
            weight = weight_low.astype(F32)
            grad_probs = dot(grad_out * one_head[h], value, NT) * weight
            inner = jnp.sum(grad_probs, -1, keepdims=True)
            grad_scores = (grad_probs - weight * inner).astype(BF16)
            terms = (
                dot(grad_scores, key * one_head[h]),
                dot(grad_scores, query * one_head[h], TN),
                dot(weight_low, grad_out * one_head[h], TN),
            )
            grads = terms if grads is None else tuple(a + b for a, b in zip(grads, terms, strict=True))
        for t, (grad, scale) in enumerate(zip(grads, (HDIM**-0.5, 1.0, 1.0), strict=True)):
            low_grad = (grad * scale).astype(BF16)
            right[6 + t, pl.ds(0, many), lanes(0, p)] = low_grad
            if t != 1:
                pay[pl.ds(99 + 2 + t // 2, 1), lanes(0, p)] = column_sums(low_grad)

    def attention_back(s):
        @pl.loop(s * pairs // 3, (s + 1) * pairs // 3)
        def _(p):
            attend_back(p)

        if s == 2:
            for t in range(3):
                right_copy(6 + t).start()

    def grad_first():
        for n in range(0, width, step):
            part = None
            for t in range(3):
                term = dot(right[6 + t, pl.ds(0, many), :], w_qkv[pl.ds(n, step), pl.ds(t * width, width)], NT)
                part = term if part is None else part + term
            work[:, pl.ds(n, step)] = part

    def first_norm():
        def block(b, sums):
            at_row = pl.ds(pl.multiple_of(b * BLOCK, BLOCK), BLOCK)
            grad = work[at_row, :]
            back, hat = norm_back(grad, stream_in[at_row, :], g1)
            mid[at_row, :] = mid[at_row, :] + back
            return sums[0] + column_sums(grad * hat), sums[1] + column_sums(grad)

        sums = lax.fori_loop(0, many // BLOCK, block, (zero, zero))
        pay[pl.ds(99, 1), :] = sums[0]
        pay[pl.ds(100, 1), :] = sums[1]
        for copy in cot_out:
            copy.wait_send()
        for k in range(SPLIT):
            staged_grad[k] = mid[pl.ds(padded * k, padded), :][:rows].astype(BF16)
        for copy in grad_copies:
            copy.start()

    def halves(v):
        high = v.astype(BF16)
        return high, (v - high.astype(F32)).astype(BF16)

    def pay_copy(bits):
        return remote(
            pay_low.at[pl.ds(16 * peer(bits), 16)], pay_in.at[low], pay_s.at[bits - 1], pay_r.at[low], at(bits)
        )

    def payz_copy(d):
        return remote(pay_mid.at[z], pay_mid.at[z], payz_s.at[d - 1], payz_r.at[z], along(d))

    def payo_copy(bits):
        return remote(pay_out.at[low], pay_out.at[low], payo_s.at[bits - 1], payo_r.at[low], at(bits))

    def position_tables():
        number = lax.broadcasted_iota(jnp.int32, (128, many), 1)
        slot = lax.broadcasted_iota(jnp.int32, (128, many), 0)
        slots = slots_of(number, slot)
        for n in range(0, width, step):
            by = sum(dot(slots, v) for v in halves(mid[:, pl.ds(n, step)]))
            table_grad = sum(dot(picks[...], v) for v in halves(by))
            pay[pl.ds(0, 99), pl.ds(n, step)] = table_grad[:99]
            pay[pl.ds(TIMES, 16), pl.ds(n, step)] = table_grad[TIMES:]
        pay[pl.ds(111, 1), :] = zero
        pay_low[...] = pay[...].astype(BF16)
        for bits in range(1, GROUP):
            pay_copy(bits).start()

    def pay_group():
        for bits in range(1, GROUP):
            remote(
                pay_low.at[pl.ds(0, 16)], pay_in.at[peer(bits)], pay_s.at[bits - 1], pay_r.at[peer(bits)], at(bits)
            ).wait_recv()
        pay_in[low] = pay_low[pl.ds(pl.multiple_of(16 * low, 16), 16), :]
        pay_mid[z] = sum(pay_in[s].astype(F32) for s in range(GROUP)).astype(BF16)
        for d in range(1, SPLIT):
            payz_copy(d).start()

    def pay_line():
        for d in range(1, SPLIT):
            k = (z + d) % SPLIT
            remote(pay_mid.at[k], pay_mid.at[k], payz_s.at[d - 1], payz_r.at[k], along(d)).wait_recv()
        pay_out[low] = sum(pay_mid[s].astype(F32) for s in range(SPLIT)).astype(BF16)
        for bits in range(1, GROUP):
            payo_copy(bits).start()

    pieces = {
        "out": out_all, "sec": grad_second, "sen": second_norm, "att": grad_attended, "fir": grad_first,
        "fin": first_norm, "tab": position_tables, "pay2": pay_group, "pay3": pay_line,
    }
    for q in range(4):
        pieces[f"gh{q}"] = functools.partial(grad_hidden, q)
    for s in range(3):
        pieces[f"ab{s}"] = functools.partial(attention_back, s)
    for i in range(UNITS):
        pieces[f"t0_{i}"] = functools.partial(product, i)
        for k, tick in enumerate((tick1, tick2, tick3, tick4, tick5)):
            pieces[f"t{k + 1}_{i}"] = functools.partial(tick, i)
    assert sorted(ORDER) == sorted(pieces)
    weights[3].wait()
    for name in ORDER:
        pieces[name]()
    for bits in range(1, GROUP):
        remote(
            pay_out.at[low], pay_out.at[peer(bits)], payo_s.at[bits - 1], payo_r.at[peer(bits)], at(bits)
        ).wait_recv()
    last = pltpu.make_async_copy(pay_out, small_hbm, w_sem.at[0])
    last.start()

    for copies in (out_copies[1:], grad_copies[1:]):
        for copy in copies:
            copy.wait_send()
    for k in range(SPLIT):
        wait_block(staged, out_hbm, out_s, out_r, k)
        wait_block(staged_grad, grad_hbm, grad_s, grad_r, k)
    for i in range(left.shape[0]):
        left_copy(i).wait_send()
    for g in range(right.shape[0]):
        right_copy(g).wait_send()

    @pl.loop(0, UNITS)
    def _(i):
        for copy in (*one_copies(i), *two_copies(i)):
            copy.wait_send()

        @pl.when(is_end)
        def _():
            end_copy(i).wait_send()

        @pl.when(is_mid)
        def _():
            mid_copy(i).wait_send()
            fin_copy(i, own_part, own_cols, 0, to_other).wait_send()
            fin_copy(i, own_part, own_cols, 1, to_end).wait_send()
            fin_copy(i, oth_part, oth_cols, 2, to_end).wait_send()

        share_copy(i).wait()

    for bits in range(1, GROUP):
        pay_copy(bits).wait_send()
        payo_copy(bits).wait_send()
    for d in range(1, SPLIT):
        payz_copy(d).wait_send()
    last.wait()


def finish_kernel(
    out_in, grad_in, shares, small,
    out, grad, freq, time, gain1, shift1, qkv, qv_bias, proj, proj_bias, gain2, shift2, fc1, fc1_bias, fc2, fc2_bias,
    rows_in, wide, rows_out, parts, small_in, f_qkv, f_proj, f_fc1, f_fc2, f_time, f_freq, f_qv, lines,
    row_sem, part_sem, out_sem,
):
    width = wide.shape[2]
    shard = parts.shape[1]
    reads = [pltpu.make_async_copy(shares.at[i], parts.at[i], part_sem.at[i]) for i in range(UNITS)]
    moves = [pltpu.make_async_copy(src, rows_in.at[i], row_sem.at[i]) for i, src in enumerate((out_in, grad_in))]
    read_small = pltpu.make_async_copy(small, small_in, row_sem.at[2])
    for copy in (*reads, *moves, read_small):
        copy.start()
    line_of = lambda i: lines.at[pl.ds(i * width, width)]
    writes = [
        pltpu.make_async_copy(src, dst, out_sem.at[i])
        for i, (src, dst) in enumerate(
            (
                (f_fc2, fc2), (f_fc1, fc1), (f_proj, proj), (f_qkv, qkv), (rows_out.at[0], out), (rows_out.at[1], grad),
                (f_time, time), (f_freq, freq), (f_qv, qv_bias), (line_of(0), gain1), (line_of(1), shift1),
                (line_of(2), proj_bias), (line_of(3), gain2), (line_of(4), shift2), (line_of(5), fc2_bias),
                (lines.at[pl.ds(6 * width, 4 * width)], fc1_bias),
            )
        )
    ]
    for i in range(UNITS):
        reads[i].wait()
        value = parts[i].astype(F32)
        if i < 4:
            f_fc2[pl.ds(i * shard, shard), :] = value
        elif i < 8:
            f_fc1[:, pl.ds((i - 4) * width, width)] = value
        elif i == 8:
            f_proj[...] = value
        else:
            f_qkv[:, pl.ds((i - 9) * width, width)] = value
        if i in (3, 7, 8, 11):
            writes[(3, 7, 8, 11).index(i)].start()
    for i in range(2):
        moves[i].wait()
        for k in range(SPLIT):
            wide[:, k, :] = rows_in[i, k].astype(F32)
        rows_out[i] = wide[...].astype(BF16)
        writes[4 + i].start()
    read_small.wait()
    f_time[...] = small_in[pl.ds(0, time.shape[0]), :].astype(F32)
    f_freq[...] = small_in[pl.ds(TIMES, freq.shape[0]), :].astype(F32)
    rest = small_in[pl.ds(96, 16), :].astype(F32)[3:]
    f_qv[...] = rest[2:4]
    for at, i in enumerate((0, 1, 4, 5, 6, 7)):
        lines[pl.ds(at * width, width)] = rest[i : i + 1].reshape(width)
    for q in range(4):
        lines[pl.ds((6 + q) * width, width)] = rest[8 + q : 9 + q].reshape(width)
    for copy in writes[6:]:
        copy.start()
    for copy in writes:
        copy.wait()


def on_device(
    tokens, freq_index, time_index, freq_table, time_table,
    norm1_gain, norm1_shift, qkv_weight, qv_bias, proj_weight, proj_bias, norm2_gain, norm2_shift,
    fc1_weight, fc1_bias, fc2_weight, fc2_bias, cotangent,
):
    clips, rows, width = tokens.shape
    times, freqs = time_table.shape[0], freq_table.shape[0]
    groups = lax.axis_size("seq")
    clip_devices = lax.axis_size("clip")
    assert clips == SPLIT and groups == SPLIT and clip_devices % GROUP == 0
    hidden_width = fc1_weight.shape[1]
    assert hidden_width == 4 * width
    padded = -(-rows // 32) * 32
    many = SPLIT * padded
    shard = width // GROUP
    half = width // 2
    heads = width // HDIM

    anywhere = pl.BlockSpec(memory_space=pl.ANY)
    dma = pltpu.SemaphoreType.DMA
    blocks = (SPLIT, rows, width)
    vectors = (freq_table, time_table, norm1_gain, norm1_shift, qv_bias, proj_bias, norm2_gain, norm2_shift, fc1_bias, fc2_bias)
    small_scratch = [pltpu.SMEM(v.shape, v.dtype) for v in (freq_index, time_index)]
    small_scratch += [pltpu.VMEM(v.shape, v.dtype) for v in vectors]
    tokens, cotangent = (v.transpose(1, 0, 2) for v in (tokens, cotangent))
    out, grad, shares, small = pl.pallas_call(
        block_kernel,
        out_shape=(
            jax.ShapeDtypeStruct(blocks, BF16),
            jax.ShapeDtypeStruct(blocks, BF16),
            jax.ShapeDtypeStruct((UNITS, shard, width), BF16),
            jax.ShapeDtypeStruct((GROUP, 16, width), BF16),
        ),
        in_specs=[anywhere] * 18,
        out_specs=(anywhere,) * 4,
        scratch_shapes=[
            *small_scratch,
            pltpu.VMEM((rows, SPLIT, width), BF16),
            pltpu.VMEM((rows, SPLIT, 256 if width % 256 == 0 else 128), F32),
            pltpu.VMEM((width, 3 * width), BF16),
            pltpu.VMEM((width, width), BF16),
            pltpu.VMEM((width, hidden_width), BF16),
            pltpu.VMEM((hidden_width, width), BF16),
            pltpu.VMEM(blocks, BF16),
            pltpu.VMEM(blocks, BF16),
            pltpu.VMEM((padded, 256 if width % 256 == 0 else 128), F32),
            pltpu.VMEM((many, width), F32),
            pltpu.VMEM((many, width), BF16),
            pltpu.VMEM((many, 3 * width), BF16),
            pltpu.VMEM((heads, many, many), BF16),
            pltpu.VMEM((many, width), BF16),
            pltpu.VMEM((many, width), F32),
            pltpu.VMEM((many, width), F32),
            pltpu.VMEM((7, 4, shard, 2 * many), BF16),
            pltpu.VMEM((7, 4, shard, many), BF16),
            pltpu.VMEM((9, 2 * many, width), BF16),
            pltpu.VMEM((UNITS, 4 * shard, width), BF16),
            pltpu.VMEM((UNITS, 2, 2, shard, half), BF16),
            pltpu.VMEM((UNITS, 2, shard, half), BF16),
            pltpu.VMEM((UNITS, shard, width), BF16),
            pltpu.VMEM((UNITS, shard, half), BF16),
            pltpu.VMEM((UNITS, shard, width), BF16),
            pltpu.VMEM(blocks, BF16),
            pltpu.VMEM(blocks, BF16),
            pltpu.VMEM((128, 128), BF16),
            pltpu.VMEM((128, width), F32),
            pltpu.VMEM((128, width), BF16),
            pltpu.VMEM((GROUP, 16, width), BF16),
            pltpu.VMEM((SPLIT, 16, width), BF16),
            pltpu.VMEM((GROUP, 16, width), BF16),
            dma((12,)), dma((2,)), dma((4,)),
            dma((3,)), dma((4,)), dma((3,)), dma((4,)), dma((3,)), dma((4,)), dma((3,)), dma((4,)),
            dma((7,)), dma((7,)), dma((9,)), dma((9,)),
            dma((UNITS, 2)), dma((UNITS, 2)), dma((UNITS, 2)), dma((UNITS, 2)),
            dma((UNITS,)), dma((UNITS,)), dma((UNITS,)), dma((UNITS,)),
            dma((UNITS, 3)), dma((UNITS, 2)), dma((UNITS,)),
            dma((7,)), dma((8,)), dma((3,)), dma((4,)), dma((7,)), dma((8,)),
        ],
        compiler_params=pltpu.CompilerParams(
            collective_id=1, has_side_effects=True, vmem_limit_bytes=63 * 2**20
        ),
    )(
        tokens, freq_index, time_index, freq_table, time_table,
        norm1_gain, norm1_shift, qkv_weight, qv_bias, proj_weight, proj_bias, norm2_gain, norm2_shift,
        fc1_weight, fc1_bias, fc2_weight, fc2_bias, cotangent,
    )
    small = small.reshape(GROUP * 16, width)
    if clip_devices == GROUP:
        shape = lambda *dims: jax.ShapeDtypeStruct(dims, F32)
        inner = jax.ShapeDtypeStruct((rows, SPLIT, width), BF16)
        line = shape(width)
        results = (
            inner, inner, shape(freqs, width), shape(times, width), line, line, shape(shard, 3 * width),
            shape(2, width), shape(shard, width), line, line, line, shape(shard, 4 * width),
            shape(4 * width), shape(4 * shard, width), line,
        )
        out, grad, *others = pl.pallas_call(
            finish_kernel,
            out_shape=results,
            in_specs=[anywhere] * 4,
            out_specs=(anywhere,) * 16,
            scratch_shapes=[
                pltpu.VMEM((2, *blocks), BF16),
                pltpu.VMEM((rows, SPLIT, width), F32),
                pltpu.VMEM((2, rows, SPLIT, width), BF16),
                pltpu.VMEM((UNITS, shard, width), BF16),
                pltpu.VMEM((GROUP * 16, width), BF16),
                pltpu.VMEM((shard, 3 * width), F32),
                pltpu.VMEM((shard, width), F32),
                pltpu.VMEM((shard, 4 * width), F32),
                pltpu.VMEM((4 * shard, width), F32),
                pltpu.VMEM((times, width), F32),
                pltpu.VMEM((freqs, width), F32),
                pltpu.VMEM((2, width), F32),
                pltpu.VMEM((10 * width,), F32),
                dma((3,)), dma((UNITS,)), dma((16,)),
            ],
            compiler_params=pltpu.CompilerParams(vmem_limit_bytes=62 * 2**20),
        )(out, grad, shares, small)
        return (out.transpose(1, 0, 2), grad.transpose(1, 0, 2), *others)
    shares, small = shares.astype(F32), small.astype(F32)
    count = clip_devices // GROUP
    same = [[h * GROUP + b for h in range(count)] for b in range(GROUP)]
    small = lax.psum(small, "clip", axis_index_groups=same)
    fc2 = shares[:4].reshape(4 * shard, width)
    rest = shares[4:].transpose(1, 0, 2).reshape(shard, 8 * width)
    summed = [
        lax.psum_scatter(v, "clip", scatter_dimension=0, axis_index_groups=same, tiled=True)
        for v in (fc2, rest)
    ]
    moves = [(h * GROUP + b, b * count + h) for h in range(count) for b in range(GROUP)]
    fc2, rest = (lax.ppermute(v, "clip", moves) for v in summed)
    fc1, proj, qkv = rest[:, : 4 * width], rest[:, 4 * width : 5 * width], rest[:, 5 * width :]
    return (
        out,
        grad,
        small[TIMES : TIMES + freqs],
        small[:times],
        small[99],
        small[100],
        qkv,
        small[101:103],
        proj,
        small[103],
        small[104],
        small[105],
        fc1,
        small[107:111].reshape(-1),
        fc2,
        small[106],
    )


def solution(mesh):
    rows_split, clip_split = P("clip", "seq", None), P("clip", None)
    in_specs = (rows_split, clip_split, clip_split) + (P(),) * 14 + (rows_split,)
    out_specs = (
        rows_split, rows_split, P(), P(), P(), P(), clip_split, P(), clip_split, P(), P(), P(), clip_split,
        P(), clip_split, P(),
    )
    return jax.shard_map(on_device, mesh=mesh, in_specs=in_specs, out_specs=out_specs, check_vma=False)
```

```python
import functools

import jax
import jax.numpy as jnp
from jax import lax
from jax.experimental import pallas as pl
from jax.experimental.pallas import tpu as pltpu
from jax.sharding import PartitionSpec as P

F32, BF16 = jnp.float32, jnp.bfloat16
MESH = pl.DeviceIdType.MESH
HDIM = 64
FKEEP = 7
TKEEP = 54
SPLIT = 4
GROUP = 8
PAD = 16
TIMES = 112
SLOTS = 64
BLOCK = 96
UNITS = 12
PARTS = tuple((i, 0, 3) for i in range(UNITS - 1)) + tuple((UNITS - 1, 2 * k, 1) for k in range(3))
ORDER = (
    "gh0", "gh1", "gh2", "t0_0", "t0_1", "gh3", "sec", "t0_2", "out0", "out1", "out2", "t1_0", "sen", "att", "t1_1",
    "t0_3", "ab0", "t0_4", "t0_5", "t2_0", "ab1", "t3_0", "t2_1", "t0_6", "t1_2", "ab2", "fir", "t3_1", "fin", "t1_4",
    "t1_3", "t0_7", "t0_8", "t1_6", "t1_5", "t2_4", "t2_2", "t4_1", "t2_3", "t3_4", "t3_2", "t4_0", "t1_8", "t0_9",
    "t1_7", "t4_2", "t0_10", "t4_4", "t2_6", "tab", "t2_8", "t2_5", "t0_11", "t0_12", "t5_0", "t3_6", "t5_1", "t3_8",
    "t5_4", "t0_13", "t3_3", "t4_6", "t4_8", "t1_10", "t3_5", "t2_7", "t5_2", "t4_3", "t1_11", "pay2", "t1_13",
    "t4_5", "t1_9", "t1_12", "t3_7", "t2_10", "t2_13", "t2_11", "t5_8", "t2_9", "t5_3", "t5_6", "t3_10", "t2_12",
    "t5_5", "t4_7", "pay3", "t3_11", "t3_13", "t4_10", "t3_9", "t4_11", "t5_7", "t3_12", "t5_10", "t4_13", "t4_9",
    "t4_12", "t5_13", "t5_11", "t5_9", "t5_12",
)
NT = (((1,), (1,)), ((), ()))
TN = (((0,), (0,)), ((), ()))
LOG2_E = 1.4426950408889634
ERF_P = 0.3275911
ERF_C = (0.254829592, -0.284496736, 1.421413741, -1.453152027, 1.061405429)


def dot(a, b, dims=(((1,), (0,)), ((), ()))):
    return lax.dot_general(a, b, dims, preferred_element_type=F32)


def normal_cdf_pdf(h):
    bell = jnp.exp2(h * h * (-0.5 * LOG2_E))
    base = 1.0 + (ERF_P * 2.0**-0.5) * jnp.abs(h)
    t = pl.reciprocal(base, approx=True)
    t = t * (2.0 - base * t)
    tail = 0.5 * ERF_C[4]
    for coefficient in ERF_C[3::-1]:
        tail = tail * t + 0.5 * coefficient
    tail = tail * t * bell
    return jnp.where(h >= 0, 1.0 - tail, tail), bell * 0.3989422804014327


def normalize(v):
    centered = v - jnp.mean(v, -1, keepdims=True)
    rstd = lax.rsqrt(jnp.mean(centered * centered, -1, keepdims=True) + 1e-06)
    return centered * rstd, rstd


def row(ref):
    return ref[...].astype(F32).reshape(1, -1)


def block_kernel(
    tokens, freq_index_hbm, time_index_hbm, freq_table_hbm, time_table_hbm,
    gain1_hbm, shift1_hbm, qkv_hbm, qv_bias_hbm, proj_hbm, proj_bias_hbm, gain2_hbm, shift2_hbm,
    fc1_hbm, fc1_bias_hbm, fc2_hbm, fc2_bias_hbm, cotangent,
    out_hbm, grad_hbm, shares_hbm, small_hbm,
    freq_index, time_index, freq_table, time_table, gain1, shift1, qv_bias, proj_bias, gain2, shift2, fc1_bias, fc2_bias,
    raw, wide, w_qkv, w_proj, w_fc1, w_fc2, tok_in, cot_in, wide_cot, stream_in, normed, qkv, probs, attended, mid,
    work, left, right, unit, got1, got2, end_in, mid_in, final, staged, staged_grad,
    picks, pay, pay_low, pay_in, pay_mid, pay_out,
    v_sem, raw_sem, w_sem, tok_s, tok_r, cot_s, cot_r, out_s, out_r, grad_s, grad_r, left_s, left_r, right_s, right_r,
    one_s, one_r, two_s, two_r, end_s, end_r, mid_s, mid_r, fin_s, fin_r, share_s,
    pay_s, pay_r, payz_s, payz_r, payo_s, payo_r,
):
    width = stream_in.shape[1]
    rows = tok_in.shape[1]
    padded = stream_in.shape[0] // SPLIT
    many = stream_in.shape[0]
    shard = width // GROUP
    half = width // 2
    pairs = width // (2 * HDIM)
    heavy = 3 * width
    step = 256 if width % 256 == 0 else 128

    c, z = lax.axis_index("clip"), lax.axis_index("seq")
    low = c % GROUP
    core, x, y = low % 2, (low // 2) % 2, low // 4
    base = c - low

    def peer(bits):
        px = 1 - x if bits & 2 else x
        py = 1 - y if bits & 4 else y
        pc = 1 - core if bits & 1 else core
        return pc + 2 * px + 4 * py

    def at(bits):
        return (base + peer(bits), z)

    def near(d):
        return (z, jnp.where(z % 2 == 0, z + 1, z - 1), jnp.where(z < 2, 2, 1), jnp.where(z < 2, 3, 0))[d]

    def along(d):
        return (c, near(d))

    is_end = (z == 0) | (z == SPLIT - 1)
    is_mid = (z == 1) | (z == 2)
    to_mid = (c, jnp.where(z == 0, 1, 2))
    to_end = (c, jnp.where(z == 1, 0, 3))
    to_other = (c, jnp.where(z == 1, 2, 1))

    def remote(src, dst, send, recv, device):
        return pltpu.make_async_remote_copy(
            src_ref=src, dst_ref=dst, send_sem=send, recv_sem=recv, device_id=device, device_id_type=MESH
        )

    small = [
        pltpu.make_async_copy(src, dst, v_sem.at[i])
        for i, (src, dst) in enumerate(
            (
                (freq_index_hbm, freq_index), (time_index_hbm, time_index),
                (freq_table_hbm, freq_table), (time_table_hbm, time_table),
                (gain1_hbm, gain1), (shift1_hbm, shift1), (qv_bias_hbm, qv_bias), (proj_bias_hbm, proj_bias),
                (gain2_hbm, gain2), (shift2_hbm, shift2), (fc1_bias_hbm, fc1_bias), (fc2_bias_hbm, fc2_bias),
            )
        )
    ]
    weights = [
        pltpu.make_async_copy(src, dst, w_sem.at[i])
        for i, (src, dst) in enumerate(
            ((qkv_hbm, w_qkv), (proj_hbm, w_proj), (fc1_hbm, w_fc1), (fc2_hbm, w_fc2))
        )
    ]
    raw_tok = pltpu.make_async_copy(tokens, raw, raw_sem.at[0])
    raw_cot = pltpu.make_async_copy(cotangent, raw, raw_sem.at[1])
    raw_tok.start()
    for copy in weights[:2]:
        copy.start()
    barrier = pltpu.get_barrier_semaphore()
    for d in range(1, SPLIT):
        pl.semaphore_signal(barrier, inc=1, device_id=along(d), device_id_type=MESH)
    for bits in range(1, GROUP):
        pl.semaphore_signal(barrier, inc=1, device_id=at(bits), device_id_type=MESH)
    for copy in small:
        copy.start()

    chunks = range(0, width, step)

    def spread(src, dst, send, recv, n):
        here, i = pl.ds(n, step), n // step
        return [
            remote(src.at[near(d), :, here], dst.at[z, :, here], send.at[d - 1, i], recv.at[z, i], along(d))
            for d in range(SPLIT - 1, 0, -1)
        ]

    def keep(src, dst, recv, n):
        here = pl.ds(n, step)
        return pltpu.make_async_copy(src.at[z, :, here], dst.at[z, :, here], recv.at[z, n // step])

    def come(src, dst, send, recv, n, k):
        here, i = pl.ds(n, step), n // step
        return remote(src.at[k, :, here], dst.at[k, :, here], send.at[0, i], recv.at[k, i], along(1))

    def wait_block(src, dst, send, recv, n, k):
        @pl.when(z == k)
        def _():
            keep(src, dst, recv, n).wait()

        @pl.when(z != k)
        def _():
            come(src, dst, send, recv, n, k).wait_recv()

    def by_clip(staging, n):
        wide[...] = raw[:, :, pl.ds(n, step)].astype(F32)
        for k in range(SPLIT):
            staging[k, :, pl.ds(n, step)] = wide[:, k, :].astype(BF16)

    raw_tok.wait()
    for n in chunks:
        by_clip(staged, n)
        if n == 0:
            pl.semaphore_wait(barrier, SPLIT - 1 + GROUP - 1)
        for copy in spread(staged, tok_in, tok_s, tok_r, n):
            copy.start()
        keep(staged, tok_in, tok_r, n).start()
    raw_cot.start()
    raw_cot.wait()
    for copy in weights[2:]:
        copy.start()
    for n in chunks:
        by_clip(staged_grad, n)
        keep(staged_grad, cot_in, cot_r, n).start()
    for copy in small:
        copy.wait()

    lane = lax.broadcasted_iota(jnp.int32, (8, 128), 1)
    index = jnp.full((8, 128), -1, jnp.int32)
    for s in range(TKEEP):
        index = jnp.where(lane == s, time_index[z, s], index)
    for s in range(FKEEP):
        index = jnp.where(lane == SLOTS + s, freq_index[z, s] + TIMES, index)
    column = lax.broadcasted_iota(jnp.int32, (128, 128), 0)
    pick = jnp.where(column == index[:1], 1.0, 0.0)
    picks[...] = pick.astype(BF16)
    pay[...] = jnp.zeros_like(pay)
    pay[pl.ds(0, time_table.shape[0]), :] = time_table[...].astype(F32)
    pay[pl.ds(TIMES, freq_table.shape[0]), :] = freq_table[...].astype(F32)
    by_slot = dot(pick.T.astype(BF16), pay[...].astype(BF16)).astype(BF16)

    def slots_of(row_number, slot):
        block = sum((row_number >= padded * k).astype(jnp.int32) for k in range(1, SPLIT))
        inside = row_number - padded * block
        patch = row_number - (padded - rows) * block - 2
        frequency = sum((patch >= TKEEP * k).astype(jnp.int32) for k in range(1, FKEEP))
        time = patch - TKEEP * frequency
        hit = (slot == time) | (slot == SLOTS + frequency)
        return jnp.where(hit & (inside < rows) & (patch >= 0), 1.0, 0.0).astype(BF16)

    g1, s1 = row(gain1), row(shift1)
    bias_q, bias_v = qv_bias[0:1, :].astype(F32), qv_bias[1:2, :].astype(F32)
    weights[0].wait()
    for d in range(SPLIT):
        k = near(d)
        place = pl.multiple_of(padded * k, 32)
        block_rows = pl.ds(place, padded)
        number = lax.broadcasted_iota(jnp.int32, (padded, 128), 0) + place
        slot = lax.broadcasted_iota(jnp.int32, (padded, 128), 1)
        position = dot(slots_of(number, slot), by_slot)
        for n in chunks:
            if d == 0:
                keep(staged, tok_in, tok_r, n).wait()
            else:
                come(staged, tok_in, tok_s, tok_r, n, k).wait_recv()
        stream_in[pl.ds(place, rows), :] = tok_in[k].astype(F32) + position[:rows]
        stream_in[pl.ds(place + rows, padded - rows), :] = jnp.zeros((padded - rows, width), F32)
        hat, _ = normalize(stream_in[block_rows, :])
        normed[block_rows, :] = (hat * g1 + s1).astype(BF16)
        for t, (bias, scale) in enumerate(((bias_q, HDIM**-0.5), (None, 1.0), (bias_v, 1.0))):
            for n in range(0, width, step):
                part = dot(normed[block_rows, :], w_qkv[:, pl.ds(t * width + n, step)])
                if bias is not None:
                    part = part + bias[:, n : n + step]
                part = part.astype(BF16)
                if scale != 1.0:
                    part = part * jnp.asarray(scale, BF16)
                qkv[block_rows, pl.ds(t * width + n, step)] = part

    for n in chunks:
        for copy in spread(staged_grad, cot_in, cot_s, cot_r, n):
            copy.start()
    part_of = [jnp.where(core == side, 0, 2) for side in range(2)]

    def left_copy(i):
        if i >= 4:
            return remote(left.at[2, i], left.at[1, i], left_s.at[i], left_r.at[i], at(1))
        return left_quarter(i)

    def left_quarter(q):
        return remote(
            left.at[2, pl.ds(0, 4), q], left.at[1, pl.ds(0, 4), q], left_s.at[q], left_r.at[q], at(1)
        )

    def blocks_in(n):
        found = []
        for block in range(n // shard, -(-(n + step) // shard)):
            found.append((block, max(n, shard * block), min(n + step, shard * (block + 1))))
        return found

    def hand_all(i, source):
        for n in range(0, width, step):
            turned = source[:, pl.ds(n, step)].T
            for block, start, stop in blocks_in(n):
                at_row = pl.ds(start - shard * block, stop - start)
                left[part_of[block % 2], i, block // 2, at_row, :] = turned[start - n : stop - n]
        left_copy(i).start()

    def right_copy(g):
        return remote(
            right.at[g, pl.ds(0, many)], right.at[g, pl.ds(many, many)], right_s.at[g], right_r.at[g], at(1)
        )

    hand_all(6, normed)

    key_number = lax.broadcasted_iota(jnp.int32, (8, many), 1)
    key_block = sum((key_number >= padded * k).astype(jnp.int32) for k in range(1, SPLIT))
    key_mask = jnp.where(key_number - padded * key_block < rows, 0.0, -1e30)[:1]
    head_lane = lax.broadcasted_iota(jnp.int32, (8, 2 * HDIM), 1)
    one_head = [
        jnp.where(head_lane < HDIM, 1.0, 0.0)[:1].astype(BF16),
        jnp.where(head_lane < HDIM, 0.0, 1.0)[:1].astype(BF16),
    ]

    def lanes(t, p):
        return pl.ds(pl.multiple_of(t * width + p * (2 * HDIM), 2 * HDIM), 2 * HDIM)

    def scores_of(p, place):
        query, key = qkv[:, lanes(0, p)], qkv[:, lanes(1, p)]
        for h in range(2):
            place[:, pl.ds(h * many, many)] = dot(query * one_head[h], key, NT)

    def weigh(p, place):
        value = qkv[:, lanes(2, p)]
        for r in range(0, many, 64):
            here = pl.ds(r, 64)
            for h in range(2):
                scores = place[here, pl.ds(h * many, many)] + key_mask
                weight = jnp.exp(scores - jnp.max(scores, -1, keepdims=True))
                weight = weight * (1.0 / jnp.sum(weight, -1, keepdims=True))
                probs[p, here, pl.ds(h * many, many)] = weight.astype(BF16)
        both = jnp.concatenate([value * one_head[0], value * one_head[1]], 0)
        attended[:, lanes(0, p)] = dot(probs[p], both).astype(BF16)

    scores_of(0, work)

    @pl.loop(0, pairs // 2)
    def _(m):
        scores_of(2 * m + 1, mid)
        weigh(2 * m, work)
        scores_of(jnp.minimum(2 * m + 2, pairs - 1), work)
        weigh(2 * m + 1, mid)

    weights[1].wait()
    hand_all(5, attended)
    bias = row(proj_bias)
    for n in range(0, width, step):
        mid[:, pl.ds(n, step)] = (
            stream_in[:, pl.ds(n, step)]
            + dot(attended[...], w_proj[:, pl.ds(n, step)])
            + bias[:, n : n + step]
        )
    g2, s2 = row(gain2), row(shift2)

    @pl.loop(0, many // BLOCK)
    def _(b):
        at_row = pl.ds(pl.multiple_of(b * BLOCK, BLOCK), BLOCK)
        hat, _ = normalize(mid[at_row, :])
        normed[at_row, :] = (hat * g2 + s2).astype(BF16)

    def column_sums(value):
        return jnp.sum(value.astype(F32), 0, keepdims=True)

    def first_matrix(q, n):
        place = pl.ds(pl.multiple_of(q * width + n, 128), step)
        work[:, pl.ds(n, step)] = dot(normed[...], w_fc1[:, place]) + fc1_bias[place].astype(F32).reshape(1, step)

    def activate(q, n):
        parts = []
        for r in range(0, many, 64):
            here = pl.ds(r, 64)
            hidden = work[here, pl.ds(n, step)]
            cdf, pdf = normal_cdf_pdf(hidden)
            active = (hidden * cdf).astype(BF16)
            unit[8 + q, here, pl.ds(n, step)] = active
            right[1 + q, here, pl.ds(n, step)] = (cdf + hidden * pdf).astype(BF16)
            parts.append(active)
        turned = jnp.concatenate(parts, 0).T
        for block, start, stop in blocks_in(n):
            at_row = pl.ds(start - shard * block, stop - start)
            left[part_of[block // 4], block % 4, q, at_row, :] = turned[start - n : stop - n]

    weights[2].wait()
    hand_all(4, normed)
    first_matrix(0, 0)

    def quarter(q, more):
        for n in range(step, width, step):
            first_matrix(q, n)
            activate(q, n - step)
        if more:
            first_matrix(q + 1, 0)
        activate(q, width - step)
        left_quarter(q).start()

    @pl.loop(0, 3)
    def _(q):
        quarter(q, True)

    wide_cot[pl.ds(rows, padded - rows), :] = jnp.zeros((padded - rows, step), F32)
    for k in range(SPLIT):
        for n in chunks:
            wait_block(staged_grad, cot_in, cot_s, cot_r, n, k)
            wide_cot[pl.ds(0, rows), :] = cot_in[k, :, pl.ds(n, step)].astype(F32)
            right[0, pl.ds(padded * k, padded), pl.ds(n, step)] = wide_cot[...].astype(BF16)
    for n in range(0, width, step):
        pay[pl.ds(99 + 7, 1), pl.ds(n, step)] = column_sums(right[0, pl.ds(0, many), pl.ds(n, step)])
    right_copy(0).start()

    quarter(3, False)

    def grid_of(j):
        return unit.at[PARTS[j][0]].reshape(2, 2, shard, width)

    def span(j, part):
        i, start, size = PARTS[j]
        size = size * width // 6
        return pl.ds(start * width // 6 + part * size, size)

    def some(j, part):
        i, start, size = PARTS[j]
        return pl.ds(start * width // 12, size * width // 6)

    def one_copies(j):
        u, i, here = grid_of(j), PARTS[j][0], some(j, 0)
        return (
            remote(u.at[:, 1 - x, :, span(j, 0)], got1.at[i, 0, :, :, here], one_s.at[j, 0], one_r.at[j, 0], at(2)),
            remote(u.at[1 - y, :, :, span(j, 1)], got1.at[i, 1, :, :, here], one_s.at[j, 1], one_r.at[j, 1], at(4)),
        )

    def two_copies(j):
        u, i, here = grid_of(j), PARTS[j][0], some(j, 0)
        return (
            remote(u.at[1 - y, x, :, span(j, 0)], got2.at[i, 0, :, here], two_s.at[j, 0], two_r.at[j, 0], at(4)),
            remote(u.at[y, 1 - x, :, span(j, 1)], got2.at[i, 1, :, here], two_s.at[j, 1], two_r.at[j, 1], at(2)),
        )

    own_part = jnp.where(z == 2, 1, 0)
    oth_part = 1 - own_part
    end_first = jnp.where(z < 2, 1, 0)

    def place_of(j, part):
        i, start, size = PARTS[j]
        size = size * width // 6
        return pl.ds(pl.multiple_of(start * width // 6 + part * size, 128), size)

    def end_copy(j, which):
        cols = place_of(j, end_first if which == 0 else 1 - end_first)
        i = PARTS[j][0]
        return remote(
            grid_of(j).at[y, x, :, cols], end_in.at[i, :, cols], end_s.at[j, which], end_r.at[j, which], to_mid
        )

    def mid_copy(j):
        return remote(
            grid_of(j).at[y, x, :, place_of(j, oth_part)], mid_in.at[PARTS[j][0], :, some(j, 0)], mid_s.at[j],
            mid_r.at[j], to_other,
        )

    def fin_copy(j, part, which, device):
        here = final.at[PARTS[j][0], :, place_of(j, part)]
        return remote(here, here, fin_s.at[j, which], fin_r.at[j, part], device)

    def share_copy(j):
        i, start, size = PARTS[j]
        cols = pl.ds(start * width // 6, size * width // 3)
        return pltpu.make_async_copy(final.at[i, :, cols], shares_hbm.at[i, :, cols], share_s.at[j])

    waited = set()

    def product(j):
        i, start, size = PARTS[j]
        l = i if i < 4 else 4 if i < 8 else 5 if i == 8 else 6
        g = 0 if i < 4 else i - 3
        for other in range(4) if l < 4 else (l,):
            if ("left", other) not in waited:
                left_copy(other).wait_recv()
                waited.add(("left", other))
        if g not in waited:
            right_copy(g).wait_recv()
            waited.add(g)
        both = jnp.concatenate([left[k, l].reshape(4 * shard, many) for k in range(2)], 1)
        for n in range(start * width // 6, (start + 2 * size) * width // 6, step):
            part = dot(both, right[g, :, pl.ds(n, step)])
            unit[i, :, pl.ds(n, step)] = part.astype(BF16)
        for copy in one_copies(j):
            copy.start()

    def tick1(j):
        u, i, here = grid_of(j), PARTS[j][0], some(j, 0)
        first, second = one_copies(j)
        after_first, after_second = two_copies(j)
        a, b = span(j, 0), span(j, 1)
        first.wait_recv()
        u[1 - y, x, :, a] = (u[1 - y, x, :, a].astype(F32) + got1[i, 0, 1 - y, :, here].astype(F32)).astype(BF16)
        after_first.start()
        second.wait_recv()
        u[y, 1 - x, :, b] = (u[y, 1 - x, :, b].astype(F32) + got1[i, 1, 1 - x, :, here].astype(F32)).astype(BF16)
        after_second.start()

    def plane_sum(j, part):
        i, here = PARTS[j][0], some(j, 0)
        near = jnp.where(part == 0, y, x)
        return (
            grid_of(j)[y, x, :, place_of(j, part)].astype(F32)
            + got1[i, part, near, :, here].astype(F32)
            + got2[i, part, :, here].astype(F32)
        )

    def tick2(j):
        for copy in two_copies(j):
            copy.wait_recv()

        @pl.when(is_end)
        def _():
            for which in range(2):
                part = end_first if which == 0 else 1 - end_first
                grid_of(j)[y, x, :, place_of(j, part)] = plane_sum(j, part).astype(BF16)
                end_copy(j, which).start()

    def line_sum(j, part):
        return plane_sum(j, part) + end_in[PARTS[j][0], :, place_of(j, part)].astype(F32)

    def tick3(j):
        @pl.when(is_mid)
        def _():
            end_copy(j, 0).wait_recv()
            grid_of(j)[y, x, :, place_of(j, oth_part)] = line_sum(j, oth_part).astype(BF16)
            mid_copy(j).start()

    def tick4(j):
        @pl.when(is_mid)
        def _():
            i = PARTS[j][0]
            end_copy(j, 1).wait_recv()
            total = line_sum(j, own_part)
            mid_copy(j).wait_recv()
            total = total + mid_in[i, :, some(j, 0)].astype(F32)
            final[i, :, place_of(j, own_part)] = total.astype(BF16)
            fin_copy(j, own_part, 0, to_other).start()
            fin_copy(j, own_part, 1, to_end).start()

    def tick5(j):
        @pl.when(is_mid)
        def _():
            fin_copy(j, oth_part, 2, to_end).wait_recv()
            fin_copy(j, oth_part, 2, to_end).start()

        @pl.when(is_end)
        def _():
            fin_copy(j, 0, 0, to_mid).wait_recv()
            fin_copy(j, 1, 0, to_mid).wait_recv()

        share_copy(j).start()

    bias_out = row(fc2_bias)

    def block_out(n):
        if n == 0:
            for m in chunks:
                for copy in spread(staged, tok_in, tok_s, tok_r, m):
                    copy.wait_send()
        part = mid[:, pl.ds(n, step)] + bias_out[:, n : n + step]
        for q in range(4):
            part = part + dot(unit[8 + q], w_fc2[pl.ds(q * width, width), pl.ds(n, step)])
        for k in range(SPLIT):
            staged[k, :, pl.ds(n, step)] = part[padded * k : padded * k + rows].astype(BF16)
        for copy in spread(staged, out_hbm, out_s, out_r, n):
            copy.start()
        keep(staged, out_hbm, out_r, n).start()

    def grad_hidden(q):
        for n in range(0, width, step):
            part = dot(right[0, pl.ds(0, many), :], w_fc2[pl.ds(q * width + n, step), :], NT)
            part = (part * right[1 + q, pl.ds(0, many), pl.ds(n, step)].astype(F32)).astype(BF16)
            right[1 + q, pl.ds(0, many), pl.ds(n, step)] = part
            pay[pl.ds(99 + 8 + q, 1), pl.ds(n, step)] = column_sums(part)
        right_copy(1 + q).start()

    def grad_second():
        for n in range(0, width, step):
            part = None
            for q in range(4):
                term = dot(right[1 + q, pl.ds(0, many), :], w_fc1[pl.ds(n, step), pl.ds(q * width, width)], NT)
                part = term if part is None else part + term
            work[:, pl.ds(n, step)] = part

    def norm_back(grad, value, gain):
        hat, rstd = normalize(value)
        g = grad * gain
        back = rstd * (g - jnp.mean(g, -1, keepdims=True) - hat * jnp.mean(g * hat, -1, keepdims=True))
        return back, hat

    zero = jnp.zeros((1, width), F32)

    def second_norm():
        def block(b, sums):
            at_row = pl.ds(pl.multiple_of(b * BLOCK, BLOCK), BLOCK)
            grad = work[at_row, :]
            back, hat = norm_back(grad, mid[at_row, :], g2)
            back = back + right[0, at_row, :].astype(F32)
            mid[at_row, :] = back
            branch = back.astype(BF16)
            right[5, at_row, :] = branch
            return (
                sums[0] + column_sums(grad * hat),
                sums[1] + column_sums(grad),
                sums[2] + column_sums(branch),
            )

        sums = lax.fori_loop(0, many // BLOCK, block, (zero, zero, zero))
        pay[pl.ds(99 + 5, 1), :] = sums[0]
        pay[pl.ds(99 + 6, 1), :] = sums[1]
        pay[pl.ds(99 + 4, 1), :] = sums[2]
        right_copy(5).start()

    def grad_attended():
        for n in range(0, width, step):
            normed[:, pl.ds(n, step)] = dot(
                right[5, pl.ds(0, many), :], w_proj[pl.ds(n, step), :], NT
            ).astype(BF16)

    def attend_back(p):
        query, key, value = (qkv[:, lanes(t, p)] for t in range(3))
        grad_out = normed[:, lanes(0, p)]
        grads = None
        for h in range(2):
            weight_low = probs[p, :, pl.ds(h * many, many)]
            weight = weight_low.astype(F32)
            grad_probs = dot(grad_out * one_head[h], value, NT) * weight
            inner = jnp.sum(grad_probs, -1, keepdims=True)
            grad_scores = (grad_probs - weight * inner).astype(BF16)
            terms = (
                dot(grad_scores, key * one_head[h]),
                dot(grad_scores, query * one_head[h], TN),
                dot(weight_low, grad_out * one_head[h], TN),
            )
            grads = terms if grads is None else tuple(a + b for a, b in zip(grads, terms, strict=True))
        for t, (grad, scale) in enumerate(zip(grads, (HDIM**-0.5, 1.0, 1.0), strict=True)):
            low_grad = (grad * scale).astype(BF16)
            right[6 + t, pl.ds(0, many), lanes(0, p)] = low_grad
            if t != 1:
                pay[pl.ds(99 + 2 + t // 2, 1), lanes(0, p)] = column_sums(low_grad)

    def attention_back(s):
        @pl.loop(s * pairs // 3, (s + 1) * pairs // 3)
        def _(p):
            attend_back(p)

        if s == 2:
            for t in range(3):
                right_copy(6 + t).start()

    def grad_first():
        for n in range(0, width, step):
            part = None
            for t in range(3):
                term = dot(right[6 + t, pl.ds(0, many), :], w_qkv[pl.ds(n, step), pl.ds(t * width, width)], NT)
                part = term if part is None else part + term
            work[:, pl.ds(n, step)] = part

    def grad_copy(d):
        if d == 0:
            return pltpu.make_async_copy(staged_grad.at[z], grad_hbm.at[z], grad_r.at[z])
        return remote(staged_grad.at[near(d)], grad_hbm.at[z], grad_s.at[d - 1], grad_r.at[z], along(d))

    def first_norm():
        for n in chunks:
            for copy in spread(staged_grad, cot_in, cot_s, cot_r, n):
                copy.wait_send()
        sums = zero, zero
        for d in range(SPLIT - 1, -1, -1):
            k = near(d)

            def block(b, sums):
                at_row = pl.ds(pl.multiple_of(padded * k + b * (padded // 2), 16), padded // 2)
                grad = work[at_row, :]
                back, hat = norm_back(grad, stream_in[at_row, :], g1)
                mid[at_row, :] = mid[at_row, :] + back
                return sums[0] + column_sums(grad * hat), sums[1] + column_sums(grad)

            sums = lax.fori_loop(0, 2, block, sums)
            staged_grad[k] = mid[pl.ds(pl.multiple_of(padded * k, 32), padded), :][:rows].astype(BF16)
            grad_copy(d).start()
        first, second = sums
        pay[pl.ds(99, 1), :] = first
        pay[pl.ds(100, 1), :] = second

    def halves(v):
        high = v.astype(BF16)
        return high, (v - high.astype(F32)).astype(BF16)

    def pay_copy(bits):
        return remote(
            pay_low.at[pl.ds(16 * peer(bits), 16)], pay_in.at[low], pay_s.at[bits - 1], pay_r.at[low], at(bits)
        )

    def payz_copy(d):
        return remote(pay_mid.at[z], pay_mid.at[z], payz_s.at[d - 1], payz_r.at[z], along(d))

    def payo_copy(bits):
        return remote(pay_out.at[low], pay_out.at[low], payo_s.at[bits - 1], payo_r.at[low], at(bits))

    def position_tables():
        number = lax.broadcasted_iota(jnp.int32, (128, many), 1)
        slot = lax.broadcasted_iota(jnp.int32, (128, many), 0)
        slots = slots_of(number, slot)
        for n in range(0, width, step):
            by = sum(dot(slots, v) for v in halves(mid[:, pl.ds(n, step)]))
            table_grad = sum(dot(picks[...], v) for v in halves(by))
            pay[pl.ds(0, 99), pl.ds(n, step)] = table_grad[:99]
            pay[pl.ds(TIMES, 16), pl.ds(n, step)] = table_grad[TIMES:]
        pay[pl.ds(111, 1), :] = zero
        pay_low[...] = pay[...].astype(BF16)
        for bits in range(1, GROUP):
            pay_copy(bits).start()

    def pay_group():
        for bits in range(1, GROUP):
            remote(
                pay_low.at[pl.ds(0, 16)], pay_in.at[peer(bits)], pay_s.at[bits - 1], pay_r.at[peer(bits)], at(bits)
            ).wait_recv()
        pay_in[low] = pay_low[pl.ds(pl.multiple_of(16 * low, 16), 16), :]
        pay_mid[z] = sum(pay_in[s].astype(F32) for s in range(GROUP)).astype(BF16)
        for d in range(1, SPLIT):
            payz_copy(d).start()

    def pay_line():
        for d in range(1, SPLIT):
            k = near(d)
            remote(pay_mid.at[k], pay_mid.at[k], payz_s.at[d - 1], payz_r.at[k], along(d)).wait_recv()
        pay_out[low] = sum(pay_mid[s].astype(F32) for s in range(SPLIT)).astype(BF16)
        for bits in range(1, GROUP):
            payo_copy(bits).start()

    pieces = {
        "sec": grad_second, "sen": second_norm, "att": grad_attended, "fir": grad_first,
        "fin": first_norm, "tab": position_tables, "pay2": pay_group, "pay3": pay_line,
    }
    for n in chunks:
        pieces[f"out{n // step}"] = functools.partial(block_out, n)
    for q in range(4):
        pieces[f"gh{q}"] = functools.partial(grad_hidden, q)
    for s in range(3):
        pieces[f"ab{s}"] = functools.partial(attention_back, s)
    for i in range(len(PARTS)):
        pieces[f"t0_{i}"] = functools.partial(product, i)
        for k, tick in enumerate((tick1, tick2, tick3, tick4, tick5)):
            pieces[f"t{k + 1}_{i}"] = functools.partial(tick, i)
    assert sorted(ORDER) == sorted(pieces)
    weights[3].wait()
    for name in ORDER:
        pieces[name]()
    for bits in range(1, GROUP):
        remote(
            pay_out.at[low], pay_out.at[peer(bits)], payo_s.at[bits - 1], payo_r.at[peer(bits)], at(bits)
        ).wait_recv()
    last = pltpu.make_async_copy(pay_out, small_hbm, w_sem.at[0])
    last.start()

    for n in chunks:
        for copy in spread(staged, out_hbm, out_s, out_r, n):
            copy.wait_send()
        for k in range(SPLIT):
            wait_block(staged, out_hbm, out_s, out_r, n, k)
    grad_copy(0).wait()
    for d in range(1, SPLIT):
        grad_copy(d).wait_send()
        k = near(d)
        remote(staged_grad.at[k], grad_hbm.at[k], grad_s.at[0], grad_r.at[k], along(1)).wait_recv()
    for i in range(left.shape[1]):
        left_copy(i).wait_send()
    for g in range(right.shape[0]):
        right_copy(g).wait_send()

    for j in range(len(PARTS)):
        for copy in (*one_copies(j), *two_copies(j)):
            copy.wait_send()

    @pl.when(is_end)
    def _():
        for j in range(len(PARTS)):
            end_copy(j, 0).wait_send()
            end_copy(j, 1).wait_send()

    @pl.when(is_mid)
    def _():
        for j in range(len(PARTS)):
            mid_copy(j).wait_send()
            fin_copy(j, own_part, 0, to_other).wait_send()
            fin_copy(j, own_part, 1, to_end).wait_send()
            fin_copy(j, oth_part, 2, to_end).wait_send()

    for j in range(len(PARTS)):
        share_copy(j).wait()

    for bits in range(1, GROUP):
        pay_copy(bits).wait_send()
        payo_copy(bits).wait_send()
    for d in range(1, SPLIT):
        payz_copy(d).wait_send()
    last.wait()


def finish_kernel(
    out_in, grad_in, shares, small,
    out, grad, freq, time, gain1, shift1, qkv, qv_bias, proj, proj_bias, gain2, shift2, fc1, fc1_bias, fc2, fc2_bias,
    rows_in, wide, rows_out, parts, small_in, f_qkv, f_proj, f_fc1, f_fc2, f_time, f_freq, f_qv, lines,
    row_sem, part_sem, out_sem,
):
    width = wide.shape[2]
    shard = parts.shape[1]
    reads = [pltpu.make_async_copy(shares.at[i], parts.at[i], part_sem.at[i]) for i in range(UNITS)]
    moves = [pltpu.make_async_copy(src, rows_in.at[i], row_sem.at[i]) for i, src in enumerate((out_in, grad_in))]
    read_small = pltpu.make_async_copy(small, small_in, row_sem.at[2])
    for copy in (*reads, *moves, read_small):
        copy.start()
    line_of = lambda i: lines.at[pl.ds(i * width, width)]
    writes = [
        pltpu.make_async_copy(src, dst, out_sem.at[i])
        for i, (src, dst) in enumerate(
            (
                (f_fc2, fc2), (f_fc1, fc1), (f_proj, proj), (f_qkv, qkv), (rows_out.at[0], out), (rows_out.at[1], grad),
                (f_time, time), (f_freq, freq), (f_qv, qv_bias), (line_of(0), gain1), (line_of(1), shift1),
                (line_of(2), proj_bias), (line_of(3), gain2), (line_of(4), shift2), (line_of(5), fc2_bias),
                (lines.at[pl.ds(6 * width, 4 * width)], fc1_bias),
            )
        )
    ]
    for i in range(UNITS):
        reads[i].wait()
        value = parts[i].astype(F32)
        if i < 4:
            f_fc2[pl.ds(i * shard, shard), :] = value
        elif i < 8:
            f_fc1[:, pl.ds((i - 4) * width, width)] = value
        elif i == 8:
            f_proj[...] = value
        else:
            f_qkv[:, pl.ds((i - 9) * width, width)] = value
        if i in (3, 7, 8, 11):
            writes[(3, 7, 8, 11).index(i)].start()
    for i in range(2):
        moves[i].wait()
        for k in range(SPLIT):
            wide[:, k, :] = rows_in[i, k].astype(F32)
        rows_out[i] = wide[...].astype(BF16)
        writes[4 + i].start()
    read_small.wait()
    f_time[...] = small_in[pl.ds(0, time.shape[0]), :].astype(F32)
    f_freq[...] = small_in[pl.ds(TIMES, freq.shape[0]), :].astype(F32)
    rest = small_in[pl.ds(96, 16), :].astype(F32)[3:]
    f_qv[...] = rest[2:4]
    for at, i in enumerate((0, 1, 4, 5, 6, 7)):
        lines[pl.ds(at * width, width)] = rest[i : i + 1].reshape(width)
    for q in range(4):
        lines[pl.ds((6 + q) * width, width)] = rest[8 + q : 9 + q].reshape(width)
    for copy in writes[6:]:
        copy.start()
    for copy in writes:
        copy.wait()


def on_device(
    tokens, freq_index, time_index, freq_table, time_table,
    norm1_gain, norm1_shift, qkv_weight, qv_bias, proj_weight, proj_bias, norm2_gain, norm2_shift,
    fc1_weight, fc1_bias, fc2_weight, fc2_bias, cotangent,
):
    clips, rows, width = tokens.shape
    count = len(PARTS)
    pieces = width // (256 if width % 256 == 0 else 128)
    times, freqs = time_table.shape[0], freq_table.shape[0]
    groups = lax.axis_size("seq")
    clip_devices = lax.axis_size("clip")
    assert clips == SPLIT and groups == SPLIT and clip_devices % GROUP == 0
    hidden_width = fc1_weight.shape[1]
    assert hidden_width == 4 * width
    padded = -(-rows // 32) * 32
    many = SPLIT * padded
    shard = width // GROUP
    half = width // 2
    heads = width // HDIM

    anywhere = pl.BlockSpec(memory_space=pl.ANY)
    dma = pltpu.SemaphoreType.DMA
    blocks = (SPLIT, rows, width)
    vectors = (freq_table, time_table, norm1_gain, norm1_shift, qv_bias, proj_bias, norm2_gain, norm2_shift, fc1_bias, fc2_bias)
    small_scratch = [pltpu.SMEM(v.shape, v.dtype) for v in (freq_index, time_index)]
    small_scratch += [pltpu.VMEM(v.shape, v.dtype) for v in vectors]
    tokens, cotangent = (v.transpose(1, 0, 2) for v in (tokens, cotangent))
    out, grad, shares, small = pl.pallas_call(
        block_kernel,
        out_shape=(
            jax.ShapeDtypeStruct(blocks, BF16),
            jax.ShapeDtypeStruct(blocks, BF16),
            jax.ShapeDtypeStruct((UNITS, shard, width), BF16),
            jax.ShapeDtypeStruct((GROUP, 16, width), BF16),
        ),
        in_specs=[anywhere] * 18,
        out_specs=(anywhere,) * 4,
        scratch_shapes=[
            *small_scratch,
            pltpu.VMEM((rows, SPLIT, width), BF16),
            pltpu.VMEM((rows, SPLIT, 256 if width % 256 == 0 else 128), F32),
            pltpu.VMEM((width, 3 * width), BF16),
            pltpu.VMEM((width, width), BF16),
            pltpu.VMEM((width, hidden_width), BF16),
            pltpu.VMEM((hidden_width, width), BF16),
            pltpu.VMEM(blocks, BF16),
            pltpu.VMEM(blocks, BF16),
            pltpu.VMEM((padded, 256 if width % 256 == 0 else 128), F32),
            pltpu.VMEM((many, width), F32),
            pltpu.VMEM((many, width), BF16),
            pltpu.VMEM((many, 3 * width), BF16),
            pltpu.VMEM((heads // 2, many, 2 * many), BF16),
            pltpu.VMEM((many, width), BF16),
            pltpu.VMEM((many, width), F32),
            pltpu.VMEM((many, width), F32),
            pltpu.VMEM((3, 7, 4, shard, many), BF16),
            pltpu.VMEM((9, 2 * many, width), BF16),
            pltpu.VMEM((UNITS, 4 * shard, width), BF16),
            pltpu.VMEM((UNITS, 2, 2, shard, half), BF16),
            pltpu.VMEM((UNITS, 2, shard, half), BF16),
            pltpu.VMEM((UNITS, shard, width), BF16),
            pltpu.VMEM((UNITS, shard, half), BF16),
            pltpu.VMEM((UNITS, shard, width), BF16),
            pltpu.VMEM(blocks, BF16),
            pltpu.VMEM(blocks, BF16),
            pltpu.VMEM((128, 128), BF16),
            pltpu.VMEM((128, width), F32),
            pltpu.VMEM((128, width), BF16),
            pltpu.VMEM((GROUP, 16, width), BF16),
            pltpu.VMEM((SPLIT, 16, width), BF16),
            pltpu.VMEM((GROUP, 16, width), BF16),
            dma((12,)), dma((2,)), dma((4,)),
            dma((3, pieces)), dma((4, pieces)), dma((3, pieces)), dma((4, pieces)), dma((3, pieces)), dma((4, pieces)),
            dma((3,)), dma((4,)),
            dma((7,)), dma((7,)), dma((9,)), dma((9,)),
            dma((count, 2)), dma((count, 2)), dma((count, 2)), dma((count, 2)),
            dma((count, 2)), dma((count, 2)), dma((count,)), dma((count,)),
            dma((count, 3)), dma((count, 2)), dma((count,)),
            dma((7,)), dma((8,)), dma((3,)), dma((4,)), dma((7,)), dma((8,)),
        ],
        compiler_params=pltpu.CompilerParams(
            collective_id=1, has_side_effects=True, vmem_limit_bytes=63 * 2**20
        ),
    )(
        tokens, freq_index, time_index, freq_table, time_table,
        norm1_gain, norm1_shift, qkv_weight, qv_bias, proj_weight, proj_bias, norm2_gain, norm2_shift,
        fc1_weight, fc1_bias, fc2_weight, fc2_bias, cotangent,
    )
    small = small.reshape(GROUP * 16, width)
    if clip_devices == GROUP:
        shape = lambda *dims: jax.ShapeDtypeStruct(dims, F32)
        inner = jax.ShapeDtypeStruct((rows, SPLIT, width), BF16)
        line = shape(width)
        results = (
            inner, inner, shape(freqs, width), shape(times, width), line, line, shape(shard, 3 * width),
            shape(2, width), shape(shard, width), line, line, line, shape(shard, 4 * width),
            shape(4 * width), shape(4 * shard, width), line,
        )
        out, grad, *others = pl.pallas_call(
            finish_kernel,
            out_shape=results,
            in_specs=[anywhere] * 4,
            out_specs=(anywhere,) * 16,
            scratch_shapes=[
                pltpu.VMEM((2, *blocks), BF16),
                pltpu.VMEM((rows, SPLIT, width), F32),
                pltpu.VMEM((2, rows, SPLIT, width), BF16),
                pltpu.VMEM((UNITS, shard, width), BF16),
                pltpu.VMEM((GROUP * 16, width), BF16),
                pltpu.VMEM((shard, 3 * width), F32),
                pltpu.VMEM((shard, width), F32),
                pltpu.VMEM((shard, 4 * width), F32),
                pltpu.VMEM((4 * shard, width), F32),
                pltpu.VMEM((times, width), F32),
                pltpu.VMEM((freqs, width), F32),
                pltpu.VMEM((2, width), F32),
                pltpu.VMEM((10 * width,), F32),
                dma((3,)), dma((UNITS,)), dma((16,)),
            ],
            compiler_params=pltpu.CompilerParams(vmem_limit_bytes=62 * 2**20),
        )(out, grad, shares, small)
        return (out.transpose(1, 0, 2), grad.transpose(1, 0, 2), *others)
    shares, small = shares.astype(F32), small.astype(F32)
    wide_count = clip_devices // GROUP
    same = [[h * GROUP + b for h in range(wide_count)] for b in range(GROUP)]
    small = lax.psum(small, "clip", axis_index_groups=same)
    fc2 = shares[:4].reshape(4 * shard, width)
    rest = shares[4:].transpose(1, 0, 2).reshape(shard, 8 * width)
    summed = [
        lax.psum_scatter(v, "clip", scatter_dimension=0, axis_index_groups=same, tiled=True)
        for v in (fc2, rest)
    ]
    moves = [(h * GROUP + b, b * wide_count + h) for h in range(wide_count) for b in range(GROUP)]
    fc2, rest = (lax.ppermute(v, "clip", moves) for v in summed)
    fc1, proj, qkv = rest[:, : 4 * width], rest[:, 4 * width : 5 * width], rest[:, 5 * width :]
    return (
        out,
        grad,
        small[TIMES : TIMES + freqs],
        small[:times],
        small[99],
        small[100],
        qkv,
        small[101:103],
        proj,
        small[103],
        small[104],
        small[105],
        fc1,
        small[107:111].reshape(-1),
        fc2,
        small[106],
    )


def solution(mesh):
    rows_split, clip_split = P("clip", "seq", None), P("clip", None)
    in_specs = (rows_split, clip_split, clip_split) + (P(),) * 14 + (rows_split,)
    out_specs = (
        rows_split, rows_split, P(), P(), P(), P(), clip_split, P(), clip_split, P(), P(), P(), clip_split,
        P(), clip_split, P(),
    )
    return jax.shard_map(on_device, mesh=mesh, in_specs=in_specs, out_specs=out_specs, check_vma=False)
```

```python
import functools

import jax
import jax.numpy as jnp
from jax import lax
from jax.experimental import pallas as pl
from jax.experimental.pallas import tpu as pltpu
from jax.sharding import PartitionSpec as P

F32, BF16 = jnp.float32, jnp.bfloat16
MESH = pl.DeviceIdType.MESH
HDIM = 64
FKEEP = 7
TKEEP = 54
SPLIT = 4
GROUP = 8
PAD = 16
TIMES = 112
SLOTS = 64
BLOCK = 96
UNITS = 12
PARTS = tuple((i, 0, 3) for i in range(UNITS))
ORDER = (
    "out0", "out1", "t0_0", "gh0", "gh1", "t0_1", "gh2", "gh3", "sec", "out2", "t0_2", "sen", "att", "t1_1", "t1_0",
    "t0_3", "t0_4", "t0_5", "ab0", "t2_1", "t3_1", "t2_0", "ab1", "t3_0", "ab2", "t4_1", "t1_2", "t0_6", "fir",
    "t4_0", "fin", "t1_3", "t0_7", "t1_5", "t1_4", "t0_8", "t1_6", "t2_3", "t3_3", "t2_2", "t2_5", "t1_7", "t0_9",
    "t2_4", "t3_2", "t5_1", "t3_5", "t4_2", "t1_8", "t2_6", "t0_10", "t4_3", "tab", "t4_5", "t0_11", "t3_4", "t2_7",
    "t5_2", "t2_8", "t1_9", "t5_3", "t3_6", "t3_7", "t5_5", "t1_10", "t5_0", "t4_4", "t4_6", "t3_8", "pay2", "t4_7",
    "t1_11", "t2_9", "t4_8", "t2_11", "t2_10", "t5_4", "t3_9", "pay3", "t5_7", "t3_11", "t5_6", "t4_9", "t3_10",
    "t5_8", "t4_11", "t5_9", "t4_10", "t5_11", "t5_10",
)
NT = (((1,), (1,)), ((), ()))
TN = (((0,), (0,)), ((), ()))
LOG2_E = 1.4426950408889634
ERF_P = 0.3275911
ERF_C = (0.254829592, -0.284496736, 1.421413741, -1.453152027, 1.061405429)


def dot(a, b, dims=(((1,), (0,)), ((), ()))):
    return lax.dot_general(a, b, dims, preferred_element_type=F32)


def normal_cdf_pdf(h):
    bell = jnp.exp2(h * h * (-0.5 * LOG2_E))
    base = 1.0 + (ERF_P * 2.0**-0.5) * jnp.abs(h)
    t = pl.reciprocal(base, approx=True)
    t = t * (2.0 - base * t)
    tail = 0.5 * ERF_C[4]
    for coefficient in ERF_C[3::-1]:
        tail = tail * t + 0.5 * coefficient
    tail = tail * t * bell
    return jnp.where(h >= 0, 1.0 - tail, tail), bell * 0.3989422804014327


def normalize(v):
    centered = v - jnp.mean(v, -1, keepdims=True)
    rstd = lax.rsqrt(jnp.mean(centered * centered, -1, keepdims=True) + 1e-06)
    return centered * rstd, rstd


def row(ref):
    return ref[...].astype(F32).reshape(1, -1)


def block_kernel(
    tokens, freq_index_hbm, time_index_hbm, freq_table_hbm, time_table_hbm,
    gain1_hbm, shift1_hbm, qkv_hbm, qv_bias_hbm, proj_hbm, proj_bias_hbm, gain2_hbm, shift2_hbm,
    fc1_hbm, fc1_bias_hbm, fc2_hbm, fc2_bias_hbm, cotangent,
    out_hbm, grad_hbm, shares_hbm, small_hbm,
    freq_index, time_index, freq_table, time_table, gain1, shift1, qv_bias, proj_bias, gain2, shift2, fc1_bias, fc2_bias,
    raw, wide, w_qkv, w_proj, w_fc1, w_fc2, tok_in, cot_in, wide_cot, stream_in, normed, qkv, probs, attended, mid,
    work, left, right, unit, got1, got2, end_in, mid_in, final, staged, staged_grad,
    picks, pay, pay_low, pay_in, pay_mid, pay_out,
    v_sem, raw_sem, w_sem, tok_s, tok_r, cot_s, cot_r, out_s, out_r, grad_s, grad_r, left_s, left_r, right_s, right_r,
    one_s, one_r, two_s, two_r, end_s, end_r, mid_s, mid_r, fin_s, fin_r, share_s,
    pay_s, pay_r, payz_s, payz_r, payo_s, payo_r,
):
    width = stream_in.shape[1]
    rows = tok_in.shape[1]
    padded = stream_in.shape[0] // SPLIT
    many = stream_in.shape[0]
    shard = width // GROUP
    half = width // 2
    pairs = width // (2 * HDIM)
    heavy = 3 * width
    step = 256 if width % 256 == 0 else 128

    c, z = lax.axis_index("clip"), lax.axis_index("seq")
    low = c % GROUP
    core, x, y = low % 2, (low // 2) % 2, low // 4
    base = c - low

    def peer(bits):
        px = 1 - x if bits & 2 else x
        py = 1 - y if bits & 4 else y
        pc = 1 - core if bits & 1 else core
        return pc + 2 * px + 4 * py

    def at(bits):
        return (base + peer(bits), z)

    def near(d):
        places = (z, jnp.where(z % 2 == 0, z + 1, z - 1), jnp.where(z < 2, 2, 1), jnp.where(z < 2, 3, 0))
        if isinstance(d, int):
            return places[d]
        return jnp.where(d == 0, places[0], jnp.where(d == 1, places[1], jnp.where(d == 2, places[2], places[3])))

    def along(d):
        return (c, near(d))

    is_end = (z == 0) | (z == SPLIT - 1)
    is_mid = (z == 1) | (z == 2)
    to_mid = (c, jnp.where(z == 0, 1, 2))
    to_end = (c, jnp.where(z == 1, 0, 3))
    to_other = (c, jnp.where(z == 1, 2, 1))

    def remote(src, dst, send, recv, device):
        return pltpu.make_async_remote_copy(
            src_ref=src, dst_ref=dst, send_sem=send, recv_sem=recv, device_id=device, device_id_type=MESH
        )

    small = [
        pltpu.make_async_copy(src, dst, v_sem.at[i])
        for i, (src, dst) in enumerate(
            (
                (freq_index_hbm, freq_index), (time_index_hbm, time_index),
                (freq_table_hbm, freq_table), (time_table_hbm, time_table),
                (gain1_hbm, gain1), (shift1_hbm, shift1), (qv_bias_hbm, qv_bias), (proj_bias_hbm, proj_bias),
                (gain2_hbm, gain2), (shift2_hbm, shift2), (fc1_bias_hbm, fc1_bias), (fc2_bias_hbm, fc2_bias),
            )
        )
    ]
    weights = [
        pltpu.make_async_copy(src, dst, w_sem.at[i])
        for i, (src, dst) in enumerate(
            ((qkv_hbm, w_qkv), (proj_hbm, w_proj), (fc1_hbm, w_fc1), (fc2_hbm, w_fc2))
        )
    ]
    raw_tok = pltpu.make_async_copy(tokens, raw, raw_sem.at[0])
    raw_cot = pltpu.make_async_copy(cotangent, raw, raw_sem.at[1])
    raw_tok.start()
    for copy in weights[:2]:
        copy.start()
    barrier = pltpu.get_barrier_semaphore()
    for d in range(1, SPLIT):
        pl.semaphore_signal(barrier, inc=1, device_id=along(d), device_id_type=MESH)
    for bits in range(1, GROUP):
        pl.semaphore_signal(barrier, inc=1, device_id=at(bits), device_id_type=MESH)
    for copy in small:
        copy.start()

    chunks = range(0, width, step)

    def spread(src, dst, send, recv, n):
        here, i = pl.ds(n, step), n // step
        return [
            remote(src.at[near(d), :, here], dst.at[z, :, here], send.at[d - 1, i], recv.at[z, i], along(d))
            for d in range(SPLIT - 1, 0, -1)
        ]

    def keep(src, dst, recv, n):
        here = pl.ds(n, step)
        return pltpu.make_async_copy(src.at[z, :, here], dst.at[z, :, here], recv.at[z, n // step])

    def come(src, dst, send, recv, n, k):
        here, i = pl.ds(n, step), n // step
        return remote(src.at[k, :, here], dst.at[k, :, here], send.at[0, i], recv.at[k, i], along(1))

    def wait_block(src, dst, send, recv, n, k):
        @pl.when(z == k)
        def _():
            keep(src, dst, recv, n).wait()

        @pl.when(z != k)
        def _():
            come(src, dst, send, recv, n, k).wait_recv()

    def by_clip(staging, n):
        wide[...] = raw[:, :, pl.ds(n, step)].astype(F32)
        for k in range(SPLIT):
            staging[k, :, pl.ds(n, step)] = wide[:, k, :].astype(BF16)

    raw_tok.wait()
    for n in chunks:
        by_clip(staged, n)
        if n == 0:
            pl.semaphore_wait(barrier, SPLIT - 1 + GROUP - 1)
        for copy in spread(staged, tok_in, tok_s, tok_r, n):
            copy.start()
        keep(staged, tok_in, tok_r, n).start()
    raw_cot.start()
    raw_cot.wait()
    for copy in weights[2:]:
        copy.start()
    for n in chunks:
        by_clip(staged_grad, n)
        keep(staged_grad, cot_in, cot_r, n).start()
    for copy in small:
        copy.wait()

    lane = lax.broadcasted_iota(jnp.int32, (8, 128), 1)
    index = jnp.full((8, 128), -1, jnp.int32)
    for s in range(TKEEP):
        index = jnp.where(lane == s, time_index[z, s], index)
    for s in range(FKEEP):
        index = jnp.where(lane == SLOTS + s, freq_index[z, s] + TIMES, index)
    column = lax.broadcasted_iota(jnp.int32, (128, 128), 0)
    pick = jnp.where(column == index[:1], 1.0, 0.0)
    picks[...] = pick.astype(BF16)
    pay[...] = jnp.zeros_like(pay)
    pay[pl.ds(0, time_table.shape[0]), :] = time_table[...].astype(F32)
    pay[pl.ds(TIMES, freq_table.shape[0]), :] = freq_table[...].astype(F32)
    by_slot = dot(pick.T.astype(BF16), pay[...].astype(BF16)).astype(BF16)

    def slots_of(row_number, slot):
        block = sum((row_number >= padded * k).astype(jnp.int32) for k in range(1, SPLIT))
        inside = row_number - padded * block
        patch = row_number - (padded - rows) * block - 2
        frequency = sum((patch >= TKEEP * k).astype(jnp.int32) for k in range(1, FKEEP))
        time = patch - TKEEP * frequency
        hit = (slot == time) | (slot == SLOTS + frequency)
        return jnp.where(hit & (inside < rows) & (patch >= 0), 1.0, 0.0).astype(BF16)

    g1, s1 = row(gain1), row(shift1)
    bias_q, bias_v = qv_bias[0:1, :].astype(F32), qv_bias[1:2, :].astype(F32)
    weights[0].wait()
    @pl.loop(0, SPLIT)
    def _(d):
        k = near(d)
        place = pl.multiple_of(padded * k, 32)
        block_rows = pl.ds(place, padded)
        number = lax.broadcasted_iota(jnp.int32, (padded, 128), 0) + place
        slot = lax.broadcasted_iota(jnp.int32, (padded, 128), 1)
        position = dot(slots_of(number, slot), by_slot)
        for n in chunks:
            wait_block(staged, tok_in, tok_s, tok_r, n, k)
        stream_in[pl.ds(place, rows), :] = tok_in[k].astype(F32) + position[:rows]
        stream_in[pl.ds(place + rows, padded - rows), :] = jnp.zeros((padded - rows, width), F32)
        hat, _ = normalize(stream_in[block_rows, :])
        normed[block_rows, :] = (hat * g1 + s1).astype(BF16)
        for t, (bias, scale) in enumerate(((bias_q, HDIM**-0.5), (None, 1.0), (bias_v, 1.0))):
            for n in range(0, width, step):
                part = dot(normed[block_rows, :], w_qkv[:, pl.ds(t * width + n, step)])
                if bias is not None:
                    part = part + bias[:, n : n + step]
                part = part.astype(BF16)
                if scale != 1.0:
                    part = part * jnp.asarray(scale, BF16)
                qkv[block_rows, pl.ds(t * width + n, step)] = part

    for n in chunks:
        for copy in spread(staged_grad, cot_in, cot_s, cot_r, n):
            copy.start()
    part_of = [jnp.where(core == side, 0, 2) for side in range(2)]

    def left_copy(i):
        if i >= 4:
            return remote(left.at[2, i], left.at[1, i], left_s.at[i], left_r.at[i], at(1))
        return left_quarter(i)

    def left_quarter(q):
        return remote(
            left.at[2, pl.ds(0, 4), q], left.at[1, pl.ds(0, 4), q], left_s.at[q], left_r.at[q], at(1)
        )

    def blocks_in(n):
        found = []
        for block in range(n // shard, -(-(n + step) // shard)):
            found.append((block, max(n, shard * block), min(n + step, shard * (block + 1))))
        return found

    def hand_all(i, source):
        for n in range(0, width, step):
            turned = source[:, pl.ds(n, step)].T
            for block, start, stop in blocks_in(n):
                at_row = pl.ds(start - shard * block, stop - start)
                left[part_of[block % 2], i, block // 2, at_row, :] = turned[start - n : stop - n]
        left_copy(i).start()

    def right_copy(g):
        return remote(
            right.at[g, pl.ds(0, many)], right.at[g, pl.ds(many, many)], right_s.at[g], right_r.at[g], at(1)
        )

    hand_all(6, normed)

    key_number = lax.broadcasted_iota(jnp.int32, (8, many), 1)
    key_block = sum((key_number >= padded * k).astype(jnp.int32) for k in range(1, SPLIT))
    key_mask = jnp.where(key_number - padded * key_block < rows, 0.0, -1e30)[:1]
    head_lane = lax.broadcasted_iota(jnp.int32, (8, 2 * HDIM), 1)
    one_head = [
        jnp.where(head_lane < HDIM, 1.0, 0.0)[:1].astype(BF16),
        jnp.where(head_lane < HDIM, 0.0, 1.0)[:1].astype(BF16),
    ]

    def lanes(t, p):
        return pl.ds(pl.multiple_of(t * width + p * (2 * HDIM), 2 * HDIM), 2 * HDIM)

    def scores_of(p, place):
        query, key = qkv[:, lanes(0, p)], qkv[:, lanes(1, p)]
        for h in range(2):
            place[:, pl.ds(h * many, many)] = dot(query * one_head[h], key, NT)

    def weigh(p, place):
        value = qkv[:, lanes(2, p)]
        for r in range(0, many, 64):
            here = pl.ds(r, 64)
            for h in range(2):
                scores = place[here, pl.ds(h * many, many)] + key_mask
                weight = jnp.exp(scores - jnp.max(scores, -1, keepdims=True))
                weight = weight * (1.0 / jnp.sum(weight, -1, keepdims=True))
                probs[p, here, pl.ds(h * many, many)] = weight.astype(BF16)
        both = jnp.concatenate([value * one_head[0], value * one_head[1]], 0)
        attended[:, lanes(0, p)] = dot(probs[p], both).astype(BF16)

    scores_of(0, work)

    @pl.loop(0, pairs // 2)
    def _(m):
        scores_of(2 * m + 1, mid)
        weigh(2 * m, work)
        scores_of(jnp.minimum(2 * m + 2, pairs - 1), work)
        weigh(2 * m + 1, mid)

    weights[1].wait()
    hand_all(5, attended)
    bias = row(proj_bias)
    for n in range(0, width, step):
        mid[:, pl.ds(n, step)] = (
            stream_in[:, pl.ds(n, step)]
            + dot(attended[...], w_proj[:, pl.ds(n, step)])
            + bias[:, n : n + step]
        )
    g2, s2 = row(gain2), row(shift2)

    @pl.loop(0, many // BLOCK)
    def _(b):
        at_row = pl.ds(pl.multiple_of(b * BLOCK, BLOCK), BLOCK)
        hat, _ = normalize(mid[at_row, :])
        normed[at_row, :] = (hat * g2 + s2).astype(BF16)

    def column_sums(value):
        return jnp.sum(value.astype(F32), 0, keepdims=True)

    def first_matrix(q, n):
        place = pl.ds(pl.multiple_of(q * width + n, 128), step)
        work[:, pl.ds(n, step)] = dot(normed[...], w_fc1[:, place]) + fc1_bias[place].astype(F32).reshape(1, step)

    def activate(q, n):
        parts = []
        for r in range(0, many, 64):
            here = pl.ds(r, 64)
            hidden = work[here, pl.ds(n, step)]
            cdf, pdf = normal_cdf_pdf(hidden)
            active = (hidden * cdf).astype(BF16)
            unit[8 + q, here, pl.ds(n, step)] = active
            right[1 + q, here, pl.ds(n, step)] = (cdf + hidden * pdf).astype(BF16)
            parts.append(active)
        turned = jnp.concatenate(parts, 0).T
        for block, start, stop in blocks_in(n):
            at_row = pl.ds(start - shard * block, stop - start)
            left[part_of[block // 4], block % 4, q, at_row, :] = turned[start - n : stop - n]

    weights[2].wait()
    hand_all(4, normed)
    first_matrix(0, 0)

    def quarter(q, more):
        for n in range(step, width, step):
            first_matrix(q, n)
            activate(q, n - step)
        if more:
            first_matrix(q + 1, 0)
        activate(q, width - step)
        left_quarter(q).start()

    @pl.loop(0, 3)
    def _(q):
        quarter(q, True)

    wide_cot[pl.ds(rows, padded - rows), :] = jnp.zeros((padded - rows, step), F32)
    for k in range(SPLIT):
        for n in chunks:
            wait_block(staged_grad, cot_in, cot_s, cot_r, n, k)
            wide_cot[pl.ds(0, rows), :] = cot_in[k, :, pl.ds(n, step)].astype(F32)
            right[0, pl.ds(padded * k, padded), pl.ds(n, step)] = wide_cot[...].astype(BF16)
    for n in range(0, width, step):
        pay[pl.ds(99 + 7, 1), pl.ds(n, step)] = column_sums(right[0, pl.ds(0, many), pl.ds(n, step)])
    right_copy(0).start()

    quarter(3, False)

    def grid_of(j):
        return unit.at[PARTS[j][0]].reshape(2, 2, shard, width)

    def span(j, part):
        i, start, size = PARTS[j]
        size = size * width // 6
        return pl.ds(start * width // 6 + part * size, size)

    def some(j, part):
        i, start, size = PARTS[j]
        return pl.ds(start * width // 12, size * width // 6)

    def one_copies(j):
        u, i, here = grid_of(j), PARTS[j][0], some(j, 0)
        return (
            remote(u.at[:, 1 - x, :, span(j, 0)], got1.at[i, 0, :, :, here], one_s.at[j, 0], one_r.at[j, 0], at(2)),
            remote(u.at[1 - y, :, :, span(j, 1)], got1.at[i, 1, :, :, here], one_s.at[j, 1], one_r.at[j, 1], at(4)),
        )

    def two_copies(j):
        u, i, here = grid_of(j), PARTS[j][0], some(j, 0)
        return (
            remote(u.at[1 - y, x, :, span(j, 0)], got2.at[i, 0, :, here], two_s.at[j, 0], two_r.at[j, 0], at(4)),
            remote(u.at[y, 1 - x, :, span(j, 1)], got2.at[i, 1, :, here], two_s.at[j, 1], two_r.at[j, 1], at(2)),
        )

    own_part = jnp.where(z == 2, 1, 0)
    oth_part = 1 - own_part
    end_first = jnp.where(z < 2, 1, 0)

    def place_of(j, part):
        i, start, size = PARTS[j]
        size = size * width // 6
        return pl.ds(pl.multiple_of(start * width // 6 + part * size, 128), size)

    def end_copy(j, which):
        cols = place_of(j, end_first if which == 0 else 1 - end_first)
        i = PARTS[j][0]
        return remote(
            grid_of(j).at[y, x, :, cols], end_in.at[i, :, cols], end_s.at[j, which], end_r.at[j, which], to_mid
        )

    def mid_copy(j):
        return remote(
            grid_of(j).at[y, x, :, place_of(j, oth_part)], mid_in.at[PARTS[j][0], :, some(j, 0)], mid_s.at[j],
            mid_r.at[j], to_other,
        )

    def fin_copy(j, part, which, device):
        here = final.at[PARTS[j][0], :, place_of(j, part)]
        return remote(here, here, fin_s.at[j, which], fin_r.at[j, part], device)

    def share_copy(j):
        i, start, size = PARTS[j]
        cols = pl.ds(start * width // 6, size * width // 3)
        return pltpu.make_async_copy(final.at[i, :, cols], shares_hbm.at[i, :, cols], share_s.at[j])

    waited = set()

    def product(j):
        i, start, size = PARTS[j]
        l = i if i < 4 else 4 if i < 8 else 5 if i == 8 else 6
        g = 0 if i < 4 else i - 3
        for other in range(4) if l < 4 else (l,):
            if ("left", other) not in waited:
                left_copy(other).wait_recv()
                waited.add(("left", other))
        if g not in waited:
            right_copy(g).wait_recv()
            waited.add(g)
        both = jnp.concatenate([left[k, l].reshape(4 * shard, many) for k in range(2)], 1)
        for n in range(start * width // 6, (start + 2 * size) * width // 6, step):
            part = dot(both, right[g, :, pl.ds(n, step)])
            unit[i, :, pl.ds(n, step)] = part.astype(BF16)
        for copy in one_copies(j):
            copy.start()

    def tick1(j):
        u, i, here = grid_of(j), PARTS[j][0], some(j, 0)
        first, second = one_copies(j)
        after_first, after_second = two_copies(j)
        a, b = span(j, 0), span(j, 1)
        first.wait_recv()
        u[1 - y, x, :, a] = (u[1 - y, x, :, a].astype(F32) + got1[i, 0, 1 - y, :, here].astype(F32)).astype(BF16)
        after_first.start()
        second.wait_recv()
        u[y, 1 - x, :, b] = (u[y, 1 - x, :, b].astype(F32) + got1[i, 1, 1 - x, :, here].astype(F32)).astype(BF16)
        after_second.start()

    def plane_sum(j, part):
        i, here = PARTS[j][0], some(j, 0)
        near = jnp.where(part == 0, y, x)
        return (
            grid_of(j)[y, x, :, place_of(j, part)].astype(F32)
            + got1[i, part, near, :, here].astype(F32)
            + got2[i, part, :, here].astype(F32)
        )

    def tick2(j):
        for copy in two_copies(j):
            copy.wait_recv()

        @pl.when(is_end)
        def _():
            for which in range(2):
                part = end_first if which == 0 else 1 - end_first
                grid_of(j)[y, x, :, place_of(j, part)] = plane_sum(j, part).astype(BF16)
                end_copy(j, which).start()

    def line_sum(j, part):
        return plane_sum(j, part) + end_in[PARTS[j][0], :, place_of(j, part)].astype(F32)

    def tick3(j):
        @pl.when(is_mid)
        def _():
            end_copy(j, 0).wait_recv()
            grid_of(j)[y, x, :, place_of(j, oth_part)] = line_sum(j, oth_part).astype(BF16)
            mid_copy(j).start()

    def tick4(j):
        @pl.when(is_mid)
        def _():
            i = PARTS[j][0]
            end_copy(j, 1).wait_recv()
            total = line_sum(j, own_part)
            mid_copy(j).wait_recv()
            total = total + mid_in[i, :, some(j, 0)].astype(F32)
            final[i, :, place_of(j, own_part)] = total.astype(BF16)
            fin_copy(j, own_part, 0, to_other).start()
            fin_copy(j, own_part, 1, to_end).start()

    def tick5(j):
        @pl.when(is_mid)
        def _():
            fin_copy(j, oth_part, 2, to_end).wait_recv()
            fin_copy(j, oth_part, 2, to_end).start()

        @pl.when(is_end)
        def _():
            fin_copy(j, 0, 0, to_mid).wait_recv()
            fin_copy(j, 1, 0, to_mid).wait_recv()

        share_copy(j).start()

    bias_out = row(fc2_bias)

    def block_out(n):
        if n == 0:
            for m in chunks:
                for copy in spread(staged, tok_in, tok_s, tok_r, m):
                    copy.wait_send()
        part = mid[:, pl.ds(n, step)] + bias_out[:, n : n + step]
        for q in range(4):
            part = part + dot(unit[8 + q], w_fc2[pl.ds(q * width, width), pl.ds(n, step)])
        for k in range(SPLIT):
            staged[k, :, pl.ds(n, step)] = part[padded * k : padded * k + rows].astype(BF16)
        for copy in spread(staged, out_hbm, out_s, out_r, n):
            copy.start()
        keep(staged, out_hbm, out_r, n).start()

    def grad_hidden(q):
        for n in range(0, width, step):
            part = dot(right[0, pl.ds(0, many), :], w_fc2[pl.ds(q * width + n, step), :], NT)
            part = (part * right[1 + q, pl.ds(0, many), pl.ds(n, step)].astype(F32)).astype(BF16)
            right[1 + q, pl.ds(0, many), pl.ds(n, step)] = part
            pay[pl.ds(99 + 8 + q, 1), pl.ds(n, step)] = column_sums(part)
        right_copy(1 + q).start()

    def grad_second():
        for n in range(0, width, step):
            part = None
            for q in range(4):
                term = dot(right[1 + q, pl.ds(0, many), :], w_fc1[pl.ds(n, step), pl.ds(q * width, width)], NT)
                part = term if part is None else part + term
            work[:, pl.ds(n, step)] = part

    def norm_back(grad, value, gain):
        hat, rstd = normalize(value)
        g = grad * gain
        back = rstd * (g - jnp.mean(g, -1, keepdims=True) - hat * jnp.mean(g * hat, -1, keepdims=True))
        return back, hat

    zero = jnp.zeros((1, width), F32)

    def second_norm():
        def block(b, sums):
            at_row = pl.ds(pl.multiple_of(b * BLOCK, BLOCK), BLOCK)
            grad = work[at_row, :]
            back, hat = norm_back(grad, mid[at_row, :], g2)
            back = back + right[0, at_row, :].astype(F32)
            mid[at_row, :] = back
            branch = back.astype(BF16)
            right[5, at_row, :] = branch
            return (
                sums[0] + column_sums(grad * hat),
                sums[1] + column_sums(grad),
                sums[2] + column_sums(branch),
            )

        sums = lax.fori_loop(0, many // BLOCK, block, (zero, zero, zero))
        pay[pl.ds(99 + 5, 1), :] = sums[0]
        pay[pl.ds(99 + 6, 1), :] = sums[1]
        pay[pl.ds(99 + 4, 1), :] = sums[2]
        right_copy(5).start()

    def grad_attended():
        for n in range(0, width, step):
            normed[:, pl.ds(n, step)] = dot(
                right[5, pl.ds(0, many), :], w_proj[pl.ds(n, step), :], NT
            ).astype(BF16)

    def attend_back(p):
        query, key, value = (qkv[:, lanes(t, p)] for t in range(3))
        grad_out = normed[:, lanes(0, p)]
        grads = None
        for h in range(2):
            weight_low = probs[p, :, pl.ds(h * many, many)]
            weight = weight_low.astype(F32)
            grad_probs = dot(grad_out * one_head[h], value, NT) * weight
            inner = jnp.sum(grad_probs, -1, keepdims=True)
            grad_scores = (grad_probs - weight * inner).astype(BF16)
            terms = (
                dot(grad_scores, key * one_head[h]),
                dot(grad_scores, query * one_head[h], TN),
                dot(weight_low, grad_out * one_head[h], TN),
            )
            grads = terms if grads is None else tuple(a + b for a, b in zip(grads, terms, strict=True))
        for t, (grad, scale) in enumerate(zip(grads, (HDIM**-0.5, 1.0, 1.0), strict=True)):
            low_grad = (grad * scale).astype(BF16)
            right[6 + t, pl.ds(0, many), lanes(0, p)] = low_grad
            if t != 1:
                pay[pl.ds(99 + 2 + t // 2, 1), lanes(0, p)] = column_sums(low_grad)

    def attention_back(s):
        @pl.loop(s * pairs // 3, (s + 1) * pairs // 3)
        def _(p):
            attend_back(p)

        if s == 2:
            for t in range(3):
                right_copy(6 + t).start()

    def grad_first():
        for n in range(0, width, step):
            part = None
            for t in range(3):
                term = dot(right[6 + t, pl.ds(0, many), :], w_qkv[pl.ds(n, step), pl.ds(t * width, width)], NT)
                part = term if part is None else part + term
            work[:, pl.ds(n, step)] = part

    def own_grad():
        return pltpu.make_async_copy(staged_grad.at[z], grad_hbm.at[z], grad_r.at[z])

    def grad_copy(d):
        return remote(staged_grad.at[near(d)], grad_hbm.at[z], grad_s.at[d - 1], grad_r.at[z], along(d))

    def first_norm():
        for n in chunks:
            for copy in spread(staged_grad, cot_in, cot_s, cot_r, n):
                copy.wait_send()
        def block(t, sums):
            d = SPLIT - 1 - t
            k = near(d)
            at_row = pl.ds(pl.multiple_of(padded * k, 32), padded)
            grad = work[at_row, :]
            back, hat = norm_back(grad, stream_in[at_row, :], g1)
            back = mid[at_row, :] + back
            mid[at_row, :] = back
            staged_grad[k] = back[:rows].astype(BF16)

            @pl.when(d == 0)
            def _():
                own_grad().start()

            @pl.when(d > 0)
            def _():
                grad_copy(d).start()

            return sums[0] + column_sums(grad * hat), sums[1] + column_sums(grad)

        sums = lax.fori_loop(0, SPLIT, block, (zero, zero))
        first, second = sums
        pay[pl.ds(99, 1), :] = first
        pay[pl.ds(100, 1), :] = second

    def halves(v):
        high = v.astype(BF16)
        return high, (v - high.astype(F32)).astype(BF16)

    def pay_copy(bits):
        return remote(
            pay_low.at[pl.ds(16 * peer(bits), 16)], pay_in.at[low], pay_s.at[bits - 1], pay_r.at[low], at(bits)
        )

    def payz_copy(d):
        return remote(pay_mid.at[z], pay_mid.at[z], payz_s.at[d - 1], payz_r.at[z], along(d))

    def payo_copy(bits):
        return remote(pay_out.at[low], pay_out.at[low], payo_s.at[bits - 1], payo_r.at[low], at(bits))

    def position_tables():
        number = lax.broadcasted_iota(jnp.int32, (128, many), 1)
        slot = lax.broadcasted_iota(jnp.int32, (128, many), 0)
        slots = slots_of(number, slot)
        for n in range(0, width, step):
            by = sum(dot(slots, v) for v in halves(mid[:, pl.ds(n, step)]))
            table_grad = sum(dot(picks[...], v) for v in halves(by))
            pay[pl.ds(0, 99), pl.ds(n, step)] = table_grad[:99]
            pay[pl.ds(TIMES, 16), pl.ds(n, step)] = table_grad[TIMES:]
        pay[pl.ds(111, 1), :] = zero
        pay_low[...] = pay[...].astype(BF16)
        for bits in range(1, GROUP):
            pay_copy(bits).start()

    def pay_group():
        for bits in range(1, GROUP):
            remote(
                pay_low.at[pl.ds(0, 16)], pay_in.at[peer(bits)], pay_s.at[bits - 1], pay_r.at[peer(bits)], at(bits)
            ).wait_recv()
        pay_in[low] = pay_low[pl.ds(pl.multiple_of(16 * low, 16), 16), :]
        pay_mid[z] = sum(pay_in[s].astype(F32) for s in range(GROUP)).astype(BF16)
        for d in range(1, SPLIT):
            payz_copy(d).start()

    def pay_line():
        for d in range(1, SPLIT):
            k = near(d)
            remote(pay_mid.at[k], pay_mid.at[k], payz_s.at[d - 1], payz_r.at[k], along(d)).wait_recv()
        pay_out[low] = sum(pay_mid[s].astype(F32) for s in range(SPLIT)).astype(BF16)
        for bits in range(1, GROUP):
            payo_copy(bits).start()

    pieces = {
        "sec": grad_second, "sen": second_norm, "att": grad_attended, "fir": grad_first,
        "fin": first_norm, "tab": position_tables, "pay2": pay_group, "pay3": pay_line,
    }
    for n in chunks:
        pieces[f"out{n // step}"] = functools.partial(block_out, n)
    for q in range(4):
        pieces[f"gh{q}"] = functools.partial(grad_hidden, q)
    for s in range(3):
        pieces[f"ab{s}"] = functools.partial(attention_back, s)
    for i in range(len(PARTS)):
        pieces[f"t0_{i}"] = functools.partial(product, i)
        for k, tick in enumerate((tick1, tick2, tick3, tick4, tick5)):
            pieces[f"t{k + 1}_{i}"] = functools.partial(tick, i)
    assert sorted(ORDER) == sorted(pieces)
    weights[3].wait()
    for name in ORDER:
        pieces[name]()
    for bits in range(1, GROUP):
        remote(
            pay_out.at[low], pay_out.at[peer(bits)], payo_s.at[bits - 1], payo_r.at[peer(bits)], at(bits)
        ).wait_recv()
    last = pltpu.make_async_copy(pay_out, small_hbm, w_sem.at[0])
    last.start()

    for n in chunks:
        for copy in spread(staged, out_hbm, out_s, out_r, n):
            copy.wait_send()
        for k in range(SPLIT):
            wait_block(staged, out_hbm, out_s, out_r, n, k)
    own_grad().wait()
    for d in range(1, SPLIT):
        grad_copy(d).wait_send()
        k = near(d)
        remote(staged_grad.at[k], grad_hbm.at[k], grad_s.at[0], grad_r.at[k], along(1)).wait_recv()
    for i in range(left.shape[1]):
        left_copy(i).wait_send()
    for g in range(right.shape[0]):
        right_copy(g).wait_send()

    for j in range(len(PARTS)):
        for copy in (*one_copies(j), *two_copies(j)):
            copy.wait_send()

    @pl.when(is_end)
    def _():
        for j in range(len(PARTS)):
            end_copy(j, 0).wait_send()
            end_copy(j, 1).wait_send()

    @pl.when(is_mid)
    def _():
        for j in range(len(PARTS)):
            mid_copy(j).wait_send()
            fin_copy(j, own_part, 0, to_other).wait_send()
            fin_copy(j, own_part, 1, to_end).wait_send()
            fin_copy(j, oth_part, 2, to_end).wait_send()

    for j in range(len(PARTS)):
        share_copy(j).wait()

    for bits in range(1, GROUP):
        pay_copy(bits).wait_send()
        payo_copy(bits).wait_send()
    for d in range(1, SPLIT):
        payz_copy(d).wait_send()
    last.wait()


def finish_kernel(
    out_in, grad_in, shares, small,
    out, grad, freq, time, gain1, shift1, qkv, qv_bias, proj, proj_bias, gain2, shift2, fc1, fc1_bias, fc2, fc2_bias,
    rows_in, wide, rows_out, parts, small_in, f_qkv, f_proj, f_fc1, f_fc2, f_time, f_freq, f_qv, lines,
    row_sem, part_sem, out_sem,
):
    width = wide.shape[2]
    shard = parts.shape[1]
    reads = [pltpu.make_async_copy(shares.at[i], parts.at[i], part_sem.at[i]) for i in range(UNITS)]
    moves = [pltpu.make_async_copy(src, rows_in.at[i], row_sem.at[i]) for i, src in enumerate((out_in, grad_in))]
    read_small = pltpu.make_async_copy(small, small_in, row_sem.at[2])
    for copy in (*reads, *moves, read_small):
        copy.start()
    line_of = lambda i: lines.at[pl.ds(i * width, width)]
    writes = [
        pltpu.make_async_copy(src, dst, out_sem.at[i])
        for i, (src, dst) in enumerate(
            (
                (f_fc2, fc2), (f_fc1, fc1), (f_proj, proj), (f_qkv, qkv), (rows_out.at[0], out), (rows_out.at[1], grad),
                (f_time, time), (f_freq, freq), (f_qv, qv_bias), (line_of(0), gain1), (line_of(1), shift1),
                (line_of(2), proj_bias), (line_of(3), gain2), (line_of(4), shift2), (line_of(5), fc2_bias),
                (lines.at[pl.ds(6 * width, 4 * width)], fc1_bias),
            )
        )
    ]
    for i in range(UNITS):
        reads[i].wait()
        value = parts[i].astype(F32)
        if i < 4:
            f_fc2[pl.ds(i * shard, shard), :] = value
        elif i < 8:
            f_fc1[:, pl.ds((i - 4) * width, width)] = value
        elif i == 8:
            f_proj[...] = value
        else:
            f_qkv[:, pl.ds((i - 9) * width, width)] = value
        if i in (3, 7, 8, 11):
            writes[(3, 7, 8, 11).index(i)].start()
    for i in range(2):
        moves[i].wait()
        for k in range(SPLIT):
            wide[:, k, :] = rows_in[i, k].astype(F32)
        rows_out[i] = wide[...].astype(BF16)
        writes[4 + i].start()
    read_small.wait()
    f_time[...] = small_in[pl.ds(0, time.shape[0]), :].astype(F32)
    f_freq[...] = small_in[pl.ds(TIMES, freq.shape[0]), :].astype(F32)
    rest = small_in[pl.ds(96, 16), :].astype(F32)[3:]
    f_qv[...] = rest[2:4]
    for at, i in enumerate((0, 1, 4, 5, 6, 7)):
        lines[pl.ds(at * width, width)] = rest[i : i + 1].reshape(width)
    for q in range(4):
        lines[pl.ds((6 + q) * width, width)] = rest[8 + q : 9 + q].reshape(width)
    for copy in writes[6:]:
        copy.start()
    for copy in writes:
        copy.wait()


def on_device(
    tokens, freq_index, time_index, freq_table, time_table,
    norm1_gain, norm1_shift, qkv_weight, qv_bias, proj_weight, proj_bias, norm2_gain, norm2_shift,
    fc1_weight, fc1_bias, fc2_weight, fc2_bias, cotangent,
):
    clips, rows, width = tokens.shape
    count = len(PARTS)
    pieces = width // (256 if width % 256 == 0 else 128)
    times, freqs = time_table.shape[0], freq_table.shape[0]
    groups = lax.axis_size("seq")
    clip_devices = lax.axis_size("clip")
    assert clips == SPLIT and groups == SPLIT and clip_devices % GROUP == 0
    hidden_width = fc1_weight.shape[1]
    assert hidden_width == 4 * width
    padded = -(-rows // 32) * 32
    many = SPLIT * padded
    shard = width // GROUP
    half = width // 2
    heads = width // HDIM

    anywhere = pl.BlockSpec(memory_space=pl.ANY)
    dma = pltpu.SemaphoreType.DMA
    blocks = (SPLIT, rows, width)
    vectors = (freq_table, time_table, norm1_gain, norm1_shift, qv_bias, proj_bias, norm2_gain, norm2_shift, fc1_bias, fc2_bias)
    small_scratch = [pltpu.SMEM(v.shape, v.dtype) for v in (freq_index, time_index)]
    small_scratch += [pltpu.VMEM(v.shape, v.dtype) for v in vectors]
    tokens, cotangent = (v.transpose(1, 0, 2) for v in (tokens, cotangent))
    out, grad, shares, small = pl.pallas_call(
        block_kernel,
        out_shape=(
            jax.ShapeDtypeStruct(blocks, BF16),
            jax.ShapeDtypeStruct(blocks, BF16),
            jax.ShapeDtypeStruct((UNITS, shard, width), BF16),
            jax.ShapeDtypeStruct((GROUP, 16, width), BF16),
        ),
        in_specs=[anywhere] * 18,
        out_specs=(anywhere,) * 4,
        scratch_shapes=[
            *small_scratch,
            pltpu.VMEM((rows, SPLIT, width), BF16),
            pltpu.VMEM((rows, SPLIT, 256 if width % 256 == 0 else 128), F32),
            pltpu.VMEM((width, 3 * width), BF16),
            pltpu.VMEM((width, width), BF16),
            pltpu.VMEM((width, hidden_width), BF16),
            pltpu.VMEM((hidden_width, width), BF16),
            pltpu.VMEM(blocks, BF16),
            pltpu.VMEM(blocks, BF16),
            pltpu.VMEM((padded, 256 if width % 256 == 0 else 128), F32),
            pltpu.VMEM((many, width), F32),
            pltpu.VMEM((many, width), BF16),
            pltpu.VMEM((many, 3 * width), BF16),
            pltpu.VMEM((heads // 2, many, 2 * many), BF16),
            pltpu.VMEM((many, width), BF16),
            pltpu.VMEM((many, width), F32),
            pltpu.VMEM((many, width), F32),
            pltpu.VMEM((3, 7, 4, shard, many), BF16),
            pltpu.VMEM((9, 2 * many, width), BF16),
            pltpu.VMEM((UNITS, 4 * shard, width), BF16),
            pltpu.VMEM((UNITS, 2, 2, shard, half), BF16),
            pltpu.VMEM((UNITS, 2, shard, half), BF16),
            pltpu.VMEM((UNITS, shard, width), BF16),
            pltpu.VMEM((UNITS, shard, half), BF16),
            pltpu.VMEM((UNITS, shard, width), BF16),
            pltpu.VMEM(blocks, BF16),
            pltpu.VMEM(blocks, BF16),
            pltpu.VMEM((128, 128), BF16),
            pltpu.VMEM((128, width), F32),
            pltpu.VMEM((128, width), BF16),
            pltpu.VMEM((GROUP, 16, width), BF16),
            pltpu.VMEM((SPLIT, 16, width), BF16),
            pltpu.VMEM((GROUP, 16, width), BF16),
            dma((12,)), dma((2,)), dma((4,)),
            dma((3, pieces)), dma((4, pieces)), dma((3, pieces)), dma((4, pieces)), dma((3, pieces)), dma((4, pieces)),
            dma((3,)), dma((4,)),
            dma((7,)), dma((7,)), dma((9,)), dma((9,)),
            dma((count, 2)), dma((count, 2)), dma((count, 2)), dma((count, 2)),
            dma((count, 2)), dma((count, 2)), dma((count,)), dma((count,)),
            dma((count, 3)), dma((count, 2)), dma((count,)),
            dma((7,)), dma((8,)), dma((3,)), dma((4,)), dma((7,)), dma((8,)),
        ],
        compiler_params=pltpu.CompilerParams(
            collective_id=1, has_side_effects=True, vmem_limit_bytes=63 * 2**20
        ),
    )(
        tokens, freq_index, time_index, freq_table, time_table,
        norm1_gain, norm1_shift, qkv_weight, qv_bias, proj_weight, proj_bias, norm2_gain, norm2_shift,
        fc1_weight, fc1_bias, fc2_weight, fc2_bias, cotangent,
    )
    small = small.reshape(GROUP * 16, width)
    if clip_devices == GROUP:
        shape = lambda *dims: jax.ShapeDtypeStruct(dims, F32)
        inner = jax.ShapeDtypeStruct((rows, SPLIT, width), BF16)
        line = shape(width)
        results = (
            inner, inner, shape(freqs, width), shape(times, width), line, line, shape(shard, 3 * width),
            shape(2, width), shape(shard, width), line, line, line, shape(shard, 4 * width),
            shape(4 * width), shape(4 * shard, width), line,
        )
        out, grad, *others = pl.pallas_call(
            finish_kernel,
            out_shape=results,
            in_specs=[anywhere] * 4,
            out_specs=(anywhere,) * 16,
            scratch_shapes=[
                pltpu.VMEM((2, *blocks), BF16),
                pltpu.VMEM((rows, SPLIT, width), F32),
                pltpu.VMEM((2, rows, SPLIT, width), BF16),
                pltpu.VMEM((UNITS, shard, width), BF16),
                pltpu.VMEM((GROUP * 16, width), BF16),
                pltpu.VMEM((shard, 3 * width), F32),
                pltpu.VMEM((shard, width), F32),
                pltpu.VMEM((shard, 4 * width), F32),
                pltpu.VMEM((4 * shard, width), F32),
                pltpu.VMEM((times, width), F32),
                pltpu.VMEM((freqs, width), F32),
                pltpu.VMEM((2, width), F32),
                pltpu.VMEM((10 * width,), F32),
                dma((3,)), dma((UNITS,)), dma((16,)),
            ],
            compiler_params=pltpu.CompilerParams(vmem_limit_bytes=62 * 2**20),
        )(out, grad, shares, small)
        return (out.transpose(1, 0, 2), grad.transpose(1, 0, 2), *others)
    shares, small = shares.astype(F32), small.astype(F32)
    wide_count = clip_devices // GROUP
    same = [[h * GROUP + b for h in range(wide_count)] for b in range(GROUP)]
    small = lax.psum(small, "clip", axis_index_groups=same)
    fc2 = shares[:4].reshape(4 * shard, width)
    rest = shares[4:].transpose(1, 0, 2).reshape(shard, 8 * width)
    summed = [
        lax.psum_scatter(v, "clip", scatter_dimension=0, axis_index_groups=same, tiled=True)
        for v in (fc2, rest)
    ]
    moves = [(h * GROUP + b, b * wide_count + h) for h in range(wide_count) for b in range(GROUP)]
    fc2, rest = (lax.ppermute(v, "clip", moves) for v in summed)
    fc1, proj, qkv = rest[:, : 4 * width], rest[:, 4 * width : 5 * width], rest[:, 5 * width :]
    return (
        out,
        grad,
        small[TIMES : TIMES + freqs],
        small[:times],
        small[99],
        small[100],
        qkv,
        small[101:103],
        proj,
        small[103],
        small[104],
        small[105],
        fc1,
        small[107:111].reshape(-1),
        fc2,
        small[106],
    )


def solution(mesh):
    rows_split, clip_split = P("clip", "seq", None), P("clip", None)
    in_specs = (rows_split, clip_split, clip_split) + (P(),) * 14 + (rows_split,)
    out_specs = (
        rows_split, rows_split, P(), P(), P(), P(), clip_split, P(), clip_split, P(), P(), P(), clip_split,
        P(), clip_split, P(),
    )
    return jax.shard_map(on_device, mesh=mesh, in_specs=in_specs, out_specs=out_specs, check_vma=False)
```

```python
import functools

import jax
import jax.numpy as jnp
from jax import lax
from jax.experimental import pallas as pl
from jax.experimental.pallas import tpu as pltpu
from jax.sharding import PartitionSpec as P

F32, BF16 = jnp.float32, jnp.bfloat16
MESH = pl.DeviceIdType.MESH
HDIM = 64
FKEEP = 7
TKEEP = 54
SPLIT = 4
GROUP = 8
PAD = 16
TIMES = 112
SLOTS = 64
BLOCK = 96
UNITS = 12
PARTS = tuple((i, 0, 3) for i in range(UNITS))
ORDER = (
    "out0", "out1", "t0_0", "gh0", "gh1", "t0_1", "gh2", "gh3", "sec", "out2", "t0_2", "sen", "att", "t1_1", "t1_0",
    "t0_3", "t0_4", "t0_5", "ab0", "t2_1", "t3_1", "t2_0", "ab1", "t3_0", "ab2", "t4_1", "t1_2", "t0_6", "fir",
    "t4_0", "fin", "t1_3", "t0_7", "t1_5", "t1_4", "t0_8", "t1_6", "t2_3", "t3_3", "t2_2", "t2_5", "t1_7", "t0_9",
    "t2_4", "t3_2", "t5_1", "t3_5", "t4_2", "t1_8", "t2_6", "t0_10", "t4_3", "tab", "t4_5", "t0_11", "t3_4", "t2_7",
    "t5_2", "t2_8", "t1_9", "t5_3", "t3_6", "t3_7", "t5_5", "t1_10", "t5_0", "t4_4", "t4_6", "t3_8", "pay2", "t4_7",
    "t1_11", "t2_9", "t4_8", "t2_11", "t2_10", "t5_4", "t3_9", "pay3", "t5_7", "t3_11", "t5_6", "t4_9", "t3_10",
    "t5_8", "t4_11", "t5_9", "t4_10", "t5_11", "t5_10",
)
NT = (((1,), (1,)), ((), ()))
TN = (((0,), (0,)), ((), ()))
LOG2_E = 1.4426950408889634
ERF_P = 0.3275911
ERF_C = (0.254829592, -0.284496736, 1.421413741, -1.453152027, 1.061405429)


def dot(a, b, dims=(((1,), (0,)), ((), ()))):
    return lax.dot_general(a, b, dims, preferred_element_type=F32)


def normal_cdf_pdf(h):
    bell = jnp.exp2(h * h * (-0.5 * LOG2_E))
    base = 1.0 + (ERF_P * 2.0**-0.5) * jnp.abs(h)
    t = pl.reciprocal(base, approx=True)
    t = t * (2.0 - base * t)
    tail = 0.5 * ERF_C[4]
    for coefficient in ERF_C[3::-1]:
        tail = tail * t + 0.5 * coefficient
    tail = tail * t * bell
    return jnp.where(h >= 0, 1.0 - tail, tail), bell * 0.3989422804014327


def normalize(v):
    centered = v - jnp.mean(v, -1, keepdims=True)
    rstd = lax.rsqrt(jnp.mean(centered * centered, -1, keepdims=True) + 1e-06)
    return centered * rstd, rstd


def row(ref):
    return ref[...].astype(F32).reshape(1, -1)


def block_kernel(
    tokens, freq_index_hbm, time_index_hbm, freq_table_hbm, time_table_hbm,
    gain1_hbm, shift1_hbm, qkv_hbm, qv_bias_hbm, proj_hbm, proj_bias_hbm, gain2_hbm, shift2_hbm,
    fc1_hbm, fc1_bias_hbm, fc2_hbm, fc2_bias_hbm, cotangent,
    out_hbm, grad_hbm, shares_hbm, small_hbm,
    freq_index, time_index, freq_table, time_table, gain1, shift1, qv_bias, proj_bias, gain2, shift2, fc1_bias, fc2_bias,
    raw, wide, w_qkv, w_proj, w_fc1, w_fc2, tok_in, cot_in, wide_cot, stream_in, normed, qkv, probs, attended, mid,
    work, left, right, unit, got1, got2, end_in, mid_in, final, staged, staged_grad,
    picks, pay, pay_low, pay_in, pay_mid, pay_out,
    v_sem, raw_sem, w_sem, tok_s, tok_r, cot_s, cot_r, out_s, out_r, grad_s, grad_r, left_s, left_r, right_s, right_r,
    one_s, one_r, two_s, two_r, end_s, end_r, mid_s, mid_r, fin_s, fin_r, share_s,
    pay_s, pay_r, payz_s, payz_r, payo_s, payo_r,
):
    width = stream_in.shape[1]
    rows = tok_in.shape[1]
    padded = stream_in.shape[0] // SPLIT
    many = stream_in.shape[0]
    shard = width // GROUP
    half = width // 2
    pairs = width // (2 * HDIM)
    heavy = 3 * width
    step = 256 if width % 256 == 0 else 128

    c, z = lax.axis_index("clip"), lax.axis_index("seq")
    low = c % GROUP
    core, x, y = low % 2, (low // 2) % 2, low // 4
    base = c - low

    def peer(bits):
        px = 1 - x if bits & 2 else x
        py = 1 - y if bits & 4 else y
        pc = 1 - core if bits & 1 else core
        return pc + 2 * px + 4 * py

    def at(bits):
        return (base + peer(bits), z)

    def near(d):
        places = (z, jnp.where(z % 2 == 0, z + 1, z - 1), jnp.where(z < 2, 2, 1), jnp.where(z < 2, 3, 0))
        if isinstance(d, int):
            return places[d]
        return jnp.where(d == 0, places[0], jnp.where(d == 1, places[1], jnp.where(d == 2, places[2], places[3])))

    def along(d):
        return (c, near(d))

    is_end = (z == 0) | (z == SPLIT - 1)
    is_mid = (z == 1) | (z == 2)
    to_mid = (c, jnp.where(z == 0, 1, 2))
    to_end = (c, jnp.where(z == 1, 0, 3))
    to_other = (c, jnp.where(z == 1, 2, 1))

    def remote(src, dst, send, recv, device):
        return pltpu.make_async_remote_copy(
            src_ref=src, dst_ref=dst, send_sem=send, recv_sem=recv, device_id=device, device_id_type=MESH
        )

    small = [
        pltpu.make_async_copy(src, dst, v_sem.at[i])
        for i, (src, dst) in enumerate(
            (
                (freq_index_hbm, freq_index), (time_index_hbm, time_index),
                (freq_table_hbm, freq_table), (time_table_hbm, time_table),
                (gain1_hbm, gain1), (shift1_hbm, shift1), (qv_bias_hbm, qv_bias), (proj_bias_hbm, proj_bias),
                (gain2_hbm, gain2), (shift2_hbm, shift2), (fc1_bias_hbm, fc1_bias), (fc2_bias_hbm, fc2_bias),
            )
        )
    ]
    weights = [
        pltpu.make_async_copy(src, dst, w_sem.at[i])
        for i, (src, dst) in enumerate(
            ((qkv_hbm, w_qkv), (proj_hbm, w_proj), (fc1_hbm, w_fc1), (fc2_hbm, w_fc2))
        )
    ]
    raw_tok = pltpu.make_async_copy(tokens, raw, raw_sem.at[0])
    raw_cot = pltpu.make_async_copy(cotangent, raw, raw_sem.at[1])
    raw_tok.start()
    for copy in weights[:2]:
        copy.start()
    barrier = pltpu.get_barrier_semaphore()
    for d in range(1, SPLIT):
        pl.semaphore_signal(barrier, inc=1, device_id=along(d), device_id_type=MESH)
    for bits in range(1, GROUP):
        pl.semaphore_signal(barrier, inc=1, device_id=at(bits), device_id_type=MESH)
    for copy in small:
        copy.start()

    chunks = range(0, width, step)

    def spread(src, dst, send, recv, n):
        here, i = pl.ds(n, step), n // step
        return [
            remote(src.at[near(d), :, here], dst.at[z, :, here], send.at[d - 1, i], recv.at[z, i], along(d))
            for d in range(SPLIT - 1, 0, -1)
        ]

    def keep(src, dst, recv, n):
        here = pl.ds(n, step)
        return pltpu.make_async_copy(src.at[z, :, here], dst.at[z, :, here], recv.at[z, n // step])

    def come(src, dst, send, recv, n, k):
        here, i = pl.ds(n, step), n // step
        return remote(src.at[k, :, here], dst.at[k, :, here], send.at[0, i], recv.at[k, i], along(1))

    def wait_block(src, dst, send, recv, n, k):
        @pl.when(z == k)
        def _():
            keep(src, dst, recv, n).wait()

        @pl.when(z != k)
        def _():
            come(src, dst, send, recv, n, k).wait_recv()

    def by_clip(staging, n):
        wide[...] = raw[:, :, pl.ds(n, step)].astype(F32)
        for k in range(SPLIT):
            staging[k, :, pl.ds(n, step)] = wide[:, k, :].astype(BF16)

    raw_tok.wait()
    for n in chunks:
        by_clip(staged, n)
        if n == 0:
            pl.semaphore_wait(barrier, SPLIT - 1 + GROUP - 1)
        for copy in spread(staged, tok_in, tok_s, tok_r, n):
            copy.start()
        keep(staged, tok_in, tok_r, n).start()
    raw_cot.start()
    raw_cot.wait()
    for copy in weights[2:]:
        copy.start()
    for n in chunks:
        by_clip(staged_grad, n)
        keep(staged_grad, cot_in, cot_r, n).start()
    for copy in small:
        copy.wait()

    lane = lax.broadcasted_iota(jnp.int32, (8, 128), 1)
    index = jnp.full((8, 128), -1, jnp.int32)
    for s in range(TKEEP):
        index = jnp.where(lane == s, time_index[z, s], index)
    for s in range(FKEEP):
        index = jnp.where(lane == SLOTS + s, freq_index[z, s] + TIMES, index)
    column = lax.broadcasted_iota(jnp.int32, (128, 128), 0)
    pick = jnp.where(column == index[:1], 1.0, 0.0)
    picks[...] = pick.astype(BF16)
    pay[...] = jnp.zeros_like(pay)
    pay[pl.ds(0, time_table.shape[0]), :] = time_table[...].astype(F32)
    pay[pl.ds(TIMES, freq_table.shape[0]), :] = freq_table[...].astype(F32)
    by_slot = dot(pick.T.astype(BF16), pay[...].astype(BF16)).astype(BF16)

    def slots_of(row_number, slot):
        block = sum((row_number >= padded * k).astype(jnp.int32) for k in range(1, SPLIT))
        inside = row_number - padded * block
        patch = row_number - (padded - rows) * block - 2
        frequency = sum((patch >= TKEEP * k).astype(jnp.int32) for k in range(1, FKEEP))
        time = patch - TKEEP * frequency
        hit = (slot == time) | (slot == SLOTS + frequency)
        return jnp.where(hit & (inside < rows) & (patch >= 0), 1.0, 0.0).astype(BF16)

    g1, s1 = row(gain1), row(shift1)
    bias_q, bias_v = qv_bias[0:1, :].astype(F32), qv_bias[1:2, :].astype(F32)
    weights[0].wait()
    @pl.loop(0, SPLIT)
    def _(d):
        k = near(d)
        place = pl.multiple_of(padded * k, 32)
        block_rows = pl.ds(place, padded)
        number = lax.broadcasted_iota(jnp.int32, (padded, 128), 0) + place
        slot = lax.broadcasted_iota(jnp.int32, (padded, 128), 1)
        position = dot(slots_of(number, slot), by_slot)
        for n in chunks:
            wait_block(staged, tok_in, tok_s, tok_r, n, k)
        stream_in[pl.ds(place, rows), :] = tok_in[k].astype(F32) + position[:rows]
        stream_in[pl.ds(place + rows, padded - rows), :] = jnp.zeros((padded - rows, width), F32)
        hat, _ = normalize(stream_in[block_rows, :])
        normed[block_rows, :] = (hat * g1 + s1).astype(BF16)
        for t, (bias, scale) in enumerate(((bias_q, HDIM**-0.5), (None, 1.0), (bias_v, 1.0))):
            for n in range(0, width, step):
                part = dot(normed[block_rows, :], w_qkv[:, pl.ds(t * width + n, step)])
                if bias is not None:
                    part = part + bias[:, n : n + step]
                part = part.astype(BF16)
                if scale != 1.0:
                    part = part * jnp.asarray(scale, BF16)
                qkv[block_rows, pl.ds(t * width + n, step)] = part

    for n in chunks:
        for copy in spread(staged_grad, cot_in, cot_s, cot_r, n):
            copy.start()
    part_of = [jnp.where(core == side, 0, 2) for side in range(2)]

    def left_copy(i):
        if i >= 4:
            return remote(left.at[2, i], left.at[1, i], left_s.at[i], left_r.at[i], at(1))
        return left_quarter(i)

    def left_quarter(q):
        return remote(
            left.at[2, pl.ds(0, 4), q], left.at[1, pl.ds(0, 4), q], left_s.at[q], left_r.at[q], at(1)
        )

    def blocks_in(n):
        found = []
        for block in range(n // shard, -(-(n + step) // shard)):
            found.append((block, max(n, shard * block), min(n + step, shard * (block + 1))))
        return found

    def hand_all(i, source):
        for n in range(0, width, step):
            turned = source[:, pl.ds(n, step)].T
            for block, start, stop in blocks_in(n):
                at_row = pl.ds(start - shard * block, stop - start)
                left[part_of[block % 2], i, block // 2, at_row, :] = turned[start - n : stop - n]
        left_copy(i).start()

    def right_copy(g):
        return remote(
            right.at[g, pl.ds(0, many)], right.at[g, pl.ds(many, many)], right_s.at[g], right_r.at[g], at(1)
        )

    hand_all(6, normed)

    key_number = lax.broadcasted_iota(jnp.int32, (8, many), 1)
    key_block = sum((key_number >= padded * k).astype(jnp.int32) for k in range(1, SPLIT))
    key_mask = jnp.where(key_number - padded * key_block < rows, 0.0, -1e30)[:1]
    head_lane = lax.broadcasted_iota(jnp.int32, (8, 2 * HDIM), 1)
    one_head = [
        jnp.where(head_lane < HDIM, 1.0, 0.0)[:1].astype(BF16),
        jnp.where(head_lane < HDIM, 0.0, 1.0)[:1].astype(BF16),
    ]

    def lanes(t, p):
        return pl.ds(pl.multiple_of(t * width + p * (2 * HDIM), 2 * HDIM), 2 * HDIM)

    def scores_of(p, place):
        query, key = qkv[:, lanes(0, p)], qkv[:, lanes(1, p)]
        for h in range(2):
            place[:, pl.ds(h * many, many)] = dot(query * one_head[h], key, NT)

    def weigh(p, place):
        value = qkv[:, lanes(2, p)]
        for r in range(0, many, 64):
            here = pl.ds(r, 64)
            for h in range(2):
                scores = place[here, pl.ds(h * many, many)] + key_mask
                weight = jnp.exp(scores - jnp.max(scores, -1, keepdims=True))
                weight = weight * (1.0 / jnp.sum(weight, -1, keepdims=True))
                probs[p, here, pl.ds(h * many, many)] = weight.astype(BF16)
        both = jnp.concatenate([value * one_head[0], value * one_head[1]], 0)
        attended[:, lanes(0, p)] = dot(probs[p], both).astype(BF16)

    scores_of(0, work)

    @pl.loop(0, pairs // 2)
    def _(m):
        scores_of(2 * m + 1, mid)
        weigh(2 * m, work)
        scores_of(jnp.minimum(2 * m + 2, pairs - 1), work)
        weigh(2 * m + 1, mid)

    weights[1].wait()
    hand_all(5, attended)
    bias = row(proj_bias)
    for n in range(0, width, step):
        mid[:, pl.ds(n, step)] = (
            stream_in[:, pl.ds(n, step)]
            + dot(attended[...], w_proj[:, pl.ds(n, step)])
            + bias[:, n : n + step]
        )
    g2, s2 = row(gain2), row(shift2)

    @pl.loop(0, many // BLOCK)
    def _(b):
        at_row = pl.ds(pl.multiple_of(b * BLOCK, BLOCK), BLOCK)
        hat, _ = normalize(mid[at_row, :])
        normed[at_row, :] = (hat * g2 + s2).astype(BF16)

    def column_sums(value):
        return jnp.sum(value.astype(F32), 0, keepdims=True)

    def first_matrix(q, n):
        place = pl.ds(pl.multiple_of(q * width + n, 128), step)
        work[:, pl.ds(n, step)] = dot(normed[...], w_fc1[:, place]) + fc1_bias[place].astype(F32).reshape(1, step)

    def activate(q, n):
        parts = []
        for r in range(0, many, 64):
            here = pl.ds(r, 64)
            hidden = work[here, pl.ds(n, step)]
            cdf, pdf = normal_cdf_pdf(hidden)
            active = (hidden * cdf).astype(BF16)
            unit[8 + q, here, pl.ds(n, step)] = active
            right[1 + q, here, pl.ds(n, step)] = (cdf + hidden * pdf).astype(BF16)
            parts.append(active)
        turned = jnp.concatenate(parts, 0).T
        for block, start, stop in blocks_in(n):
            at_row = pl.ds(start - shard * block, stop - start)
            left[part_of[block // 4], block % 4, q, at_row, :] = turned[start - n : stop - n]

    weights[2].wait()
    hand_all(4, normed)
    first_matrix(0, 0)

    def quarter(q, more):
        for n in range(step, width, step):
            first_matrix(q, n)
            activate(q, n - step)
        if more:
            first_matrix(q + 1, 0)
        activate(q, width - step)
        left_quarter(q).start()

    @pl.loop(0, 3)
    def _(q):
        quarter(q, True)

    wide_cot[pl.ds(rows, padded - rows), :] = jnp.zeros((padded - rows, step), F32)
    for k in range(SPLIT):
        for n in chunks:
            wait_block(staged_grad, cot_in, cot_s, cot_r, n, k)
            wide_cot[pl.ds(0, rows), :] = cot_in[k, :, pl.ds(n, step)].astype(F32)
            right[0, pl.ds(padded * k, padded), pl.ds(n, step)] = wide_cot[...].astype(BF16)
    for n in range(0, width, step):
        pay[pl.ds(99 + 7, 1), pl.ds(n, step)] = column_sums(right[0, pl.ds(0, many), pl.ds(n, step)])
    right_copy(0).start()

    quarter(3, False)

    def grid_of(j):
        return unit.at[PARTS[j][0]].reshape(2, 2, shard, width)

    def span(j, part):
        i, start, size = PARTS[j]
        size = size * width // 6
        return pl.ds(start * width // 6 + part * size, size)

    def some(j, part):
        i, start, size = PARTS[j]
        return pl.ds(start * width // 12, size * width // 6)

    def one_copies(j):
        u, i, here = grid_of(j), PARTS[j][0], some(j, 0)
        return (
            remote(u.at[:, 1 - x, :, span(j, 0)], got1.at[i, 0, :, :, here], one_s.at[j, 0], one_r.at[j, 0], at(2)),
            remote(u.at[1 - y, :, :, span(j, 1)], got1.at[i, 1, :, :, here], one_s.at[j, 1], one_r.at[j, 1], at(4)),
        )

    def two_copies(j):
        u, i, here = grid_of(j), PARTS[j][0], some(j, 0)
        return (
            remote(u.at[1 - y, x, :, span(j, 0)], got2.at[i, 0, :, here], two_s.at[j, 0], two_r.at[j, 0], at(4)),
            remote(u.at[y, 1 - x, :, span(j, 1)], got2.at[i, 1, :, here], two_s.at[j, 1], two_r.at[j, 1], at(2)),
        )

    own_part = jnp.where(z == 2, 1, 0)
    oth_part = 1 - own_part
    end_first = jnp.where(z < 2, 1, 0)

    def place_of(j, part):
        i, start, size = PARTS[j]
        size = size * width // 6
        return pl.ds(pl.multiple_of(start * width // 6 + part * size, 128), size)

    def end_copy(j, which):
        cols = place_of(j, end_first if which == 0 else 1 - end_first)
        i = PARTS[j][0]
        return remote(
            grid_of(j).at[y, x, :, cols], end_in.at[i, :, cols], end_s.at[j, which], end_r.at[j, which], to_mid
        )

    def mid_copy(j):
        return remote(
            grid_of(j).at[y, x, :, place_of(j, oth_part)], mid_in.at[PARTS[j][0], :, some(j, 0)], mid_s.at[j],
            mid_r.at[j], to_other,
        )

    def fin_copy(j, part, which, device):
        here = final.at[PARTS[j][0], :, place_of(j, part)]
        return remote(here, here, fin_s.at[j, which], fin_r.at[j, part], device)

    def share_copy(j):
        i, start, size = PARTS[j]
        cols = pl.ds(start * width // 6, size * width // 3)
        return pltpu.make_async_copy(final.at[i, :, cols], shares_hbm.at[i, :, cols], share_s.at[j])

    waited = set()

    def product(j):
        i, start, size = PARTS[j]
        l = i if i < 4 else 4 if i < 8 else 5 if i == 8 else 6
        g = 0 if i < 4 else i - 3
        for other in range(4) if l < 4 else (l,):
            if ("left", other) not in waited:
                left_copy(other).wait_recv()
                waited.add(("left", other))
        if g not in waited:
            right_copy(g).wait_recv()
            waited.add(g)
        both = jnp.concatenate([left[k, l].reshape(4 * shard, many) for k in range(2)], 1)
        for n in range(start * width // 6, (start + 2 * size) * width // 6, step):
            part = dot(both, right[g, :, pl.ds(n, step)])
            unit[i, :, pl.ds(n, step)] = part.astype(BF16)
        for copy in one_copies(j):
            copy.start()

    def tick1(j):
        u, i, here = grid_of(j), PARTS[j][0], some(j, 0)
        first, second = one_copies(j)
        after_first, after_second = two_copies(j)
        a, b = span(j, 0), span(j, 1)
        first.wait_recv()
        u[1 - y, x, :, a] = (u[1 - y, x, :, a].astype(F32) + got1[i, 0, 1 - y, :, here].astype(F32)).astype(BF16)
        after_first.start()
        second.wait_recv()
        u[y, 1 - x, :, b] = (u[y, 1 - x, :, b].astype(F32) + got1[i, 1, 1 - x, :, here].astype(F32)).astype(BF16)
        after_second.start()

    def plane_sum(j, part):
        i, here = PARTS[j][0], some(j, 0)
        near = jnp.where(part == 0, y, x)
        return (
            grid_of(j)[y, x, :, place_of(j, part)].astype(F32)
            + got1[i, part, near, :, here].astype(F32)
            + got2[i, part, :, here].astype(F32)
        )

    def tick2(j):
        for copy in two_copies(j):
            copy.wait_recv()

        @pl.when(is_end)
        def _():
            for which in range(2):
                part = end_first if which == 0 else 1 - end_first
                grid_of(j)[y, x, :, place_of(j, part)] = plane_sum(j, part).astype(BF16)
                end_copy(j, which).start()

    def line_sum(j, part):
        return plane_sum(j, part) + end_in[PARTS[j][0], :, place_of(j, part)].astype(F32)

    def tick3(j):
        @pl.when(is_mid)
        def _():
            end_copy(j, 0).wait_recv()
            grid_of(j)[y, x, :, place_of(j, oth_part)] = line_sum(j, oth_part).astype(BF16)
            mid_copy(j).start()

    def tick4(j):
        @pl.when(is_mid)
        def _():
            i = PARTS[j][0]
            end_copy(j, 1).wait_recv()
            total = line_sum(j, own_part)
            mid_copy(j).wait_recv()
            total = total + mid_in[i, :, some(j, 0)].astype(F32)
            final[i, :, place_of(j, own_part)] = total.astype(BF16)
            fin_copy(j, own_part, 0, to_other).start()
            fin_copy(j, own_part, 1, to_end).start()

    def tick5(j):
        @pl.when(is_mid)
        def _():
            fin_copy(j, oth_part, 2, to_end).wait_recv()
            fin_copy(j, oth_part, 2, to_end).start()

        @pl.when(is_end)
        def _():
            fin_copy(j, 0, 0, to_mid).wait_recv()
            fin_copy(j, 1, 0, to_mid).wait_recv()

        share_copy(j).start()

    bias_out = row(fc2_bias)

    def block_out(n):
        if n == 0:
            for m in chunks:
                for copy in spread(staged, tok_in, tok_s, tok_r, m):
                    copy.wait_send()
        part = mid[:, pl.ds(n, step)] + bias_out[:, n : n + step]
        for q in range(4):
            part = part + dot(unit[8 + q], w_fc2[pl.ds(q * width, width), pl.ds(n, step)])
        for k in range(SPLIT):
            staged[k, :, pl.ds(n, step)] = part[padded * k : padded * k + rows].astype(BF16)
        for copy in spread(staged, out_hbm, out_s, out_r, n):
            copy.start()
        keep(staged, out_hbm, out_r, n).start()

    def grad_hidden(q):
        for n in range(0, width, step):
            part = dot(right[0, pl.ds(0, many), :], w_fc2[pl.ds(q * width + n, step), :], NT)
            part = (part * right[1 + q, pl.ds(0, many), pl.ds(n, step)].astype(F32)).astype(BF16)
            right[1 + q, pl.ds(0, many), pl.ds(n, step)] = part
            pay[pl.ds(99 + 8 + q, 1), pl.ds(n, step)] = column_sums(part)
        right_copy(1 + q).start()

    def grad_second():
        for n in range(0, width, step):
            part = None
            for q in range(4):
                term = dot(right[1 + q, pl.ds(0, many), :], w_fc1[pl.ds(n, step), pl.ds(q * width, width)], NT)
                part = term if part is None else part + term
            work[:, pl.ds(n, step)] = part

    def norm_back(grad, value, gain):
        hat, rstd = normalize(value)
        g = grad * gain
        back = rstd * (g - jnp.mean(g, -1, keepdims=True) - hat * jnp.mean(g * hat, -1, keepdims=True))
        return back, hat

    zero = jnp.zeros((1, width), F32)

    def second_norm():
        def block(b, sums):
            at_row = pl.ds(pl.multiple_of(b * BLOCK, BLOCK), BLOCK)
            grad = work[at_row, :]
            back, hat = norm_back(grad, mid[at_row, :], g2)
            back = back + right[0, at_row, :].astype(F32)
            mid[at_row, :] = back
            branch = back.astype(BF16)
            right[5, at_row, :] = branch
            return (
                sums[0] + column_sums(grad * hat),
                sums[1] + column_sums(grad),
                sums[2] + column_sums(branch),
            )

        sums = lax.fori_loop(0, many // BLOCK, block, (zero, zero, zero))
        pay[pl.ds(99 + 5, 1), :] = sums[0]
        pay[pl.ds(99 + 6, 1), :] = sums[1]
        pay[pl.ds(99 + 4, 1), :] = sums[2]
        right_copy(5).start()

    def grad_attended():
        for n in range(0, width, step):
            normed[:, pl.ds(n, step)] = dot(
                right[5, pl.ds(0, many), :], w_proj[pl.ds(n, step), :], NT
            ).astype(BF16)

    def attend_back(p):
        query, key, value = (qkv[:, lanes(t, p)] for t in range(3))
        grad_out = normed[:, lanes(0, p)]
        grads = None
        for h in range(2):
            weight_low = probs[p, :, pl.ds(h * many, many)]
            weight = weight_low.astype(F32)
            grad_probs = dot(grad_out * one_head[h], value, NT) * weight
            inner = jnp.sum(grad_probs, -1, keepdims=True)
            grad_scores = (grad_probs - weight * inner).astype(BF16)
            terms = (
                dot(grad_scores, key * one_head[h]),
                dot(grad_scores, query * one_head[h], TN),
                dot(weight_low, grad_out * one_head[h], TN),
            )
            grads = terms if grads is None else tuple(a + b for a, b in zip(grads, terms, strict=True))
        for t, (grad, scale) in enumerate(zip(grads, (HDIM**-0.5, 1.0, 1.0), strict=True)):
            low_grad = (grad * scale).astype(BF16)
            right[6 + t, pl.ds(0, many), lanes(0, p)] = low_grad
            if t != 1:
                pay[pl.ds(99 + 2 + t // 2, 1), lanes(0, p)] = column_sums(low_grad)

    def attention_back(s):
        @pl.loop(s * pairs // 3, (s + 1) * pairs // 3)
        def _(p):
            attend_back(p)

        if s == 2:
            for t in range(3):
                right_copy(6 + t).start()

    def grad_first():
        for n in range(0, width, step):
            part = None
            for t in range(3):
                term = dot(right[6 + t, pl.ds(0, many), :], w_qkv[pl.ds(n, step), pl.ds(t * width, width)], NT)
                part = term if part is None else part + term
            work[:, pl.ds(n, step)] = part

    def own_grad():
        return pltpu.make_async_copy(staged_grad.at[z], grad_hbm.at[z], grad_r.at[z])

    def grad_copy(d):
        return remote(staged_grad.at[near(d)], grad_hbm.at[z], grad_s.at[d - 1], grad_r.at[z], along(d))

    def first_norm():
        for n in chunks:
            for copy in spread(staged_grad, cot_in, cot_s, cot_r, n):
                copy.wait_send()
        def block(t, sums):
            d = SPLIT - 1 - t
            k = near(d)
            at_row = pl.ds(pl.multiple_of(padded * k, 32), padded)
            grad = work[at_row, :]
            back, hat = norm_back(grad, stream_in[at_row, :], g1)
            back = mid[at_row, :] + back
            mid[at_row, :] = back
            staged_grad[k] = back[:rows].astype(BF16)

            @pl.when(d == 0)
            def _():
                own_grad().start()

            @pl.when(d > 0)
            def _():
                grad_copy(d).start()

            return sums[0] + column_sums(grad * hat), sums[1] + column_sums(grad)

        sums = lax.fori_loop(0, SPLIT, block, (zero, zero))
        first, second = sums
        pay[pl.ds(99, 1), :] = first
        pay[pl.ds(100, 1), :] = second

    def halves(v):
        high = v.astype(BF16)
        return high, (v - high.astype(F32)).astype(BF16)

    def pay_copy(bits):
        return remote(
            pay_low.at[pl.ds(16 * peer(bits), 16)], pay_in.at[low], pay_s.at[bits - 1], pay_r.at[low], at(bits)
        )

    def payz_copy(d):
        return remote(pay_mid.at[z], pay_mid.at[z], payz_s.at[d - 1], payz_r.at[z], along(d))

    def payo_copy(bits):
        return remote(pay_out.at[low], pay_out.at[low], payo_s.at[bits - 1], payo_r.at[low], at(bits))

    def position_tables():
        number = lax.broadcasted_iota(jnp.int32, (128, many), 1)
        slot = lax.broadcasted_iota(jnp.int32, (128, many), 0)
        slots = slots_of(number, slot)
        for n in range(0, width, step):
            by = sum(dot(slots, v) for v in halves(mid[:, pl.ds(n, step)]))
            table_grad = sum(dot(picks[...], v) for v in halves(by))
            pay[pl.ds(0, 99), pl.ds(n, step)] = table_grad[:99]
            pay[pl.ds(TIMES, 16), pl.ds(n, step)] = table_grad[TIMES:]
        pay[pl.ds(111, 1), :] = zero
        pay_low[...] = pay[...].astype(BF16)
        for bits in range(1, GROUP):
            pay_copy(bits).start()

    def pay_group():
        for bits in range(1, GROUP):
            remote(
                pay_low.at[pl.ds(0, 16)], pay_in.at[peer(bits)], pay_s.at[bits - 1], pay_r.at[peer(bits)], at(bits)
            ).wait_recv()
        pay_in[low] = pay_low[pl.ds(pl.multiple_of(16 * low, 16), 16), :]
        pay_mid[z] = sum(pay_in[s].astype(F32) for s in range(GROUP)).astype(BF16)
        for d in range(1, SPLIT):
            payz_copy(d).start()

    def pay_line():
        for d in range(1, SPLIT):
            k = near(d)
            remote(pay_mid.at[k], pay_mid.at[k], payz_s.at[d - 1], payz_r.at[k], along(d)).wait_recv()
        pay_out[low] = sum(pay_mid[s].astype(F32) for s in range(SPLIT)).astype(BF16)
        for bits in range(1, GROUP):
            payo_copy(bits).start()

    pieces = {
        "sec": grad_second, "sen": second_norm, "att": grad_attended, "fir": grad_first,
        "fin": first_norm, "tab": position_tables, "pay2": pay_group, "pay3": pay_line,
    }
    for n in chunks:
        pieces[f"out{n // step}"] = functools.partial(block_out, n)
    for q in range(4):
        pieces[f"gh{q}"] = functools.partial(grad_hidden, q)
    for s in range(3):
        pieces[f"ab{s}"] = functools.partial(attention_back, s)
    for i in range(len(PARTS)):
        pieces[f"t0_{i}"] = functools.partial(product, i)
        for k, tick in enumerate((tick1, tick2, tick3, tick4, tick5)):
            pieces[f"t{k + 1}_{i}"] = functools.partial(tick, i)
    assert sorted(ORDER) == sorted(pieces)
    weights[3].wait()
    def finished():
        for n in chunks:
            for copy in spread(staged, out_hbm, out_s, out_r, n):
                copy.wait_send()
            for k in range(SPLIT):
                wait_block(staged, out_hbm, out_s, out_r, n, k)
        own_grad().wait()
        for d in range(1, SPLIT):
            grad_copy(d).wait_send()
            k = near(d)
            remote(staged_grad.at[k], grad_hbm.at[k], grad_s.at[0], grad_r.at[k], along(1)).wait_recv()
        for i in range(left.shape[1]):
            left_copy(i).wait_send()
        for g in range(right.shape[0]):
            right_copy(g).wait_send()

        for j in range(len(PARTS)):
            for copy in (*one_copies(j), *two_copies(j)):
                copy.wait_send()

        @pl.when(is_end)
        def _():
            for j in range(len(PARTS)):
                end_copy(j, 0).wait_send()
                end_copy(j, 1).wait_send()

    for number, name in enumerate(ORDER):
        if number == len(ORDER) - 3:
            finished()
        pieces[name]()
    for bits in range(1, GROUP):
        remote(
            pay_out.at[low], pay_out.at[peer(bits)], payo_s.at[bits - 1], payo_r.at[peer(bits)], at(bits)
        ).wait_recv()
    last = pltpu.make_async_copy(pay_out, small_hbm, w_sem.at[0])
    last.start()

    @pl.when(is_mid)
    def _():
        for j in range(len(PARTS)):
            mid_copy(j).wait_send()
            fin_copy(j, own_part, 0, to_other).wait_send()
            fin_copy(j, own_part, 1, to_end).wait_send()
            fin_copy(j, oth_part, 2, to_end).wait_send()

    for j in range(len(PARTS)):
        share_copy(j).wait()

    for bits in range(1, GROUP):
        pay_copy(bits).wait_send()
        payo_copy(bits).wait_send()
    for d in range(1, SPLIT):
        payz_copy(d).wait_send()
    last.wait()


def finish_kernel(
    out_in, grad_in, shares, small,
    out, grad, freq, time, gain1, shift1, qkv, qv_bias, proj, proj_bias, gain2, shift2, fc1, fc1_bias, fc2, fc2_bias,
    rows_in, wide, rows_out, parts, small_in, f_qkv, f_proj, f_fc1, f_fc2, f_time, f_freq, f_qv, lines,
    row_sem, part_sem, out_sem,
):
    width = wide.shape[2]
    shard = parts.shape[1]
    reads = [pltpu.make_async_copy(shares.at[i], parts.at[i], part_sem.at[i]) for i in range(UNITS)]
    moves = [pltpu.make_async_copy(src, rows_in.at[i], row_sem.at[i]) for i, src in enumerate((out_in, grad_in))]
    read_small = pltpu.make_async_copy(small, small_in, row_sem.at[2])
    for copy in (*reads, *moves, read_small):
        copy.start()
    line_of = lambda i: lines.at[pl.ds(i * width, width)]
    writes = [
        pltpu.make_async_copy(src, dst, out_sem.at[i])
        for i, (src, dst) in enumerate(
            (
                (f_fc2, fc2), (f_fc1, fc1), (f_proj, proj), (f_qkv, qkv), (rows_out.at[0], out), (rows_out.at[1], grad),
                (f_time, time), (f_freq, freq), (f_qv, qv_bias), (line_of(0), gain1), (line_of(1), shift1),
                (line_of(2), proj_bias), (line_of(3), gain2), (line_of(4), shift2), (line_of(5), fc2_bias),
                (lines.at[pl.ds(6 * width, 4 * width)], fc1_bias),
            )
        )
    ]
    for i in range(UNITS):
        reads[i].wait()
        value = parts[i].astype(F32)
        if i < 4:
            f_fc2[pl.ds(i * shard, shard), :] = value
        elif i < 8:
            f_fc1[:, pl.ds((i - 4) * width, width)] = value
        elif i == 8:
            f_proj[...] = value
        else:
            f_qkv[:, pl.ds((i - 9) * width, width)] = value
        if i in (3, 7, 8, 11):
            writes[(3, 7, 8, 11).index(i)].start()
    for i in range(2):
        moves[i].wait()
        for k in range(SPLIT):
            wide[:, k, :] = rows_in[i, k].astype(F32)
        rows_out[i] = wide[...].astype(BF16)
        writes[4 + i].start()
    read_small.wait()
    f_time[...] = small_in[pl.ds(0, time.shape[0]), :].astype(F32)
    f_freq[...] = small_in[pl.ds(TIMES, freq.shape[0]), :].astype(F32)
    rest = small_in[pl.ds(96, 16), :].astype(F32)[3:]
    f_qv[...] = rest[2:4]
    for at, i in enumerate((0, 1, 4, 5, 6, 7)):
        lines[pl.ds(at * width, width)] = rest[i : i + 1].reshape(width)
    for q in range(4):
        lines[pl.ds((6 + q) * width, width)] = rest[8 + q : 9 + q].reshape(width)
    for copy in writes[6:]:
        copy.start()
    for copy in writes:
        copy.wait()


def on_device(
    tokens, freq_index, time_index, freq_table, time_table,
    norm1_gain, norm1_shift, qkv_weight, qv_bias, proj_weight, proj_bias, norm2_gain, norm2_shift,
    fc1_weight, fc1_bias, fc2_weight, fc2_bias, cotangent,
):
    clips, rows, width = tokens.shape
    count = len(PARTS)
    pieces = width // (256 if width % 256 == 0 else 128)
    times, freqs = time_table.shape[0], freq_table.shape[0]
    groups = lax.axis_size("seq")
    clip_devices = lax.axis_size("clip")
    assert clips == SPLIT and groups == SPLIT and clip_devices % GROUP == 0
    hidden_width = fc1_weight.shape[1]
    assert hidden_width == 4 * width
    padded = -(-rows // 32) * 32
    many = SPLIT * padded
    shard = width // GROUP
    half = width // 2
    heads = width // HDIM

    anywhere = pl.BlockSpec(memory_space=pl.ANY)
    dma = pltpu.SemaphoreType.DMA
    blocks = (SPLIT, rows, width)
    vectors = (freq_table, time_table, norm1_gain, norm1_shift, qv_bias, proj_bias, norm2_gain, norm2_shift, fc1_bias, fc2_bias)
    small_scratch = [pltpu.SMEM(v.shape, v.dtype) for v in (freq_index, time_index)]
    small_scratch += [pltpu.VMEM(v.shape, v.dtype) for v in vectors]
    tokens, cotangent = (v.transpose(1, 0, 2) for v in (tokens, cotangent))
    out, grad, shares, small = pl.pallas_call(
        block_kernel,
        out_shape=(
            jax.ShapeDtypeStruct(blocks, BF16),
            jax.ShapeDtypeStruct(blocks, BF16),
            jax.ShapeDtypeStruct((UNITS, shard, width), BF16),
            jax.ShapeDtypeStruct((GROUP, 16, width), BF16),
        ),
        in_specs=[anywhere] * 18,
        out_specs=(anywhere,) * 4,
        scratch_shapes=[
            *small_scratch,
            pltpu.VMEM((rows, SPLIT, width), BF16),
            pltpu.VMEM((rows, SPLIT, 256 if width % 256 == 0 else 128), F32),
            pltpu.VMEM((width, 3 * width), BF16),
            pltpu.VMEM((width, width), BF16),
            pltpu.VMEM((width, hidden_width), BF16),
            pltpu.VMEM((hidden_width, width), BF16),
            pltpu.VMEM(blocks, BF16),
            pltpu.VMEM(blocks, BF16),
            pltpu.VMEM((padded, 256 if width % 256 == 0 else 128), F32),
            pltpu.VMEM((many, width), F32),
            pltpu.VMEM((many, width), BF16),
            pltpu.VMEM((many, 3 * width), BF16),
            pltpu.VMEM((heads // 2, many, 2 * many), BF16),
            pltpu.VMEM((many, width), BF16),
            pltpu.VMEM((many, width), F32),
            pltpu.VMEM((many, width), F32),
            pltpu.VMEM((3, 7, 4, shard, many), BF16),
            pltpu.VMEM((9, 2 * many, width), BF16),
            pltpu.VMEM((UNITS, 4 * shard, width), BF16),
            pltpu.VMEM((UNITS, 2, 2, shard, half), BF16),
            pltpu.VMEM((UNITS, 2, shard, half), BF16),
            pltpu.VMEM((UNITS, shard, width), BF16),
            pltpu.VMEM((UNITS, shard, half), BF16),
            pltpu.VMEM((UNITS, shard, width), BF16),
            pltpu.VMEM(blocks, BF16),
            pltpu.VMEM(blocks, BF16),
            pltpu.VMEM((128, 128), BF16),
            pltpu.VMEM((128, width), F32),
            pltpu.VMEM((128, width), BF16),
            pltpu.VMEM((GROUP, 16, width), BF16),
            pltpu.VMEM((SPLIT, 16, width), BF16),
            pltpu.VMEM((GROUP, 16, width), BF16),
            dma((12,)), dma((2,)), dma((4,)),
            dma((3, pieces)), dma((4, pieces)), dma((3, pieces)), dma((4, pieces)), dma((3, pieces)), dma((4, pieces)),
            dma((3,)), dma((4,)),
            dma((7,)), dma((7,)), dma((9,)), dma((9,)),
            dma((count, 2)), dma((count, 2)), dma((count, 2)), dma((count, 2)),
            dma((count, 2)), dma((count, 2)), dma((count,)), dma((count,)),
            dma((count, 3)), dma((count, 2)), dma((count,)),
            dma((7,)), dma((8,)), dma((3,)), dma((4,)), dma((7,)), dma((8,)),
        ],
        compiler_params=pltpu.CompilerParams(
            collective_id=1, has_side_effects=True, vmem_limit_bytes=63 * 2**20
        ),
    )(
        tokens, freq_index, time_index, freq_table, time_table,
        norm1_gain, norm1_shift, qkv_weight, qv_bias, proj_weight, proj_bias, norm2_gain, norm2_shift,
        fc1_weight, fc1_bias, fc2_weight, fc2_bias, cotangent,
    )
    small = small.reshape(GROUP * 16, width)
    if clip_devices == GROUP:
        shape = lambda *dims: jax.ShapeDtypeStruct(dims, F32)
        inner = jax.ShapeDtypeStruct((rows, SPLIT, width), BF16)
        line = shape(width)
        results = (
            inner, inner, shape(freqs, width), shape(times, width), line, line, shape(shard, 3 * width),
            shape(2, width), shape(shard, width), line, line, line, shape(shard, 4 * width),
            shape(4 * width), shape(4 * shard, width), line,
        )
        out, grad, *others = pl.pallas_call(
            finish_kernel,
            out_shape=results,
            in_specs=[anywhere] * 4,
            out_specs=(anywhere,) * 16,
            scratch_shapes=[
                pltpu.VMEM((2, *blocks), BF16),
                pltpu.VMEM((rows, SPLIT, width), F32),
                pltpu.VMEM((2, rows, SPLIT, width), BF16),
                pltpu.VMEM((UNITS, shard, width), BF16),
                pltpu.VMEM((GROUP * 16, width), BF16),
                pltpu.VMEM((shard, 3 * width), F32),
                pltpu.VMEM((shard, width), F32),
                pltpu.VMEM((shard, 4 * width), F32),
                pltpu.VMEM((4 * shard, width), F32),
                pltpu.VMEM((times, width), F32),
                pltpu.VMEM((freqs, width), F32),
                pltpu.VMEM((2, width), F32),
                pltpu.VMEM((10 * width,), F32),
                dma((3,)), dma((UNITS,)), dma((16,)),
            ],
            compiler_params=pltpu.CompilerParams(vmem_limit_bytes=62 * 2**20),
        )(out, grad, shares, small)
        return (out.transpose(1, 0, 2), grad.transpose(1, 0, 2), *others)
    shares, small = shares.astype(F32), small.astype(F32)
    wide_count = clip_devices // GROUP
    same = [[h * GROUP + b for h in range(wide_count)] for b in range(GROUP)]
    small = lax.psum(small, "clip", axis_index_groups=same)
    fc2 = shares[:4].reshape(4 * shard, width)
    rest = shares[4:].transpose(1, 0, 2).reshape(shard, 8 * width)
    summed = [
        lax.psum_scatter(v, "clip", scatter_dimension=0, axis_index_groups=same, tiled=True)
        for v in (fc2, rest)
    ]
    moves = [(h * GROUP + b, b * wide_count + h) for h in range(wide_count) for b in range(GROUP)]
    fc2, rest = (lax.ppermute(v, "clip", moves) for v in summed)
    fc1, proj, qkv = rest[:, : 4 * width], rest[:, 4 * width : 5 * width], rest[:, 5 * width :]
    return (
        out,
        grad,
        small[TIMES : TIMES + freqs],
        small[:times],
        small[99],
        small[100],
        qkv,
        small[101:103],
        proj,
        small[103],
        small[104],
        small[105],
        fc1,
        small[107:111].reshape(-1),
        fc2,
        small[106],
    )


def solution(mesh):
    rows_split, clip_split = P("clip", "seq", None), P("clip", None)
    in_specs = (rows_split, clip_split, clip_split) + (P(),) * 14 + (rows_split,)
    out_specs = (
        rows_split, rows_split, P(), P(), P(), P(), clip_split, P(), clip_split, P(), P(), P(), clip_split,
        P(), clip_split, P(),
    )
    return jax.shard_map(on_device, mesh=mesh, in_specs=in_specs, out_specs=out_specs, check_vma=False)
```
